32 devices in a mesh: groups: 2 (over x), seq: 16 (over z, y, core).
Axes of the slice: x: 2, y: 2, z: 4, core: 2. Of those that a mesh axis runs over, the one named last changes fastest.
Arguments:
- audio_qkv: bfloat16 [2048, 3, 16, 128], P(('groups', 'seq')), parts along dimension 0, may hold values from -8 to 8
- video_q: bfloat16 [16384, 16, 128], P(('groups', 'seq')), parts along dimension 0, may hold values from -8 to 8
- pairs: int32 [128, 4], P(('groups', 'seq')), parts along dimension 0, may hold values from 0 to 31, as said below
- counts: int32 [128], P(('groups', 'seq')), parts along dimension 0, may hold values from 1 to 4
Outputs:
- audio_attn: bfloat16 [2048, 16, 128], P(('groups', 'seq')), parts along dimension 0
- video_cross: bfloat16 [16384, 16, 128], P(('groups', 'seq')), parts along dimension 0
The draws below stay inside these ranges and needn't reach their ends.
There are 2 independent parts, one for each index of `groups`. The reference program is written for one: setup_inputs(seed, part) draws one part's arguments, and reference() takes and returns one part's arrays. A program takes and returns all parts, laid end to end along the dimension named above; each array names one. Nothing has to cross between parts.
Inputs may be any that keep to these rules, and one draw needn't show every extreme that they name: `pairs`: entry 0 of row b is c = (b * 32) // 64; every entry is c plus an offset within -2 .. 2, clipped to the audio blocks; the offsets of entries 1 .. 3 of a row are distinct and nonzero.
All inputs are finite; a program needn't handle non-finite values.
Results may differ from the reference program's by a relative error of at most 0.0034.
Values may be sent and summed in bfloat16 or wider, within the bound.
No kernel may reach another device: no remote copies, remote signals or barrier semaphores. Data moves between devices by JAX's collectives and lax.ppermute only.
A program may use at most 64 MiB of HBM per device.

```python
import jax
import jax.numpy as jnp
from jax import lax

HEADS = 16
HD = 128
ABLK = 32
VBLK = 128
REACH = 2
KLIST = 4
TOKA = 1024
TOKV = 8192
ABLOCKS = 32
VBLOCKS = 64


def draw_audio_qkv(key, part):
    key = jax.random.fold_in(key, 1)
    spread = jnp.array([1.6, 1.6, 1.0], jnp.float32)[None, :, None, None]
    drawn = jnp.clip(jax.random.normal(key, (TOKA, 3, HEADS, HD), jnp.float32), -5.0, 5.0) * spread
    return drawn.astype(jnp.bfloat16)


def draw_video_q(key, part):
    key = jax.random.fold_in(key, 2)
    drawn = jnp.clip(jax.random.normal(key, (TOKV, HEADS, HD), jnp.float32), -5.0, 5.0) * 1.6
    return drawn.astype(jnp.bfloat16)


def draw_pairs(key, part):
    key = jax.random.fold_in(key, 3)
    centers = jnp.arange(VBLOCKS) * ABLOCKS // VBLOCKS
    offsets = jnp.concatenate([jnp.arange(-REACH, 0), jnp.arange(1, REACH + 1)])
    orders = jax.vmap(lambda one_key: jax.random.permutation(one_key, 2 * REACH))(jax.random.split(key, VBLOCKS))
    picked = offsets[orders[:, :KLIST - 1]].astype(jnp.int32)
    shifted = jnp.concatenate([jnp.zeros((VBLOCKS, 1), jnp.int32), picked], axis=1)
    return jnp.clip(centers[:, None] + shifted, 0, ABLOCKS - 1).astype(jnp.int32)


def set_ends(result, stream_key, least, high):
    longest = result.shape.index(max(result.shape))
    spots = []
    for shift in (0, 1):
        where = [jax.random.randint(jax.random.fold_in(stream_key, axis), (), 0, length) for axis, length in enumerate(result.shape)]
        where[longest] = (where[longest] + shift) % result.shape[longest]
        spots.append(tuple(where))
    return result.at[spots[0]].set(least).at[spots[1]].set(high)


def setup_inputs(seed: int = 0, part: int = 0) -> dict:
    splits = jax.random.split(jax.random.key(seed), 5)
    own_keys = jax.random.split(jax.random.fold_in(splits[4], part), 5)
    audio_qkv = draw_audio_qkv(jax.random.fold_in(jax.random.fold_in(splits[4], part), 71), part)
    video_q = draw_video_q(jax.random.fold_in(jax.random.fold_in(splits[4], part), 71), part)
    pairs = draw_pairs(jax.random.fold_in(jax.random.fold_in(splits[4], part), 71), part)
    counts = set_ends(jax.random.randint(own_keys[3], (VBLOCKS,), 1, KLIST + 1), jax.random.fold_in(own_keys[3], 1), 1, KLIST).astype(jnp.int32)
    return dict(audio_qkv=audio_qkv, video_q=video_q, pairs=pairs, counts=counts)


def block_count(total, most):
    count = max(1, total // most)
    while total % count:
        count += 1
    return count


def reference(audio_qkv, video_q, pairs, counts):
    score_scale = HD ** -0.5
    by_head = audio_qkv.transpose(2, 1, 0, 3)
    query_blocks = block_count(TOKA, 512)

    def one_head(head_data):
        queries = head_data[0].reshape(query_blocks, -1, HD)

        def one_block(query_block):
            scores = jnp.dot(query_block, head_data[1].T, preferred_element_type=jnp.float32) * score_scale
            row_top = jnp.max(scores, axis=1)
            weights = jnp.exp(scores - row_top[:, None])
            row_total = jnp.sum(weights, axis=1)
            summed = jnp.dot(weights.astype(jnp.bfloat16), head_data[2], preferred_element_type=jnp.float32)
            return summed / row_total[:, None]

        return lax.map(one_block, queries).reshape(TOKA, HD)

    audio_out = lax.map(one_head, by_head).transpose(1, 0, 2).astype(jnp.bfloat16)

    key_blocks = audio_qkv[:, 1].reshape(ABLOCKS, ABLK, HEADS, HD)
    value_blocks = audio_qkv[:, 2].reshape(ABLOCKS, ABLK, HEADS, HD)
    video_blocks = video_q.reshape(VBLOCKS, VBLK, HEADS, HD)

    def one_video(item):
        query_block, chosen, live = item
        key_rows = key_blocks[chosen].reshape(KLIST * ABLK, HEADS, HD)
        value_rows = value_blocks[chosen].reshape(KLIST * ABLK, HEADS, HD)
        scores = jnp.einsum("qhd,khd->hqk", query_block.astype(jnp.float32), key_rows.astype(jnp.float32)) * score_scale
        slot_live = (jnp.arange(KLIST * ABLK) // ABLK) < live
        scores = jnp.where(slot_live[None, None, :], scores, -1e30)
        row_top = jnp.max(scores, axis=2)
        weights = jnp.exp(scores - row_top[:, :, None])
        row_total = jnp.sum(weights, axis=2)
        rounded = lax.optimization_barrier(weights.astype(jnp.bfloat16)).astype(jnp.float32)
        summed = jnp.einsum("hqk,khd->qhd", rounded, value_rows.astype(jnp.float32))
        return (summed / row_total.transpose(1, 0)[:, :, None]).astype(jnp.bfloat16)

    video_out = lax.map(one_video, (video_blocks, pairs, counts)).reshape(TOKV, HEADS, HD)
    return audio_out, video_out
```

```python
import functools

import jax
import jax.numpy as jnp
from jax import lax
from jax.experimental import pallas as pl
from jax.experimental.pallas import tpu as pltpu
from jax.sharding import PartitionSpec as P

ABLK = 32
VBLK = 128
LOG2E = 1.4426950408889634
LOWEST = -1e30
VMEM_LIMIT = 48 * 1024 * 1024


def params():
    return pltpu.CompilerParams(vmem_limit_bytes=VMEM_LIMIT)


def whole(shape):
    return pl.BlockSpec(shape, lambda *unused: (0,) * len(shape))


def arrange_kernel(rows, qkv_ref, send_ref, kv_ref):
    for part in range(3):
        by_head = jnp.swapaxes(qkv_ref[:, part], 0, 1)
        send_ref[:, part * rows : (part + 1) * rows] = by_head
        if part:
            kv_ref[:, (part - 1) * rows : part * rows] = by_head


def arrange(audio_qkv):
    rows, unused, heads, size = audio_qkv.shape
    dtype = audio_qkv.dtype
    return pl.pallas_call(
        functools.partial(arrange_kernel, rows),
        out_shape=(
            jax.ShapeDtypeStruct((heads, 3 * rows, size), dtype),
            jax.ShapeDtypeStruct((heads, 2 * rows, size), dtype),
        ),
        compiler_params=params(),
        name="arrange",
    )(audio_qkv)


def attend_kernel(query_rows, rows, scale, fused, *refs):
    if fused:
        recv_ref, out_ref = refs
        query_ref, base = recv_ref, query_rows
    else:
        query_ref, recv_ref, out_ref = refs
        base = 0
    sources = recv_ref.shape[0]
    size = recv_ref.shape[2]
    group = max(1, 256 // query_rows)
    key_group = min(sources, 16)
    factor = scale * LOG2E
    for first in range(0, sources, group):
        queries = query_ref[first : first + group, :query_rows].reshape(group * query_rows, size)

        def advance(step, state):
            top, total, summed = state
            at = pl.ds(step * key_group, key_group)
            keys = recv_ref[at, base : base + rows].reshape(key_group * rows, size)
            values = recv_ref[at, base + rows : base + 2 * rows].reshape(key_group * rows, size)
            scores = lax.dot_general(
                queries, keys, (((1,), (1,)), ((), ())), preferred_element_type=jnp.float32
            )
            new_top = jnp.max(scores, axis=1, keepdims=True)
            if state[0] is not None:
                new_top = jnp.maximum(top, new_top)
            weights = jnp.exp2((scores - new_top) * factor)
            new_total = jnp.sum(weights, axis=1, keepdims=True)
            new_summed = jnp.dot(
                weights.astype(jnp.bfloat16), values, preferred_element_type=jnp.float32
            )
            if state[0] is not None:
                rescale = jnp.exp2((top - new_top) * factor)
                new_total = total * rescale + new_total
                new_summed = summed * rescale + new_summed
            return new_top, new_total, new_summed

        state = advance(0, (None, None, None))
        if sources > key_group:
            state = lax.fori_loop(1, sources // key_group, advance, state)
        result = (state[2] / state[1]).astype(jnp.bfloat16)
        out_ref[first : first + group] = result.reshape(group, query_rows, size)


def attend(operands, sources, query_rows, rows, size, scale):
    work = sources * query_rows * sources * rows
    return pl.pallas_call(
        functools.partial(attend_kernel, query_rows, rows, scale, len(operands) == 1),
        out_shape=jax.ShapeDtypeStruct((sources, query_rows, size), jnp.bfloat16),
        compiler_params=params(),
        cost_estimate=pl.CostEstimate(
            flops=4 * work * size, bytes_accessed=8 * sources * rows * size, transcendentals=work
        ),
        name="attend",
    )(*operands)


def collect_kernel(by_head_ref, out_ref):
    out_ref[...] = jnp.swapaxes(by_head_ref[...], 0, 1)


def collect(by_head):
    heads, rows, size = by_head.shape
    return pl.pallas_call(
        collect_kernel,
        out_shape=jax.ShapeDtypeStruct((rows, heads, size), by_head.dtype),
        compiler_params=params(),
        name="collect",
    )(by_head)


def video_kernel(
    rows, slots, scale, pairs_ref, counts_ref, first_ref,
    video_ref, before_ref, own_ref, after_ref, out_ref,
    near_keys, near_values, keys_ref, values_ref, queries_ref, result_ref,
):
    block = pl.program_id(0)
    heads = own_ref.shape[0]

    @pl.when(block == 0)
    def _():
        for place, ref in enumerate((before_ref, own_ref, after_ref)):
            near_keys[:, place * rows : (place + 1) * rows] = ref[:, :rows]
            near_values[:, place * rows : (place + 1) * rows] = ref[:, rows:]

    queries_ref[...] = jnp.swapaxes(video_ref[...], 0, 1)
    for slot in range(slots):
        start = pl.multiple_of((pairs_ref[block, slot] - first_ref[0]) * ABLK, ABLK)
        here = slice(slot * ABLK, (slot + 1) * ABLK)
        keys_ref[:, here] = near_keys[:, pl.ds(start, ABLK)]
        values_ref[:, here] = near_values[:, pl.ds(start, ABLK)]
    column = lax.broadcasted_iota(jnp.int32, (VBLK, slots * ABLK), 1)
    live = column < counts_ref[block] * ABLK
    factor = scale * LOG2E
    for head in range(heads):
        scores = lax.dot_general(
            queries_ref[head], keys_ref[head], (((1,), (1,)), ((), ())),
            preferred_element_type=jnp.float32,
        )
        scores = jnp.where(live, scores, LOWEST)
        top = jnp.max(scores, axis=1, keepdims=True)
        weights = jnp.exp2((scores - top) * factor)
        total = jnp.sum(weights, axis=1, keepdims=True)
        summed = jnp.dot(
            weights.astype(jnp.bfloat16), values_ref[head], preferred_element_type=jnp.float32
        )
        result_ref[head] = (summed / total).astype(jnp.bfloat16)
    out_ref[...] = jnp.swapaxes(result_ref[...], 0, 1)


def video(video_q, before, own, after, pairs, counts, first, scale):
    total, heads, size = video_q.shape
    rows = own.shape[1] // 2
    slots = pairs.shape[1]
    blocks = total // VBLK
    block_spec = pl.BlockSpec((VBLK, heads, size), lambda i, *unused: (i, 0, 0))
    work = total * heads * slots * ABLK
    return pl.pallas_call(
        functools.partial(video_kernel, rows, slots, scale),
        grid_spec=pltpu.PrefetchScalarGridSpec(
            num_scalar_prefetch=3,
            grid=(blocks,),
            in_specs=[block_spec] + [whole(own.shape)] * 3,
            out_specs=block_spec,
            scratch_shapes=[
                pltpu.VMEM((heads, 3 * rows, size), jnp.bfloat16),
                pltpu.VMEM((heads, 3 * rows, size), jnp.bfloat16),
                pltpu.VMEM((heads, slots * ABLK, size), jnp.bfloat16),
                pltpu.VMEM((heads, slots * ABLK, size), jnp.bfloat16),
                pltpu.VMEM((heads, VBLK, size), jnp.bfloat16),
                pltpu.VMEM((heads, VBLK, size), jnp.bfloat16),
            ],
        ),
        out_shape=jax.ShapeDtypeStruct(video_q.shape, jnp.bfloat16),
        compiler_params=params(),
        cost_estimate=pl.CostEstimate(
            flops=4 * work * size, bytes_accessed=4 * total * heads * size, transcendentals=work
        ),
        name="video",
    )(pairs, counts, first, video_q, before, own, after)


def local(audio_qkv, video_q, pairs, counts):
    devices = lax.axis_size("seq")
    rows, unused, heads, size = audio_qkv.shape
    bands = devices // heads
    band_rows = rows // bands
    scale = size ** (-0.5)
    send, kv = arrange(audio_qkv)
    ends = devices - 1
    before = lax.ppermute(kv, "seq", [(i, i + 1) for i in range(ends)])
    after = lax.ppermute(kv, "seq", [(i + 1, i) for i in range(ends)])

    def exchange(value):
        return lax.all_to_all(value, "seq", split_axis=0, concat_axis=0, tiled=True)

    if bands == 1:
        operands = (exchange(send),)
    else:
        queries = exchange(send[:, :rows].reshape(devices, band_rows, size))
        spread = jnp.broadcast_to(kv[:, None], (heads, bands, 2 * rows, size))
        operands = (queries, exchange(spread.reshape(devices, 2 * rows, size)))
    head_out = attend(operands, devices, band_rows, rows, size, scale)
    audio_attn = collect(exchange(head_out).reshape(heads, rows, size))
    first = (lax.axis_index("seq") * (rows // ABLK) - rows // ABLK).astype(jnp.int32).reshape(1)
    video_cross = video(video_q, before, kv, after, pairs, counts, first, scale)
    return audio_attn, video_cross


def solution(mesh):
    in_specs = (
        P(("groups", "seq"), None, None, None),
        P(("groups", "seq"), None, None),
        P(("groups", "seq"), None),
        P(("groups", "seq")),
    )
    out_specs = (P(("groups", "seq"), None, None), P(("groups", "seq"), None, None))
    return jax.shard_map(local, mesh=mesh, in_specs=in_specs, out_specs=out_specs, check_vma=False)
```

```python
import functools

import jax
import jax.numpy as jnp
from jax import lax
from jax.experimental import pallas as pl
from jax.experimental.pallas import tpu as pltpu
from jax.sharding import PartitionSpec as P

ABLK = 32
VBLK = 128
LOG2E = 1.4426950408889634
LOWEST = -1e30
VMEM_LIMIT = 48 * 1024 * 1024


def params():
    return pltpu.CompilerParams(vmem_limit_bytes=VMEM_LIMIT)


def whole(shape):
    return pl.BlockSpec(shape, lambda *unused: (0,) * len(shape))


def arrange_kernel(rows, qkv_ref, send_ref, kv_ref, came, turned, in_sems, out_sems):
    order = (1, 2, 0)
    arrivals = [
        pltpu.make_async_copy(qkv_ref.at[:, part], came.at[part], in_sems.at[part]) for part in order
    ]
    for arrival in arrivals:
        arrival.start()
    departures = []
    for arrival, part in zip(arrivals, order):
        arrival.wait()
        by_head = jnp.swapaxes(came[part], 0, 1)
        turned[part] = by_head
        departure = pltpu.make_async_copy(
            turned.at[part], send_ref.at[:, pl.ds(part * rows, rows)], out_sems.at[part]
        )
        departure.start()
        departures.append(departure)
        if part:
            kv_ref[:, (part - 1) * rows : part * rows] = by_head
    for departure in departures:
        departure.wait()


def arrange(audio_qkv):
    rows, parts, heads, size = audio_qkv.shape
    dtype = audio_qkv.dtype
    return pl.pallas_call(
        functools.partial(arrange_kernel, rows),
        in_specs=[pl.BlockSpec(memory_space=pltpu.HBM)],
        out_specs=(
            pl.BlockSpec(memory_space=pltpu.HBM),
            pl.BlockSpec(memory_space=pltpu.VMEM),
        ),
        out_shape=(
            pltpu.HBM((heads, parts * rows, size), dtype),
            jax.ShapeDtypeStruct((heads, 2 * rows, size), dtype),
        ),
        scratch_shapes=[
            pltpu.VMEM((parts, rows, heads, size), dtype),
            pltpu.VMEM((parts, heads, rows, size), dtype),
            pltpu.SemaphoreType.DMA((parts,)),
            pltpu.SemaphoreType.DMA((parts,)),
        ],
        compiler_params=params(),
        name="arrange",
    )(pltpu.with_memory_space_constraint(audio_qkv, pltpu.HBM))


def attend_kernel(query_rows, rows, scale, fused, *refs):
    if fused:
        recv_ref, out_ref, held, sems = refs
        query_ref, base = recv_ref, query_rows
    else:
        query_ref, recv_ref, out_ref, held, sems = refs
        base = 0
    sources = recv_ref.shape[0]
    size = recv_ref.shape[2]
    group = max(1, 256 // query_rows)
    key_group = min(sources, 16)
    factor = scale * LOG2E
    departures = []
    for first in range(0, sources, group):
        queries = query_ref[first : first + group, :query_rows].reshape(group * query_rows, size)

        def advance(step, state):
            top, total, summed = state
            at = pl.ds(step * key_group, key_group)
            keys = recv_ref[at, base : base + rows].reshape(key_group * rows, size)
            values = recv_ref[at, base + rows : base + 2 * rows].reshape(key_group * rows, size)
            scores = lax.dot_general(
                queries, keys, (((1,), (1,)), ((), ())), preferred_element_type=jnp.float32
            )
            new_top = jnp.max(scores, axis=1, keepdims=True)
            if state[0] is not None:
                new_top = jnp.maximum(top, new_top)
            weights = jnp.exp2((scores - new_top) * factor)
            new_total = jnp.sum(weights, axis=1, keepdims=True)
            new_summed = jnp.dot(
                weights.astype(jnp.bfloat16), values, preferred_element_type=jnp.float32
            )
            if state[0] is not None:
                rescale = jnp.exp2((top - new_top) * factor)
                new_total = total * rescale + new_total
                new_summed = summed * rescale + new_summed
            return new_top, new_total, new_summed

        state = advance(0, (None, None, None))
        if sources > key_group:
            state = lax.fori_loop(1, sources // key_group, advance, state)
        result = (state[2] / state[1]).astype(jnp.bfloat16)
        held[first : first + group] = result.reshape(group, query_rows, size)
        departure = pltpu.make_async_copy(
            held.at[pl.ds(first, group)], out_ref.at[pl.ds(first, group)], sems.at[first // group]
        )
        departure.start()
        departures.append(departure)
    for departure in departures:
        departure.wait()


def attend(operands, sources, query_rows, rows, size, scale):
    work = sources * query_rows * sources * rows
    return pl.pallas_call(
        functools.partial(attend_kernel, query_rows, rows, scale, len(operands) == 1),
        in_specs=[pl.BlockSpec(memory_space=pltpu.VMEM)] * len(operands),
        out_specs=pl.BlockSpec(memory_space=pltpu.HBM),
        out_shape=pltpu.HBM((sources, query_rows, size), jnp.bfloat16),
        scratch_shapes=[
            pltpu.VMEM((sources, query_rows, size), jnp.bfloat16),
            pltpu.SemaphoreType.DMA((sources * query_rows // 256,)),
        ],
        compiler_params=params(),
        cost_estimate=pl.CostEstimate(
            flops=4 * work * size, bytes_accessed=8 * sources * rows * size, transcendentals=work
        ),
        name="attend",
    )(*operands)


def collect_kernel(by_head_ref, out_ref):
    out_ref[...] = jnp.swapaxes(by_head_ref[...], 0, 1)


def collect(by_head):
    heads, rows, size = by_head.shape
    return pl.pallas_call(
        collect_kernel,
        out_shape=jax.ShapeDtypeStruct((rows, heads, size), by_head.dtype),
        compiler_params=params(),
        name="collect",
    )(by_head)


def video_kernel(
    rows, slots, scale, group, pairs_ref, counts_ref, where_ref,
    video_ref, own_ref, core_ref, chip_ref, out_ref,
    near_keys, near_values, keys_ref, values_ref, queries_ref, result_ref,
):
    block = pl.program_id(0)
    heads, unused, size = own_ref.shape

    @pl.when(block == 0)
    def _():
        for ref, place in ((own_ref, rows), (core_ref, where_ref[1]), (chip_ref, where_ref[2])):
            at = pl.ds(pl.multiple_of(place, rows), rows)
            near_keys[:, at] = ref[:, :rows]
            near_values[:, at] = ref[:, rows:]
        values_ref[:, :, size:] = jnp.ones((heads, slots * ABLK, size), jnp.bfloat16)

    queries_ref[...] = jnp.swapaxes(video_ref[...], 0, 1)
    for slot in range(slots):
        start = pl.multiple_of((pairs_ref[block, slot] - where_ref[0]) * ABLK, ABLK)
        here = slice(slot * ABLK, (slot + 1) * ABLK)
        keys_ref[:, here] = near_keys[:, pl.ds(start, ABLK)]
        values_ref[:, here, :size] = near_values[:, pl.ds(start, ABLK)]
    column = lax.broadcasted_iota(jnp.int32, (VBLK, slots * ABLK), 1)
    live = column < counts_ref[block] * ABLK
    factor = scale * LOG2E
    for first in range(0, heads, group):
        members = range(first, first + group)
        scores = [
            lax.dot_general(
                queries_ref[head], keys_ref[head], (((1,), (1,)), ((), ())),
                preferred_element_type=jnp.float32,
            )
            for head in members
        ]
        scores = jnp.stack([jnp.where(live, one, LOWEST) for one in scores])
        top = jnp.max(scores, axis=2, keepdims=True)
        weights = jnp.exp2((scores - top) * factor).astype(jnp.bfloat16)
        summed = [
            jnp.dot(weights[head - first], values_ref[head], preferred_element_type=jnp.float32)
            for head in members
        ]
        for head in members:
            both = summed[head - first]
            result_ref[head] = (both[:, :size] / both[:, size:]).astype(jnp.bfloat16)
    out_ref[...] = jnp.swapaxes(result_ref[...], 0, 1)


def video(video_q, own, core, chip, pairs, counts, where, scale):
    total, heads, size = video_q.shape
    rows = own.shape[1] // 2
    slots = pairs.shape[1]
    blocks = total // VBLK
    block_spec = pl.BlockSpec((VBLK, heads, size), lambda i, *unused: (i, 0, 0))
    work = total * heads * slots * ABLK
    return pl.pallas_call(
        functools.partial(video_kernel, rows, slots, scale, 4),
        grid_spec=pltpu.PrefetchScalarGridSpec(
            num_scalar_prefetch=3,
            grid=(blocks,),
            in_specs=[block_spec] + [whole(own.shape)] * 3,
            out_specs=block_spec,
            scratch_shapes=[
                pltpu.VMEM((heads, 3 * rows, size), jnp.bfloat16),
                pltpu.VMEM((heads, 3 * rows, size), jnp.bfloat16),
                pltpu.VMEM((heads, slots * ABLK, size), jnp.bfloat16),
                pltpu.VMEM((heads, slots * ABLK, 2 * size), jnp.bfloat16),
                pltpu.VMEM((heads, VBLK, size), jnp.bfloat16),
                pltpu.VMEM((heads, VBLK, size), jnp.bfloat16),
            ],
        ),
        out_shape=jax.ShapeDtypeStruct(video_q.shape, jnp.bfloat16),
        compiler_params=params(),
        cost_estimate=pl.CostEstimate(
            flops=4 * work * size, bytes_accessed=4 * total * heads * size, transcendentals=work
        ),
        name="video",
    )(pairs, counts, where, video_q, own, core, chip)


def local(audio_qkv, video_q, pairs, counts):
    devices = lax.axis_size("seq")
    rows, unused, heads, size = audio_qkv.shape
    bands = devices // heads
    band_rows = rows // bands
    scale = size ** (-0.5)
    send, kv = arrange(audio_qkv)
    core_pairs = [(i, i ^ 1) for i in range(devices)]
    chip_pairs = [(i, ((i + 1) ^ 1) - 1) for i in range(1, devices - 1)]

    def exchange(value):
        return lax.all_to_all(value, "seq", split_axis=0, concat_axis=0, tiled=True)

    if bands == 1:
        operands = (exchange(send),)
    else:
        queries = exchange(send[:, :rows].reshape(devices, band_rows, size))
        spread = jnp.broadcast_to(kv[:, None], (heads, bands, 2 * rows, size))
        operands = (queries, exchange(spread.reshape(devices, 2 * rows, size)))
    core = lax.ppermute(kv, "seq", core_pairs)
    operands, late = lax.optimization_barrier((operands, kv))
    chip = lax.ppermute(late, "seq", chip_pairs)
    head_out = attend(operands, devices, band_rows, rows, size, scale)
    audio_attn = collect(exchange(head_out).reshape(heads, rows, size))
    me = lax.axis_index("seq")
    odd = me & 1
    where = jnp.stack([(me - 1) * (rows // ABLK), 2 * (1 - odd) * rows, 2 * odd * rows])
    video_cross = video(
        video_q, kv, core, chip, pairs, counts, where.astype(jnp.int32), scale
    )
    return audio_attn, video_cross


def solution(mesh):
    in_specs = (
        P(("groups", "seq"), None, None, None),
        P(("groups", "seq"), None, None),
        P(("groups", "seq"), None),
        P(("groups", "seq")),
    )
    out_specs = (P(("groups", "seq"), None, None), P(("groups", "seq"), None, None))
    return jax.shard_map(local, mesh=mesh, in_specs=in_specs, out_specs=out_specs, check_vma=False)
```

```python
import functools

import jax
import jax.numpy as jnp
from jax import lax
from jax.experimental import pallas as pl
from jax.experimental.pallas import tpu as pltpu
from jax.sharding import PartitionSpec as P

ABLK = 32
VBLK = 128
LOG2E = 1.4426950408889634
LOWEST = -1e30
VMEM_LIMIT = 48 * 1024 * 1024


def params():
    return pltpu.CompilerParams(vmem_limit_bytes=VMEM_LIMIT)


def whole(shape):
    return pl.BlockSpec(shape, lambda *unused: (0,) * len(shape))


def arrange_kernel(rows, qkv_ref, send_ref, kv_ref, came, turned, in_sems, out_sems):
    order = (1, 2, 0)
    arrivals = [
        pltpu.make_async_copy(qkv_ref.at[:, part], came.at[part], in_sems.at[part]) for part in order
    ]
    for arrival in arrivals:
        arrival.start()
    departures = []
    for arrival, part in zip(arrivals, order):
        arrival.wait()
        by_head = jnp.swapaxes(came[part], 0, 1)
        turned[part] = by_head
        departure = pltpu.make_async_copy(
            turned.at[part], send_ref.at[:, pl.ds(part * rows, rows)], out_sems.at[part]
        )
        departure.start()
        departures.append(departure)
        if part:
            kv_ref[:, (part - 1) * rows : part * rows] = by_head
    for departure in departures:
        departure.wait()


def arrange(audio_qkv):
    rows, parts, heads, size = audio_qkv.shape
    dtype = audio_qkv.dtype
    return pl.pallas_call(
        functools.partial(arrange_kernel, rows),
        in_specs=[pl.BlockSpec(memory_space=pltpu.HBM)],
        out_specs=(
            pl.BlockSpec(memory_space=pltpu.HBM),
            pl.BlockSpec(memory_space=pltpu.VMEM),
        ),
        out_shape=(
            pltpu.HBM((heads, parts * rows, size), dtype),
            jax.ShapeDtypeStruct((heads, 2 * rows, size), dtype),
        ),
        scratch_shapes=[
            pltpu.VMEM((parts, rows, heads, size), dtype),
            pltpu.VMEM((parts, heads, rows, size), dtype),
            pltpu.SemaphoreType.DMA((parts,)),
            pltpu.SemaphoreType.DMA((parts,)),
        ],
        compiler_params=params(),
        name="arrange",
    )(pltpu.with_memory_space_constraint(audio_qkv, pltpu.HBM))


def attend_kernel(query_rows, rows, scale, fused, *refs):
    if fused:
        recv_ref, out_ref, held, sems = refs
        query_ref, base = recv_ref, query_rows
    else:
        query_ref, recv_ref, out_ref, held, sems = refs
        base = 0
    sources = recv_ref.shape[0]
    size = recv_ref.shape[2]
    group = max(1, 256 // query_rows)
    key_group = min(sources, 16)
    factor = scale * LOG2E
    departures = []
    for first in range(0, sources, group):
        queries = query_ref[first : first + group, :query_rows].reshape(group * query_rows, size)

        def advance(step, state):
            top, total, summed = state
            at = pl.ds(step * key_group, key_group)
            keys = recv_ref[at, base : base + rows].reshape(key_group * rows, size)
            values = recv_ref[at, base + rows : base + 2 * rows].reshape(key_group * rows, size)
            scores = lax.dot_general(
                queries, keys, (((1,), (1,)), ((), ())), preferred_element_type=jnp.float32
            )
            new_top = jnp.max(scores, axis=1, keepdims=True)
            if state[0] is not None:
                new_top = jnp.maximum(top, new_top)
            weights = jnp.exp2((scores - new_top) * factor)
            new_total = jnp.sum(weights, axis=1, keepdims=True)
            new_summed = jnp.dot(
                weights.astype(jnp.bfloat16), values, preferred_element_type=jnp.float32
            )
            if state[0] is not None:
                rescale = jnp.exp2((top - new_top) * factor)
                new_total = total * rescale + new_total
                new_summed = summed * rescale + new_summed
            return new_top, new_total, new_summed

        state = advance(0, (None, None, None))
        if sources > key_group:
            state = lax.fori_loop(1, sources // key_group, advance, state)
        result = (state[2] / state[1]).astype(jnp.bfloat16)
        held[first : first + group] = result.reshape(group, query_rows, size)
        departure = pltpu.make_async_copy(
            held.at[pl.ds(first, group)], out_ref.at[pl.ds(first, group)], sems.at[first // group]
        )
        departure.start()
        departures.append(departure)
    for departure in departures:
        departure.wait()


def attend(operands, sources, query_rows, rows, size, scale):
    work = sources * query_rows * sources * rows
    return pl.pallas_call(
        functools.partial(attend_kernel, query_rows, rows, scale, len(operands) == 1),
        in_specs=[pl.BlockSpec(memory_space=pltpu.VMEM)] * len(operands),
        out_specs=pl.BlockSpec(memory_space=pltpu.HBM),
        out_shape=pltpu.HBM((sources, query_rows, size), jnp.bfloat16),
        scratch_shapes=[
            pltpu.VMEM((sources, query_rows, size), jnp.bfloat16),
            pltpu.SemaphoreType.DMA((sources * query_rows // 256,)),
        ],
        compiler_params=params(),
        cost_estimate=pl.CostEstimate(
            flops=4 * work * size, bytes_accessed=8 * sources * rows * size, transcendentals=work
        ),
        name="attend",
    )(*operands)


def collect_kernel(by_head_ref, out_ref):
    out_ref[...] = jnp.swapaxes(by_head_ref[...], 0, 1)


def collect(by_head):
    heads, rows, size = by_head.shape
    return pl.pallas_call(
        collect_kernel,
        out_shape=jax.ShapeDtypeStruct((rows, heads, size), by_head.dtype),
        compiler_params=params(),
        name="collect",
    )(by_head)


def video_kernel(
    rows, slots, scale, group, pairs_ref, counts_ref, where_ref,
    video_ref, own_ref, core_ref, chip_ref, out_ref,
    near_keys, near_values, keys_ref, values_ref, queries_ref, result_ref,
):
    block = pl.program_id(0)
    heads, unused, size = own_ref.shape

    @pl.when(block == 0)
    def _():
        for ref, place in ((own_ref, rows), (core_ref, where_ref[1]), (chip_ref, where_ref[2])):
            at = pl.ds(pl.multiple_of(place, rows), rows)
            near_keys[:, at] = ref[:, :rows]
            near_values[:, at] = ref[:, rows:]
        values_ref[:, :, size:] = jnp.ones((heads, slots * ABLK, size), jnp.bfloat16)

    queries_ref[...] = jnp.swapaxes(video_ref[...], 0, 1)
    for slot in range(slots):
        start = pl.multiple_of((pairs_ref[block, slot] - where_ref[0]) * ABLK, ABLK)
        here = slice(slot * ABLK, (slot + 1) * ABLK)
        keys_ref[:, here] = near_keys[:, pl.ds(start, ABLK)]
        values_ref[:, here, :size] = near_values[:, pl.ds(start, ABLK)]
    column = lax.broadcasted_iota(jnp.int32, (VBLK, slots * ABLK), 1)
    live = column < counts_ref[block] * ABLK
    factor = scale * LOG2E
    for first in range(0, heads, group):
        members = range(first, first + group)
        scores = [
            lax.dot_general(
                queries_ref[head], keys_ref[head], (((1,), (1,)), ((), ())),
                preferred_element_type=jnp.float32,
            )
            for head in members
        ]
        scores = jnp.stack([jnp.where(live, one, LOWEST) for one in scores])
        top = jnp.max(scores, axis=2, keepdims=True)
        weights = jnp.exp2((scores - top) * factor).astype(jnp.bfloat16)
        summed = [
            jnp.dot(weights[head - first], values_ref[head], preferred_element_type=jnp.float32)
            for head in members
        ]
        for head in members:
            both = summed[head - first]
            result_ref[head] = (both[:, :size] / both[:, size:]).astype(jnp.bfloat16)
    out_ref[...] = jnp.swapaxes(result_ref[...], 0, 1)


def video(video_q, own, core, chip, pairs, counts, where, scale):
    total, heads, size = video_q.shape
    rows = own.shape[1] // 2
    slots = pairs.shape[1]
    blocks = total // VBLK
    block_spec = pl.BlockSpec((VBLK, heads, size), lambda i, *unused: (i, 0, 0))
    work = total * heads * slots * ABLK
    return pl.pallas_call(
        functools.partial(video_kernel, rows, slots, scale, 4),
        grid_spec=pltpu.PrefetchScalarGridSpec(
            num_scalar_prefetch=3,
            grid=(blocks,),
            in_specs=[block_spec] + [whole(own.shape)] * 3,
            out_specs=block_spec,
            scratch_shapes=[
                pltpu.VMEM((heads, 3 * rows, size), jnp.bfloat16),
                pltpu.VMEM((heads, 3 * rows, size), jnp.bfloat16),
                pltpu.VMEM((heads, slots * ABLK, size), jnp.bfloat16),
                pltpu.VMEM((heads, slots * ABLK, 2 * size), jnp.bfloat16),
                pltpu.VMEM((heads, VBLK, size), jnp.bfloat16),
                pltpu.VMEM((heads, VBLK, size), jnp.bfloat16),
            ],
        ),
        out_shape=jax.ShapeDtypeStruct(video_q.shape, jnp.bfloat16),
        compiler_params=params(),
        cost_estimate=pl.CostEstimate(
            flops=4 * work * size, bytes_accessed=4 * total * heads * size, transcendentals=work
        ),
        name="video",
    )(pairs, counts, where, video_q, own, core, chip)


def local(audio_qkv, video_q, pairs, counts):
    devices = lax.axis_size("seq")
    rows, unused, heads, size = audio_qkv.shape
    bands = devices // heads
    band_rows = rows // bands
    scale = size ** (-0.5)
    send, kv = arrange(audio_qkv)
    core_pairs = [(i, i ^ 1) for i in range(devices)]
    chip_pairs = [(i, ((i + 1) ^ 1) - 1) for i in range(1, devices - 1)]

    def exchange(value):
        return lax.all_to_all(value, "seq", split_axis=0, concat_axis=0, tiled=True)

    if bands == 1:
        operands = (exchange(send),)
    else:
        queries = exchange(send[:, :rows].reshape(devices, band_rows, size))
        spread = jnp.broadcast_to(kv[:, None], (heads, bands, 2 * rows, size))
        operands = (queries, exchange(spread.reshape(devices, 2 * rows, size)))
    core = lax.ppermute(kv, "seq", core_pairs)
    chip = lax.ppermute(kv, "seq", chip_pairs)
    me = lax.axis_index("seq")
    odd = me & 1
    where = jnp.stack([(me - 1) * (rows // ABLK), 2 * (1 - odd) * rows, 2 * odd * rows])
    video_cross = video(
        video_q, kv, core, chip, pairs, counts, where.astype(jnp.int32), scale
    )
    operands, video_cross = lax.optimization_barrier((operands, video_cross))
    head_out = attend(operands, devices, band_rows, rows, size, scale)
    audio_attn = collect(exchange(head_out).reshape(heads, rows, size))
    return audio_attn, video_cross


def solution(mesh):
    in_specs = (
        P(("groups", "seq"), None, None, None),
        P(("groups", "seq"), None, None),
        P(("groups", "seq"), None),
        P(("groups", "seq")),
    )
    out_specs = (P(("groups", "seq"), None, None), P(("groups", "seq"), None, None))
    return jax.shard_map(local, mesh=mesh, in_specs=in_specs, out_specs=out_specs, check_vma=False)
```

```python
import functools

import jax
import jax.numpy as jnp
from jax import lax
from jax.experimental import pallas as pl
from jax.experimental.pallas import tpu as pltpu
from jax.sharding import PartitionSpec as P

ABLK = 32
VBLK = 128
LOG2E = 1.4426950408889634
LOWEST = -1e30
VMEM_LIMIT = 48 * 1024 * 1024


def params():
    return pltpu.CompilerParams(vmem_limit_bytes=VMEM_LIMIT)


def whole(shape):
    return pl.BlockSpec(shape, lambda *unused: (0,) * len(shape))


def arrange_kernel(rows, pieces, qkv_ref, queries_ref, kv_ref, came, sems):
    step = rows // pieces
    arrivals = [
        pltpu.make_async_copy(
            qkv_ref.at[pl.ds(piece * step, step)], came.at[piece], sems.at[piece]
        )
        for piece in range(pieces)
    ]
    for arrival in arrivals:
        arrival.start()
    for piece, arrival in enumerate(arrivals):
        arrival.wait()
        at = piece * step
        queries_ref[:, at : at + step] = jnp.swapaxes(came[piece, :, 0], 0, 1)
        kv_ref[:, at : at + step] = jnp.swapaxes(came[piece, :, 1], 0, 1)
        kv_ref[:, rows + at : rows + at + step] = jnp.swapaxes(came[piece, :, 2], 0, 1)


def arrange(audio_qkv):
    rows, parts, heads, size = audio_qkv.shape
    dtype = audio_qkv.dtype
    pieces = 4
    return pl.pallas_call(
        functools.partial(arrange_kernel, rows, pieces),
        in_specs=[pl.BlockSpec(memory_space=pltpu.HBM)],
        out_specs=(pl.BlockSpec(memory_space=pltpu.VMEM),) * 2,
        out_shape=(
            jax.ShapeDtypeStruct((heads, rows, size), dtype),
            jax.ShapeDtypeStruct((heads, 2 * rows, size), dtype),
        ),
        scratch_shapes=[
            pltpu.VMEM((pieces, rows // pieces, parts, heads, size), dtype),
            pltpu.SemaphoreType.DMA((pieces,)),
        ],
        compiler_params=params(),
        name="arrange",
    )(pltpu.with_memory_space_constraint(audio_qkv, pltpu.HBM))


def join_kernel(pieces, queries_ref, kv_ref, send_ref, sems):
    heads, rows, unused = queries_ref.shape
    step = heads // pieces
    departures = []
    for piece in range(pieces):
        at = pl.ds(piece * step, step)
        for half, ref in enumerate((queries_ref, kv_ref)):
            departures.append(
                pltpu.make_async_copy(
                    ref.at[at],
                    send_ref.at[at, pl.ds(half * rows, ref.shape[1])],
                    sems.at[2 * piece + half],
                )
            )
    for departure in departures:
        departure.start()
    for departure in departures:
        departure.wait()


def join(queries, kv):
    heads, rows, size = queries.shape
    pieces = 2
    return pl.pallas_call(
        functools.partial(join_kernel, pieces),
        in_specs=[pl.BlockSpec(memory_space=pltpu.VMEM)] * 2,
        out_specs=pl.BlockSpec(memory_space=pltpu.HBM),
        out_shape=pltpu.HBM((heads, rows + kv.shape[1], size), queries.dtype),
        scratch_shapes=[pltpu.SemaphoreType.DMA((2 * pieces,))],
        compiler_params=params(),
        name="join",
    )(queries, kv)


def attend_kernel(query_rows, rows, scale, fused, *refs):
    if fused:
        recv_ref, out_ref, held, sems = refs
        query_ref, base = recv_ref, query_rows
    else:
        query_ref, recv_ref, out_ref, held, sems = refs
        base = 0
    sources = recv_ref.shape[0]
    size = recv_ref.shape[2]
    group = max(1, 256 // query_rows)
    key_group = min(sources, 16)
    factor = scale * LOG2E
    departures = []
    for first in range(0, sources, group):
        queries = query_ref[first : first + group, :query_rows].reshape(group * query_rows, size)

        def advance(step, state):
            top, total, summed = state
            at = pl.ds(step * key_group, key_group)
            keys = recv_ref[at, base : base + rows].reshape(key_group * rows, size)
            values = recv_ref[at, base + rows : base + 2 * rows].reshape(key_group * rows, size)
            scores = lax.dot_general(
                queries, keys, (((1,), (1,)), ((), ())), preferred_element_type=jnp.float32
            )
            new_top = jnp.max(scores, axis=1, keepdims=True)
            if state[0] is not None:
                new_top = jnp.maximum(top, new_top)
            weights = jnp.exp2((scores - new_top) * factor)
            new_total = jnp.sum(weights, axis=1, keepdims=True)
            new_summed = jnp.dot(
                weights.astype(jnp.bfloat16), values, preferred_element_type=jnp.float32
            )
            if state[0] is not None:
                rescale = jnp.exp2((top - new_top) * factor)
                new_total = total * rescale + new_total
                new_summed = summed * rescale + new_summed
            return new_top, new_total, new_summed

        state = advance(0, (None, None, None))
        if sources > key_group:
            state = lax.fori_loop(1, sources // key_group, advance, state)
        result = (state[2] / state[1]).astype(jnp.bfloat16)
        held[first : first + group] = result.reshape(group, query_rows, size)
        departure = pltpu.make_async_copy(
            held.at[pl.ds(first, group)], out_ref.at[pl.ds(first, group)], sems.at[first // group]
        )
        departure.start()
        departures.append(departure)
    for departure in departures:
        departure.wait()


def attend(operands, sources, query_rows, rows, size, scale):
    work = sources * query_rows * sources * rows
    return pl.pallas_call(
        functools.partial(attend_kernel, query_rows, rows, scale, len(operands) == 1),
        in_specs=[pl.BlockSpec(memory_space=pltpu.VMEM)] * len(operands),
        out_specs=pl.BlockSpec(memory_space=pltpu.HBM),
        out_shape=pltpu.HBM((sources, query_rows, size), jnp.bfloat16),
        scratch_shapes=[
            pltpu.VMEM((sources, query_rows, size), jnp.bfloat16),
            pltpu.SemaphoreType.DMA((sources * query_rows // 256,)),
        ],
        compiler_params=params(),
        cost_estimate=pl.CostEstimate(
            flops=4 * work * size, bytes_accessed=8 * sources * rows * size, transcendentals=work
        ),
        name="attend",
    )(*operands)


def collect_kernel(by_head_ref, out_ref):
    out_ref[...] = jnp.swapaxes(by_head_ref[...], 0, 1)


def collect(by_head):
    heads, rows, size = by_head.shape
    return pl.pallas_call(
        collect_kernel,
        out_shape=jax.ShapeDtypeStruct((rows, heads, size), by_head.dtype),
        compiler_params=params(),
        name="collect",
    )(by_head)


def video_kernel(
    rows, slots, scale, group, pairs_ref, counts_ref, where_ref,
    video_ref, own_ref, core_ref, chip_ref, out_ref,
    near_keys, near_values, keys_ref, values_ref, queries_ref, result_ref,
):
    block = pl.program_id(0)
    heads, unused, size = own_ref.shape

    @pl.when(block == 0)
    def _():
        for ref, place in ((own_ref, rows), (core_ref, where_ref[1]), (chip_ref, where_ref[2])):
            at = pl.ds(pl.multiple_of(place, rows), rows)
            near_keys[:, at] = ref[:, :rows]
            near_values[:, at] = ref[:, rows:]
        values_ref[:, :, size:] = jnp.ones((heads, slots * ABLK, size), jnp.bfloat16)

    queries_ref[...] = jnp.swapaxes(video_ref[...], 0, 1)
    for slot in range(slots):
        start = pl.multiple_of((pairs_ref[block, slot] - where_ref[0]) * ABLK, ABLK)
        here = slice(slot * ABLK, (slot + 1) * ABLK)
        keys_ref[:, here] = near_keys[:, pl.ds(start, ABLK)]
        values_ref[:, here, :size] = near_values[:, pl.ds(start, ABLK)]
    column = lax.broadcasted_iota(jnp.int32, (VBLK, slots * ABLK), 1)
    live = column < counts_ref[block] * ABLK
    factor = scale * LOG2E
    for first in range(0, heads, group):
        members = range(first, first + group)
        scores = [
            lax.dot_general(
                queries_ref[head], keys_ref[head], (((1,), (1,)), ((), ())),
                preferred_element_type=jnp.float32,
            )
            for head in members
        ]
        scores = jnp.stack([jnp.where(live, one, LOWEST) for one in scores])
        top = jnp.max(scores, axis=2, keepdims=True)
        weights = jnp.exp2((scores - top) * factor).astype(jnp.bfloat16)
        summed = [
            jnp.dot(weights[head - first], values_ref[head], preferred_element_type=jnp.float32)
            for head in members
        ]
        for head in members:
            both = summed[head - first]
            result_ref[head] = (both[:, :size] / both[:, size:]).astype(jnp.bfloat16)
    out_ref[...] = jnp.swapaxes(result_ref[...], 0, 1)


def video(video_q, own, core, chip, pairs, counts, where, scale):
    total, heads, size = video_q.shape
    rows = own.shape[1] // 2
    slots = pairs.shape[1]
    blocks = total // VBLK
    block_spec = pl.BlockSpec((VBLK, heads, size), lambda i, *unused: (i, 0, 0))
    work = total * heads * slots * ABLK
    return pl.pallas_call(
        functools.partial(video_kernel, rows, slots, scale, 4),
        grid_spec=pltpu.PrefetchScalarGridSpec(
            num_scalar_prefetch=3,
            grid=(blocks,),
            in_specs=[block_spec] + [whole(own.shape)] * 3,
            out_specs=block_spec,
            scratch_shapes=[
                pltpu.VMEM((heads, 3 * rows, size), jnp.bfloat16),
                pltpu.VMEM((heads, 3 * rows, size), jnp.bfloat16),
                pltpu.VMEM((heads, slots * ABLK, size), jnp.bfloat16),
                pltpu.VMEM((heads, slots * ABLK, 2 * size), jnp.bfloat16),
                pltpu.VMEM((heads, VBLK, size), jnp.bfloat16),
                pltpu.VMEM((heads, VBLK, size), jnp.bfloat16),
            ],
        ),
        out_shape=jax.ShapeDtypeStruct(video_q.shape, jnp.bfloat16),
        compiler_params=params(),
        cost_estimate=pl.CostEstimate(
            flops=4 * work * size, bytes_accessed=4 * total * heads * size, transcendentals=work
        ),
        name="video",
    )(pairs, counts, where, video_q, own, core, chip)


def local(audio_qkv, video_q, pairs, counts):
    devices = lax.axis_size("seq")
    rows, unused, heads, size = audio_qkv.shape
    bands = devices // heads
    band_rows = rows // bands
    scale = size ** (-0.5)
    queries, kv = arrange(audio_qkv)
    core_pairs = [(i, i ^ 1) for i in range(devices)]
    chip_pairs = [(i, ((i + 1) ^ 1) - 1) for i in range(1, devices - 1)]

    chip = lax.ppermute(kv, "seq", chip_pairs)

    def exchange(value):
        return lax.all_to_all(value, "seq", split_axis=0, concat_axis=0, tiled=True)

    if bands == 1:
        operands = (exchange(join(queries, kv)),)
    else:
        queries = exchange(queries.reshape(devices, band_rows, size))
        spread = jnp.broadcast_to(kv[:, None], (heads, bands, 2 * rows, size))
        operands = (queries, exchange(spread.reshape(devices, 2 * rows, size)))
    core = lax.ppermute(kv, "seq", core_pairs)
    me = lax.axis_index("seq")
    odd = me & 1
    where = jnp.stack([(me - 1) * (rows // ABLK), 2 * (1 - odd) * rows, 2 * odd * rows])
    video_cross = video(
        video_q, kv, core, chip, pairs, counts, where.astype(jnp.int32), scale
    )
    operands, video_cross = lax.optimization_barrier((operands, video_cross))
    head_out = attend(operands, devices, band_rows, rows, size, scale)
    audio_attn = collect(exchange(head_out).reshape(heads, rows, size))
    return audio_attn, video_cross


def solution(mesh):
    in_specs = (
        P(("groups", "seq"), None, None, None),
        P(("groups", "seq"), None, None),
        P(("groups", "seq"), None),
        P(("groups", "seq")),
    )
    out_specs = (P(("groups", "seq"), None, None), P(("groups", "seq"), None, None))
    return jax.shard_map(local, mesh=mesh, in_specs=in_specs, out_specs=out_specs, check_vma=False)
```

```python
import functools

import jax
import jax.numpy as jnp
from jax import lax
from jax.experimental import pallas as pl
from jax.experimental.pallas import tpu as pltpu
from jax.sharding import PartitionSpec as P

ABLK = 32
VBLK = 128
LOG2E = 1.4426950408889634
LOWEST = -1e30
VMEM_LIMIT = 48 * 1024 * 1024


def params():
    return pltpu.CompilerParams(vmem_limit_bytes=VMEM_LIMIT)


def whole(shape):
    return pl.BlockSpec(shape, lambda *unused: (0,) * len(shape))


def arrange_kernel(rows, pieces, qkv_ref, queries_ref, kv_ref, came, sems):
    step = rows // pieces
    arrivals = [
        pltpu.make_async_copy(
            qkv_ref.at[pl.ds(piece * step, step)], came.at[piece], sems.at[piece]
        )
        for piece in range(pieces)
    ]
    for arrival in arrivals:
        arrival.start()
    for piece, arrival in enumerate(arrivals):
        arrival.wait()
        at = piece * step
        queries_ref[:, at : at + step] = jnp.swapaxes(came[piece, :, 0], 0, 1)
        kv_ref[:, at : at + step] = jnp.swapaxes(came[piece, :, 1], 0, 1)
        kv_ref[:, rows + at : rows + at + step] = jnp.swapaxes(came[piece, :, 2], 0, 1)


def arrange(audio_qkv):
    rows, parts, heads, size = audio_qkv.shape
    dtype = audio_qkv.dtype
    pieces = 4
    return pl.pallas_call(
        functools.partial(arrange_kernel, rows, pieces),
        in_specs=[pl.BlockSpec(memory_space=pltpu.HBM)],
        out_specs=(pl.BlockSpec(memory_space=pltpu.VMEM),) * 2,
        out_shape=(
            jax.ShapeDtypeStruct((heads, rows, size), dtype),
            jax.ShapeDtypeStruct((heads, 2 * rows, size), dtype),
        ),
        scratch_shapes=[
            pltpu.VMEM((pieces, rows // pieces, parts, heads, size), dtype),
            pltpu.SemaphoreType.DMA((pieces,)),
        ],
        compiler_params=params(),
        name="arrange",
    )(pltpu.with_memory_space_constraint(audio_qkv, pltpu.HBM))


def join_kernel(pieces, queries_ref, kv_ref, send_ref, sems):
    heads, rows, unused = queries_ref.shape
    step = heads // pieces
    departures = []
    for piece in range(pieces):
        at = pl.ds(piece * step, step)
        for half, ref in enumerate((queries_ref, kv_ref)):
            departures.append(
                pltpu.make_async_copy(
                    ref.at[at],
                    send_ref.at[at, pl.ds(half * rows, ref.shape[1])],
                    sems.at[2 * piece + half],
                )
            )
    for departure in departures:
        departure.start()
    for departure in departures:
        departure.wait()


def join(queries, kv):
    heads, rows, size = queries.shape
    pieces = 2
    return pl.pallas_call(
        functools.partial(join_kernel, pieces),
        in_specs=[pl.BlockSpec(memory_space=pltpu.VMEM)] * 2,
        out_specs=pl.BlockSpec(memory_space=pltpu.HBM),
        out_shape=pltpu.HBM((heads, rows + kv.shape[1], size), queries.dtype),
        scratch_shapes=[pltpu.SemaphoreType.DMA((2 * pieces,))],
        compiler_params=params(),
        name="join",
    )(queries, kv)


def attend_kernel(query_rows, rows, scale, fused, *refs):
    if fused:
        recv_ref, out_ref, held, sems = refs
        query_ref, base = recv_ref, query_rows
    else:
        query_ref, recv_ref, out_ref, held, sems = refs
        base = 0
    sources = recv_ref.shape[0]
    size = recv_ref.shape[2]
    group = max(1, 256 // query_rows)
    key_group = min(sources, 16)
    factor = scale * LOG2E
    departures = []
    for first in range(0, sources, group):
        queries = query_ref[first : first + group, :query_rows].reshape(group * query_rows, size)

        def advance(step, state):
            top, total, summed = state
            at = pl.ds(step * key_group, key_group)
            keys = recv_ref[at, base : base + rows].reshape(key_group * rows, size)
            values = recv_ref[at, base + rows : base + 2 * rows].reshape(key_group * rows, size)
            scores = lax.dot_general(
                queries, keys, (((1,), (1,)), ((), ())), preferred_element_type=jnp.float32
            )
            new_top = jnp.max(scores, axis=1, keepdims=True)
            if state[0] is not None:
                new_top = jnp.maximum(top, new_top)
            weights = jnp.exp2((scores - new_top) * factor)
            new_total = jnp.sum(weights, axis=1, keepdims=True)
            new_summed = jnp.dot(
                weights.astype(jnp.bfloat16), values, preferred_element_type=jnp.float32
            )
            if state[0] is not None:
                rescale = jnp.exp2((top - new_top) * factor)
                new_total = total * rescale + new_total
                new_summed = summed * rescale + new_summed
            return new_top, new_total, new_summed

        state = advance(0, (None, None, None))
        if sources > key_group:
            state = lax.fori_loop(1, sources // key_group, advance, state)
        result = (state[2] / state[1]).astype(jnp.bfloat16)
        held[first : first + group] = result.reshape(group, query_rows, size)
        departure = pltpu.make_async_copy(
            held.at[pl.ds(first, group)], out_ref.at[pl.ds(first, group)], sems.at[first // group]
        )
        departure.start()
        departures.append(departure)
    for departure in departures:
        departure.wait()


def attend(operands, sources, query_rows, rows, size, scale):
    work = sources * query_rows * sources * rows
    return pl.pallas_call(
        functools.partial(attend_kernel, query_rows, rows, scale, len(operands) == 1),
        in_specs=[pl.BlockSpec(memory_space=pltpu.VMEM)] * len(operands),
        out_specs=pl.BlockSpec(memory_space=pltpu.HBM),
        out_shape=pltpu.HBM((sources, query_rows, size), jnp.bfloat16),
        scratch_shapes=[
            pltpu.VMEM((sources, query_rows, size), jnp.bfloat16),
            pltpu.SemaphoreType.DMA((sources * query_rows // 256,)),
        ],
        compiler_params=params(),
        cost_estimate=pl.CostEstimate(
            flops=4 * work * size, bytes_accessed=8 * sources * rows * size, transcendentals=work
        ),
        name="attend",
    )(*operands)


def collect_kernel(by_head_ref, out_ref):
    out_ref[...] = jnp.swapaxes(by_head_ref[...], 0, 1)


def collect(by_head):
    heads, rows, size = by_head.shape
    return pl.pallas_call(
        collect_kernel,
        out_shape=jax.ShapeDtypeStruct((rows, heads, size), by_head.dtype),
        compiler_params=params(),
        name="collect",
    )(by_head)


def video_kernel(
    rows, slots, scale, group, pairs_ref, counts_ref, where_ref,
    video_ref, own_ref, core_ref, chip_ref, out_ref,
    near_keys, near_values, keys_ref, values_ref, queries_ref, result_ref,
):
    block = pl.program_id(0)
    heads, unused, size = own_ref.shape

    @pl.when(block == 0)
    def _():
        for ref, place in ((own_ref, rows), (core_ref, where_ref[1]), (chip_ref, where_ref[2])):
            at = pl.ds(pl.multiple_of(place, rows), rows)
            near_keys[:, at] = ref[:, :rows]
            near_values[:, at] = ref[:, rows:]
        values_ref[:, :, size:] = jnp.ones((heads, slots * ABLK, size), jnp.bfloat16)

    queries_ref[...] = jnp.swapaxes(video_ref[...], 0, 1)
    for slot in range(slots):
        start = pl.multiple_of((pairs_ref[block, slot] - where_ref[0]) * ABLK, ABLK)
        here = slice(slot * ABLK, (slot + 1) * ABLK)
        keys_ref[:, here] = near_keys[:, pl.ds(start, ABLK)]
        values_ref[:, here, :size] = near_values[:, pl.ds(start, ABLK)]
    column = lax.broadcasted_iota(jnp.int32, (VBLK, slots * ABLK), 1)
    live = column < counts_ref[block] * ABLK
    factor = scale * LOG2E
    for first in range(0, heads, group):
        members = range(first, first + group)
        scores = [
            lax.dot_general(
                queries_ref[head], keys_ref[head], (((1,), (1,)), ((), ())),
                preferred_element_type=jnp.float32,
            )
            for head in members
        ]
        scores = jnp.stack([jnp.where(live, one, LOWEST) for one in scores])
        top = jnp.max(scores, axis=2, keepdims=True)
        weights = jnp.exp2((scores - top) * factor).astype(jnp.bfloat16)
        summed = [
            jnp.dot(weights[head - first], values_ref[head], preferred_element_type=jnp.float32)
            for head in members
        ]
        for head in members:
            both = summed[head - first]
            result_ref[head] = (both[:, :size] / both[:, size:]).astype(jnp.bfloat16)
    out_ref[...] = jnp.swapaxes(result_ref[...], 0, 1)


def video(video_q, own, core, chip, pairs, counts, where, scale):
    total, heads, size = video_q.shape
    rows = own.shape[1] // 2
    slots = pairs.shape[1]
    blocks = total // VBLK
    block_spec = pl.BlockSpec((VBLK, heads, size), lambda i, *unused: (i, 0, 0))
    work = total * heads * slots * ABLK
    return pl.pallas_call(
        functools.partial(video_kernel, rows, slots, scale, 4),
        grid_spec=pltpu.PrefetchScalarGridSpec(
            num_scalar_prefetch=3,
            grid=(blocks,),
            in_specs=[
                block_spec,
                whole(own.shape),
                whole(core.shape),
                pl.BlockSpec((None,) + own.shape, lambda i, p, c, where: (where[3], 0, 0, 0)),
            ],
            out_specs=block_spec,
            scratch_shapes=[
                pltpu.VMEM((heads, 3 * rows, size), jnp.bfloat16),
                pltpu.VMEM((heads, 3 * rows, size), jnp.bfloat16),
                pltpu.VMEM((heads, slots * ABLK, size), jnp.bfloat16),
                pltpu.VMEM((heads, slots * ABLK, 2 * size), jnp.bfloat16),
                pltpu.VMEM((heads, VBLK, size), jnp.bfloat16),
                pltpu.VMEM((heads, VBLK, size), jnp.bfloat16),
            ],
        ),
        out_shape=jax.ShapeDtypeStruct(video_q.shape, jnp.bfloat16),
        compiler_params=params(),
        cost_estimate=pl.CostEstimate(
            flops=4 * work * size, bytes_accessed=4 * total * heads * size, transcendentals=work
        ),
        name="video",
    )(pairs, counts, where, video_q, own, core, chip)


def local(audio_qkv, video_q, pairs, counts):
    devices = lax.axis_size("seq")
    rows, unused, heads, size = audio_qkv.shape
    bands = devices // heads
    band_rows = rows // bands
    scale = size ** (-0.5)
    queries, kv = arrange(audio_qkv)
    core_pairs = [(i, i ^ 1) for i in range(devices)]
    clips = lax.axis_size("groups")
    chip_pairs = [
        [clip * devices + i, clip * devices + i + 1]
        for clip in range(clips)
        for i in range(1, devices - 1, 2)
    ] + [
        [clip * devices + i, (clip + 1) * devices + i]
        for clip in range(0, clips, 2)
        for i in (0, devices - 1)
    ]

    chip = lax.all_gather(kv, ("groups", "seq"), axis_index_groups=chip_pairs)

    def exchange(value):
        return lax.all_to_all(value, "seq", split_axis=0, concat_axis=0, tiled=True)

    if bands == 1:
        operands = (exchange(join(queries, kv)),)
    else:
        queries = exchange(queries.reshape(devices, band_rows, size))
        spread = jnp.broadcast_to(kv[:, None], (heads, bands, 2 * rows, size))
        operands = (queries, exchange(spread.reshape(devices, 2 * rows, size)))
    core = lax.ppermute(kv, "seq", core_pairs)
    me = lax.axis_index("seq")
    odd = me & 1
    where = jnp.stack([(me - 1) * (rows // ABLK), 2 * (1 - odd) * rows, 2 * odd * rows, odd])
    video_cross = video(
        video_q, kv, core, chip, pairs, counts, where.astype(jnp.int32), scale
    )
    operands, video_cross = lax.optimization_barrier((operands, video_cross))
    head_out = attend(operands, devices, band_rows, rows, size, scale)
    audio_attn = collect(exchange(head_out).reshape(heads, rows, size))
    return audio_attn, video_cross


def solution(mesh):
    in_specs = (
        P(("groups", "seq"), None, None, None),
        P(("groups", "seq"), None, None),
        P(("groups", "seq"), None),
        P(("groups", "seq")),
    )
    out_specs = (P(("groups", "seq"), None, None), P(("groups", "seq"), None, None))
    return jax.shard_map(local, mesh=mesh, in_specs=in_specs, out_specs=out_specs, check_vma=False)
```

```python
import functools

import jax
import jax.numpy as jnp
from jax import lax
from jax.experimental import pallas as pl
from jax.experimental.pallas import tpu as pltpu
from jax.sharding import PartitionSpec as P

ABLK = 32
VBLK = 128
LOG2E = 1.4426950408889634
LOWEST = -1e30
VMEM_LIMIT = 48 * 1024 * 1024


def params():
    return pltpu.CompilerParams(vmem_limit_bytes=VMEM_LIMIT)


def whole(shape):
    return pl.BlockSpec(shape, lambda *unused: (0,) * len(shape))


def arrange_kernel(rows, pieces, qkv_ref, queries_ref, kv_ref, came, sems):
    step = rows // pieces
    arrivals = [
        pltpu.make_async_copy(
            qkv_ref.at[pl.ds(piece * step, step)], came.at[piece], sems.at[piece]
        )
        for piece in range(pieces)
    ]
    for arrival in arrivals:
        arrival.start()
    for piece, arrival in enumerate(arrivals):
        arrival.wait()
        at = piece * step
        queries_ref[:, at : at + step] = jnp.swapaxes(came[piece, :, 0], 0, 1)
        kv_ref[:, at : at + step] = jnp.swapaxes(came[piece, :, 1], 0, 1)
        kv_ref[:, rows + at : rows + at + step] = jnp.swapaxes(came[piece, :, 2], 0, 1)


def arrange(audio_qkv):
    rows, parts, heads, size = audio_qkv.shape
    dtype = audio_qkv.dtype
    pieces = 4
    return pl.pallas_call(
        functools.partial(arrange_kernel, rows, pieces),
        in_specs=[pl.BlockSpec(memory_space=pltpu.HBM)],
        out_specs=(pl.BlockSpec(memory_space=pltpu.VMEM),) * 2,
        out_shape=(
            jax.ShapeDtypeStruct((heads, rows, size), dtype),
            jax.ShapeDtypeStruct((heads, 2 * rows, size), dtype),
        ),
        scratch_shapes=[
            pltpu.VMEM((pieces, rows // pieces, parts, heads, size), dtype),
            pltpu.SemaphoreType.DMA((pieces,)),
        ],
        compiler_params=params(),
        name="arrange",
    )(pltpu.with_memory_space_constraint(audio_qkv, pltpu.HBM))


def join_kernel(pieces, queries_ref, kv_ref, send_ref, sems):
    heads, rows, unused = queries_ref.shape
    step = heads // pieces
    departures = []
    for piece in range(pieces):
        at = pl.ds(piece * step, step)
        for half, ref in enumerate((queries_ref, kv_ref)):
            departures.append(
                pltpu.make_async_copy(
                    ref.at[at],
                    send_ref.at[at, pl.ds(half * rows, ref.shape[1])],
                    sems.at[2 * piece + half],
                )
            )
    for departure in departures:
        departure.start()
    for departure in departures:
        departure.wait()


def join(queries, kv):
    heads, rows, size = queries.shape
    pieces = 2
    return pl.pallas_call(
        functools.partial(join_kernel, pieces),
        in_specs=[pl.BlockSpec(memory_space=pltpu.VMEM)] * 2,
        out_specs=pl.BlockSpec(memory_space=pltpu.HBM),
        out_shape=pltpu.HBM((heads, rows + kv.shape[1], size), queries.dtype),
        scratch_shapes=[pltpu.SemaphoreType.DMA((2 * pieces,))],
        compiler_params=params(),
        cost_estimate=pl.CostEstimate(flops=0, bytes_accessed=64 * 1024 * 1024, transcendentals=0),
        name="join",
    )(queries, kv)


def attend_kernel(query_rows, rows, scale, fused, *refs):
    if fused:
        recv_ref, out_ref, held, sems = refs
        query_ref, base = recv_ref, query_rows
    else:
        query_ref, recv_ref, out_ref, held, sems = refs
        base = 0
    sources = recv_ref.shape[0]
    size = recv_ref.shape[2]
    group = max(1, 256 // query_rows)
    key_group = min(sources, 16)
    factor = scale * LOG2E
    departures = []
    for first in range(0, sources, group):
        queries = query_ref[first : first + group, :query_rows].reshape(group * query_rows, size)

        def advance(step, state):
            top, total, summed = state
            at = pl.ds(step * key_group, key_group)
            keys = recv_ref[at, base : base + rows].reshape(key_group * rows, size)
            values = recv_ref[at, base + rows : base + 2 * rows].reshape(key_group * rows, size)
            scores = lax.dot_general(
                queries, keys, (((1,), (1,)), ((), ())), preferred_element_type=jnp.float32
            )
            new_top = jnp.max(scores, axis=1, keepdims=True)
            if state[0] is not None:
                new_top = jnp.maximum(top, new_top)
            weights = jnp.exp2((scores - new_top) * factor)
            new_total = jnp.sum(weights, axis=1, keepdims=True)
            new_summed = jnp.dot(
                weights.astype(jnp.bfloat16), values, preferred_element_type=jnp.float32
            )
            if state[0] is not None:
                rescale = jnp.exp2((top - new_top) * factor)
                new_total = total * rescale + new_total
                new_summed = summed * rescale + new_summed
            return new_top, new_total, new_summed

        state = advance(0, (None, None, None))
        if sources > key_group:
            state = lax.fori_loop(1, sources // key_group, advance, state)
        result = (state[2] / state[1]).astype(jnp.bfloat16)
        held[first : first + group] = result.reshape(group, query_rows, size)
        departure = pltpu.make_async_copy(
            held.at[pl.ds(first, group)], out_ref.at[pl.ds(first, group)], sems.at[first // group]
        )
        departure.start()
        departures.append(departure)
    for departure in departures:
        departure.wait()


def attend(operands, sources, query_rows, rows, size, scale):
    work = sources * query_rows * sources * rows
    return pl.pallas_call(
        functools.partial(attend_kernel, query_rows, rows, scale, len(operands) == 1),
        in_specs=[pl.BlockSpec(memory_space=pltpu.VMEM)] * len(operands),
        out_specs=pl.BlockSpec(memory_space=pltpu.HBM),
        out_shape=pltpu.HBM((sources, query_rows, size), jnp.bfloat16),
        scratch_shapes=[
            pltpu.VMEM((sources, query_rows, size), jnp.bfloat16),
            pltpu.SemaphoreType.DMA((sources * query_rows // 256,)),
        ],
        compiler_params=params(),
        cost_estimate=pl.CostEstimate(
            flops=4 * work * size, bytes_accessed=8 * sources * rows * size, transcendentals=work
        ),
        name="attend",
    )(*operands)


def collect_kernel(by_head_ref, out_ref):
    out_ref[...] = jnp.swapaxes(by_head_ref[...], 0, 1)


def collect(by_head):
    heads, rows, size = by_head.shape
    return pl.pallas_call(
        collect_kernel,
        out_shape=jax.ShapeDtypeStruct((rows, heads, size), by_head.dtype),
        compiler_params=params(),
        name="collect",
    )(by_head)


def video_kernel(
    rows, slots, scale, group, pairs_ref, counts_ref, where_ref,
    video_ref, own_ref, core_ref, chip_ref, out_ref,
    near_keys, near_values, keys_ref, values_ref, queries_ref, result_ref,
):
    block = pl.program_id(0)
    heads, unused, size = own_ref.shape

    @pl.when(block == 0)
    def _():
        for ref, place in ((own_ref, rows), (core_ref, where_ref[1]), (chip_ref, where_ref[2])):
            at = pl.ds(pl.multiple_of(place, rows), rows)
            near_keys[:, at] = ref[:, :rows]
            near_values[:, at] = ref[:, rows:]
        values_ref[:, :, size:] = jnp.ones((heads, slots * ABLK, size), jnp.bfloat16)

    queries_ref[...] = jnp.swapaxes(video_ref[...], 0, 1)
    for slot in range(slots):
        start = pl.multiple_of((pairs_ref[block, slot] - where_ref[0]) * ABLK, ABLK)
        here = slice(slot * ABLK, (slot + 1) * ABLK)
        keys_ref[:, here] = near_keys[:, pl.ds(start, ABLK)]
        values_ref[:, here, :size] = near_values[:, pl.ds(start, ABLK)]
    column = lax.broadcasted_iota(jnp.int32, (VBLK, slots * ABLK), 1)
    live = column < counts_ref[block] * ABLK
    factor = scale * LOG2E
    for first in range(0, heads, group):
        members = range(first, first + group)
        scores = [
            lax.dot_general(
                queries_ref[head], keys_ref[head], (((1,), (1,)), ((), ())),
                preferred_element_type=jnp.float32,
            )
            for head in members
        ]
        scores = jnp.stack([jnp.where(live, one, LOWEST) for one in scores])
        top = jnp.max(scores, axis=2, keepdims=True)
        weights = jnp.exp2((scores - top) * factor).astype(jnp.bfloat16)
        summed = [
            jnp.dot(weights[head - first], values_ref[head], preferred_element_type=jnp.float32)
            for head in members
        ]
        for head in members:
            both = summed[head - first]
            result_ref[head] = (both[:, :size] / both[:, size:]).astype(jnp.bfloat16)
    out_ref[...] = jnp.swapaxes(result_ref[...], 0, 1)


def video(video_q, own, core, chip, pairs, counts, where, scale):
    total, heads, size = video_q.shape
    rows = own.shape[1] // 2
    slots = pairs.shape[1]
    blocks = total // VBLK
    block_spec = pl.BlockSpec((VBLK, heads, size), lambda i, *unused: (i, 0, 0))
    work = total * heads * slots * ABLK
    return pl.pallas_call(
        functools.partial(video_kernel, rows, slots, scale, 4),
        grid_spec=pltpu.PrefetchScalarGridSpec(
            num_scalar_prefetch=3,
            grid=(blocks,),
            in_specs=[block_spec] + [whole(own.shape)] * 3,
            out_specs=block_spec,
            scratch_shapes=[
                pltpu.VMEM((heads, 3 * rows, size), jnp.bfloat16),
                pltpu.VMEM((heads, 3 * rows, size), jnp.bfloat16),
                pltpu.VMEM((heads, slots * ABLK, size), jnp.bfloat16),
                pltpu.VMEM((heads, slots * ABLK, 2 * size), jnp.bfloat16),
                pltpu.VMEM((heads, VBLK, size), jnp.bfloat16),
                pltpu.VMEM((heads, VBLK, size), jnp.bfloat16),
            ],
        ),
        out_shape=jax.ShapeDtypeStruct(video_q.shape, jnp.bfloat16),
        compiler_params=params(),
        cost_estimate=pl.CostEstimate(
            flops=4 * work * size, bytes_accessed=160 * total * heads * size, transcendentals=work
        ),
        name="video",
    )(pairs, counts, where, video_q, own, core, chip)


def local(audio_qkv, video_q, pairs, counts):
    devices = lax.axis_size("seq")
    rows, unused, heads, size = audio_qkv.shape
    bands = devices // heads
    band_rows = rows // bands
    scale = size ** (-0.5)
    queries, kv = arrange(audio_qkv)
    core_pairs = [(i, i ^ 1) for i in range(devices)]
    chip_pairs = [(i, ((i + 1) ^ 1) - 1) for i in range(1, devices - 1)]

    chip = lax.ppermute(kv, "seq", chip_pairs)

    def exchange(value):
        return lax.all_to_all(value, "seq", split_axis=0, concat_axis=0, tiled=True)

    if bands == 1:
        operands = (exchange(join(queries, kv)),)
    else:
        queries = exchange(queries.reshape(devices, band_rows, size))
        spread = jnp.broadcast_to(kv[:, None], (heads, bands, 2 * rows, size))
        operands = (queries, exchange(spread.reshape(devices, 2 * rows, size)))
    core = lax.ppermute(kv, "seq", core_pairs)
    me = lax.axis_index("seq")
    odd = me & 1
    where = jnp.stack([(me - 1) * (rows // ABLK), 2 * (1 - odd) * rows, 2 * odd * rows])
    video_cross = video(
        video_q, kv, core, chip, pairs, counts, where.astype(jnp.int32), scale
    )
    operands, video_cross = lax.optimization_barrier((operands, video_cross))
    head_out = attend(operands, devices, band_rows, rows, size, scale)
    audio_attn = collect(exchange(head_out).reshape(heads, rows, size))
    return audio_attn, video_cross


def solution(mesh):
    in_specs = (
        P(("groups", "seq"), None, None, None),
        P(("groups", "seq"), None, None),
        P(("groups", "seq"), None),
        P(("groups", "seq")),
    )
    out_specs = (P(("groups", "seq"), None, None), P(("groups", "seq"), None, None))
    return jax.shard_map(local, mesh=mesh, in_specs=in_specs, out_specs=out_specs, check_vma=False)
```

```python
import functools

import jax
import jax.numpy as jnp
from jax import lax
from jax.experimental import pallas as pl
from jax.experimental.pallas import tpu as pltpu
from jax.sharding import PartitionSpec as P

ABLK = 32
VBLK = 128
LOG2E = 1.4426950408889634
LOWEST = -1e30
VMEM_LIMIT = 48 * 1024 * 1024


def params():
    return pltpu.CompilerParams(vmem_limit_bytes=VMEM_LIMIT)


def whole(shape):
    return pl.BlockSpec(shape, lambda *unused: (0,) * len(shape))


def arrange_kernel(rows, pieces, qkv_ref, queries_ref, kv_ref, came, sems):
    step = rows // pieces
    arrivals = [
        pltpu.make_async_copy(
            qkv_ref.at[pl.ds(piece * step, step)], came.at[piece], sems.at[piece]
        )
        for piece in range(pieces)
    ]
    for arrival in arrivals:
        arrival.start()
    for piece, arrival in enumerate(arrivals):
        arrival.wait()
        at = piece * step
        queries_ref[:, at : at + step] = jnp.swapaxes(came[piece, :, 0], 0, 1)
        kv_ref[:, at : at + step] = jnp.swapaxes(came[piece, :, 1], 0, 1)
        kv_ref[:, rows + at : rows + at + step] = jnp.swapaxes(came[piece, :, 2], 0, 1)


def arrange(audio_qkv):
    rows, parts, heads, size = audio_qkv.shape
    dtype = audio_qkv.dtype
    pieces = 4
    return pl.pallas_call(
        functools.partial(arrange_kernel, rows, pieces),
        in_specs=[pl.BlockSpec(memory_space=pltpu.HBM)],
        out_specs=(pl.BlockSpec(memory_space=pltpu.VMEM),) * 2,
        out_shape=(
            jax.ShapeDtypeStruct((heads, rows, size), dtype),
            jax.ShapeDtypeStruct((heads, 2 * rows, size), dtype),
        ),
        scratch_shapes=[
            pltpu.VMEM((pieces, rows // pieces, parts, heads, size), dtype),
            pltpu.SemaphoreType.DMA((pieces,)),
        ],
        compiler_params=params(),
        name="arrange",
    )(pltpu.with_memory_space_constraint(audio_qkv, pltpu.HBM))


def join_kernel(pieces, queries_ref, kv_ref, send_ref, sems):
    heads, rows, unused = queries_ref.shape
    step = heads // pieces
    departures = []
    for piece in range(pieces):
        at = pl.ds(piece * step, step)
        for half, ref in enumerate((queries_ref, kv_ref)):
            departures.append(
                pltpu.make_async_copy(
                    ref.at[at],
                    send_ref.at[at, pl.ds(half * rows, ref.shape[1])],
                    sems.at[2 * piece + half],
                )
            )
    for departure in departures:
        departure.start()
    for departure in departures:
        departure.wait()


def join(queries, kv):
    heads, rows, size = queries.shape
    pieces = 2
    return pl.pallas_call(
        functools.partial(join_kernel, pieces),
        in_specs=[pl.BlockSpec(memory_space=pltpu.VMEM)] * 2,
        out_specs=pl.BlockSpec(memory_space=pltpu.HBM),
        out_shape=pltpu.HBM((heads, rows + kv.shape[1], size), queries.dtype),
        scratch_shapes=[pltpu.SemaphoreType.DMA((2 * pieces,))],
        compiler_params=params(),
        name="join",
    )(queries, kv)


def attend_kernel(query_rows, rows, scale, fused, *refs):
    if fused:
        recv_ref, out_ref, held, sems = refs
        query_ref, base = recv_ref, query_rows
    else:
        query_ref, recv_ref, out_ref, held, sems = refs
        base = 0
    sources = recv_ref.shape[0]
    size = recv_ref.shape[2]
    group = max(1, 256 // query_rows)
    key_group = min(sources, 16)
    factor = scale * LOG2E
    departures = []
    for first in range(0, sources, group):
        queries = query_ref[first : first + group, :query_rows].reshape(group * query_rows, size)

        def advance(step, state):
            top, total, summed = state
            at = pl.ds(step * key_group, key_group)
            keys = recv_ref[at, base : base + rows].reshape(key_group * rows, size)
            values = recv_ref[at, base + rows : base + 2 * rows].reshape(key_group * rows, size)
            scores = lax.dot_general(
                queries, keys, (((1,), (1,)), ((), ())), preferred_element_type=jnp.float32
            )
            new_top = jnp.max(scores, axis=1, keepdims=True)
            if state[0] is not None:
                new_top = jnp.maximum(top, new_top)
            weights = jnp.exp2((scores - new_top) * factor)
            new_total = jnp.sum(weights, axis=1, keepdims=True)
            new_summed = jnp.dot(
                weights.astype(jnp.bfloat16), values, preferred_element_type=jnp.float32
            )
            if state[0] is not None:
                rescale = jnp.exp2((top - new_top) * factor)
                new_total = total * rescale + new_total
                new_summed = summed * rescale + new_summed
            return new_top, new_total, new_summed

        state = advance(0, (None, None, None))
        if sources > key_group:
            state = lax.fori_loop(1, sources // key_group, advance, state)
        result = (state[2] / state[1]).astype(jnp.bfloat16)
        held[first : first + group] = result.reshape(group, query_rows, size)
        departure = pltpu.make_async_copy(
            held.at[pl.ds(first, group)], out_ref.at[pl.ds(first, group)], sems.at[first // group]
        )
        departure.start()
        departures.append(departure)
    for departure in departures:
        departure.wait()


def attend(operands, sources, query_rows, rows, size, scale):
    work = sources * query_rows * sources * rows
    return pl.pallas_call(
        functools.partial(attend_kernel, query_rows, rows, scale, len(operands) == 1),
        in_specs=[pl.BlockSpec(memory_space=pltpu.VMEM)] * len(operands),
        out_specs=pl.BlockSpec(memory_space=pltpu.HBM),
        out_shape=pltpu.HBM((sources, query_rows, size), jnp.bfloat16),
        scratch_shapes=[
            pltpu.VMEM((sources, query_rows, size), jnp.bfloat16),
            pltpu.SemaphoreType.DMA((sources * query_rows // 256,)),
        ],
        compiler_params=params(),
        cost_estimate=pl.CostEstimate(
            flops=4 * work * size, bytes_accessed=8 * sources * rows * size, transcendentals=work
        ),
        name="attend",
    )(*operands)


def collect_kernel(by_head_ref, out_ref):
    out_ref[...] = jnp.swapaxes(by_head_ref[...], 0, 1)


def collect(by_head):
    heads, rows, size = by_head.shape
    return pl.pallas_call(
        collect_kernel,
        out_shape=jax.ShapeDtypeStruct((rows, heads, size), by_head.dtype),
        compiler_params=params(),
        name="collect",
    )(by_head)


def video_kernel(
    rows, slots, scale, group, pairs_ref, counts_ref, where_ref,
    video_ref, own_ref, core_ref, chip_ref, out_ref,
    near_keys, near_values, keys_ref, values_ref, queries_ref, result_ref,
):
    block = pl.program_id(0)
    heads, unused, size = own_ref.shape

    @pl.when(block == 0)
    def _():
        for ref, place in ((own_ref, rows), (core_ref, where_ref[1]), (chip_ref, where_ref[2])):
            at = pl.ds(pl.multiple_of(place, rows), rows)
            near_keys[:, at] = ref[:, :rows]
            near_values[:, at] = ref[:, rows:]
        values_ref[:, :, size:] = jnp.ones((heads, slots * ABLK, size), jnp.bfloat16)

    queries_ref[...] = jnp.swapaxes(video_ref[...], 0, 1)
    for slot in range(slots):
        start = pl.multiple_of((pairs_ref[block, slot] - where_ref[0]) * ABLK, ABLK)
        here = slice(slot * ABLK, (slot + 1) * ABLK)
        keys_ref[:, here] = near_keys[:, pl.ds(start, ABLK)]
        values_ref[:, here, :size] = near_values[:, pl.ds(start, ABLK)]
    column = lax.broadcasted_iota(jnp.int32, (VBLK, slots * ABLK), 1)
    live = column < counts_ref[block] * ABLK
    factor = scale * LOG2E
    for first in range(0, heads, group):
        members = range(first, first + group)
        scores = [
            lax.dot_general(
                queries_ref[head], keys_ref[head], (((1,), (1,)), ((), ())),
                preferred_element_type=jnp.float32,
            )
            for head in members
        ]
        scores = jnp.stack([jnp.where(live, one, LOWEST) for one in scores])
        top = jnp.max(scores, axis=2, keepdims=True)
        weights = jnp.exp2((scores - top) * factor).astype(jnp.bfloat16)
        summed = [
            jnp.dot(weights[head - first], values_ref[head], preferred_element_type=jnp.float32)
            for head in members
        ]
        for head in members:
            both = summed[head - first]
            result_ref[head] = (both[:, :size] / both[:, size:]).astype(jnp.bfloat16)
    out_ref[...] = jnp.swapaxes(result_ref[...], 0, 1)


def video(video_q, own, core, chip, pairs, counts, where, scale):
    total, heads, size = video_q.shape
    rows = own.shape[1] // 2
    slots = pairs.shape[1]
    blocks = total // VBLK
    block_spec = pl.BlockSpec((VBLK, heads, size), lambda i, *unused: (i, 0, 0))
    work = total * heads * slots * ABLK
    return pl.pallas_call(
        functools.partial(video_kernel, rows, slots, scale, 4),
        grid_spec=pltpu.PrefetchScalarGridSpec(
            num_scalar_prefetch=3,
            grid=(blocks,),
            in_specs=[block_spec] + [whole(own.shape)] * 3,
            out_specs=block_spec,
            scratch_shapes=[
                pltpu.VMEM((heads, 3 * rows, size), jnp.bfloat16),
                pltpu.VMEM((heads, 3 * rows, size), jnp.bfloat16),
                pltpu.VMEM((heads, slots * ABLK, size), jnp.bfloat16),
                pltpu.VMEM((heads, slots * ABLK, 2 * size), jnp.bfloat16),
                pltpu.VMEM((heads, VBLK, size), jnp.bfloat16),
                pltpu.VMEM((heads, VBLK, size), jnp.bfloat16),
            ],
        ),
        out_shape=jax.ShapeDtypeStruct(video_q.shape, jnp.bfloat16),
        compiler_params=params(),
        cost_estimate=pl.CostEstimate(
            flops=4 * work * size, bytes_accessed=32 * total * heads * size, transcendentals=work
        ),
        name="video",
    )(pairs, counts, where, video_q, own, core, chip)


def local(audio_qkv, video_q, pairs, counts):
    devices = lax.axis_size("seq")
    rows, unused, heads, size = audio_qkv.shape
    bands = devices // heads
    band_rows = rows // bands
    scale = size ** (-0.5)
    queries, kv = arrange(audio_qkv)
    core_pairs = [(i, i ^ 1) for i in range(devices)]
    chip_pairs = [(i, ((i + 1) ^ 1) - 1) for i in range(1, devices - 1)]

    chip = lax.ppermute(kv, "seq", chip_pairs)

    def exchange(value):
        return lax.all_to_all(value, "seq", split_axis=0, concat_axis=0, tiled=True)

    if bands == 1:
        operands = (exchange(join(queries, kv)),)
    else:
        queries = exchange(queries.reshape(devices, band_rows, size))
        spread = jnp.broadcast_to(kv[:, None], (heads, bands, 2 * rows, size))
        operands = (queries, exchange(spread.reshape(devices, 2 * rows, size)))
    core = lax.ppermute(kv, "seq", core_pairs)
    me = lax.axis_index("seq")
    odd = me & 1
    where = jnp.stack([(me - 1) * (rows // ABLK), 2 * (1 - odd) * rows, 2 * odd * rows])
    video_cross = video(
        video_q, kv, core, chip, pairs, counts, where.astype(jnp.int32), scale
    )
    head_out = attend(operands, devices, band_rows, rows, size, scale)
    returned, video_cross = lax.optimization_barrier((exchange(head_out), video_cross))
    audio_attn = collect(returned.reshape(heads, rows, size))
    return audio_attn, video_cross


def solution(mesh):
    in_specs = (
        P(("groups", "seq"), None, None, None),
        P(("groups", "seq"), None, None),
        P(("groups", "seq"), None),
        P(("groups", "seq")),
    )
    out_specs = (P(("groups", "seq"), None, None), P(("groups", "seq"), None, None))
    return jax.shard_map(local, mesh=mesh, in_specs=in_specs, out_specs=out_specs, check_vma=False)
```

```python
import functools

import jax
import jax.numpy as jnp
from jax import lax
from jax.experimental import pallas as pl
from jax.experimental.pallas import tpu as pltpu
from jax.sharding import PartitionSpec as P

ABLK = 32
VBLK = 128
LOG2E = 1.4426950408889634
LOWEST = -1e30
VMEM_LIMIT = 48 * 1024 * 1024


def params():
    return pltpu.CompilerParams(vmem_limit_bytes=VMEM_LIMIT)


def whole(shape):
    return pl.BlockSpec(shape, lambda *unused: (0,) * len(shape))


PIECE = 16


def arrange_kernel(pieces, qkv_ref, send_ref, kv_ref, came, turned, in_sems, out_sems):
    rows = pieces * PIECE
    arrivals = [
        pltpu.make_async_copy(
            qkv_ref.at[pl.ds(piece * PIECE, PIECE)], came.at[piece], in_sems.at[piece]
        )
        for piece in range(pieces)
    ]
    for arrival in arrivals:
        arrival.start()
    departures = []
    for piece, arrival in enumerate(arrivals):
        arrival.wait()
        for part in range(3):
            by_head = jnp.swapaxes(came[piece, :, part], 0, 1)
            turned[piece, :, part * PIECE : (part + 1) * PIECE] = by_head
            if part:
                at = (part - 1) * rows + piece * PIECE
                kv_ref[:, at : at + PIECE] = by_head
        departure = pltpu.make_async_copy(
            turned.at[piece], send_ref.at[:, piece], out_sems.at[piece]
        )
        departure.start()
        departures.append(departure)
    for departure in departures:
        departure.wait()


def arrange(audio_qkv):
    rows, parts, heads, size = audio_qkv.shape
    dtype = audio_qkv.dtype
    pieces = rows // PIECE
    return pl.pallas_call(
        functools.partial(arrange_kernel, pieces),
        in_specs=[pl.BlockSpec(memory_space=pltpu.HBM)],
        out_specs=(
            pl.BlockSpec(memory_space=pltpu.HBM),
            pl.BlockSpec(memory_space=pltpu.VMEM),
        ),
        out_shape=(
            pltpu.HBM((heads, pieces, parts * PIECE, size), dtype),
            jax.ShapeDtypeStruct((heads, 2 * rows, size), dtype),
        ),
        scratch_shapes=[
            pltpu.VMEM((pieces, PIECE, parts, heads, size), dtype),
            pltpu.VMEM((pieces, heads, parts * PIECE, size), dtype),
            pltpu.SemaphoreType.DMA((pieces,)),
            pltpu.SemaphoreType.DMA((pieces,)),
        ],
        compiler_params=params(),
        name="arrange",
    )(pltpu.with_memory_space_constraint(audio_qkv, pltpu.HBM))


def scores_of(queries, keys):
    return lax.dot_general(
        queries, keys, (((1,), (1,)), ((), ())), preferred_element_type=jnp.float32
    )


def attend_kernel(scale, recv_ref, out_ref, held, sems):
    sources, pieces, unused, size = recv_ref.shape
    total = sources * pieces * PIECE
    chunk = total // sems.shape[0]
    group = chunk // (pieces * PIECE)
    factor = scale * LOG2E
    keys = recv_ref[:, :, PIECE : 2 * PIECE].reshape(total, size)
    values = recv_ref[:, :, 2 * PIECE :].reshape(total, size)
    chunks = total // chunk
    scores, weights, sums, departures = {}, {}, {}, []
    for step in range(chunks + 2):
        if step < chunks:
            first = step * group
            queries = recv_ref[first : first + group, :, :PIECE].reshape(chunk, size)
            scores[step] = scores_of(queries, keys)
        if 0 <= step - 1 < chunks:
            now = scores.pop(step - 1)
            top = jnp.max(now, axis=1, keepdims=True)
            exact = jnp.exp2((now - top) * factor)
            sums[step - 1] = jnp.sum(exact, axis=1, keepdims=True)
            weights[step - 1] = exact.astype(jnp.bfloat16)
        if step >= 2:
            summed = jnp.dot(
                weights.pop(step - 2), values, preferred_element_type=jnp.float32
            )
            result = (summed / sums.pop(step - 2)).astype(jnp.bfloat16)
            at = (step - 2) * group
            held[at : at + group] = result.reshape(group, pieces * PIECE, size)
            departure = pltpu.make_async_copy(
                held.at[pl.ds(at, group)], out_ref.at[pl.ds(at, group)], sems.at[step - 2]
            )
            departure.start()
            departures.append(departure)
    for departure in departures:
        departure.wait()


def attend(recv, scale):
    sources, pieces, unused, size = recv.shape
    rows = pieces * PIECE
    total = sources * rows
    return pl.pallas_call(
        functools.partial(attend_kernel, scale),
        in_specs=[pl.BlockSpec(memory_space=pltpu.VMEM)],
        out_specs=pl.BlockSpec(memory_space=pltpu.HBM),
        out_shape=pltpu.HBM((sources, rows, size), jnp.bfloat16),
        scratch_shapes=[
            pltpu.VMEM((sources, rows, size), jnp.bfloat16),
            pltpu.SemaphoreType.DMA((total // 128,)),
        ],
        compiler_params=params(),
        cost_estimate=pl.CostEstimate(
            flops=4 * total * total * size, bytes_accessed=8 * total * size,
            transcendentals=total * total,
        ),
        name="attend",
    )(recv)


def attend_band_kernel(query_rows, scale, query_ref, recv_ref, out_ref):
    sources, both, size = recv_ref.shape
    rows = both // 2
    group = 256 // query_rows
    factor = scale * LOG2E
    for first in range(0, sources, group):
        queries = query_ref[first : first + group].reshape(group * query_rows, size)

        def advance(step, state):
            top, total, summed = state
            at = pl.ds(step * PIECE, PIECE)
            keys = recv_ref[at, :rows].reshape(PIECE * rows, size)
            values = recv_ref[at, rows:].reshape(PIECE * rows, size)
            scores = scores_of(queries, keys)
            new_top = jnp.maximum(top, jnp.max(scores, axis=1, keepdims=True))
            weights = jnp.exp2((scores - new_top) * factor)
            rescale = jnp.exp2((top - new_top) * factor)
            new_total = total * rescale + jnp.sum(weights, axis=1, keepdims=True)
            new_summed = summed * rescale + jnp.dot(
                weights.astype(jnp.bfloat16), values, preferred_element_type=jnp.float32
            )
            return new_top, new_total, new_summed

        start = (
            jnp.full((group * query_rows, 1), LOWEST, jnp.float32),
            jnp.zeros((group * query_rows, 1), jnp.float32),
            jnp.zeros((group * query_rows, size), jnp.float32),
        )
        state = lax.fori_loop(0, sources // PIECE, advance, start)
        result = (state[2] / state[1]).astype(jnp.bfloat16)
        out_ref[first : first + group] = result.reshape(group, query_rows, size)


def attend_band(queries, recv, scale):
    return pl.pallas_call(
        functools.partial(attend_band_kernel, queries.shape[1], scale),
        out_shape=jax.ShapeDtypeStruct(queries.shape, jnp.bfloat16),
        compiler_params=params(),
        name="attend_band",
    )(queries, recv)


def collect_kernel(by_head_ref, out_ref, turned, sems):
    departures = []
    for piece in range(by_head_ref.shape[1] // PIECE):
        at = pl.ds(piece * PIECE, PIECE)
        turned[at] = jnp.swapaxes(by_head_ref[:, at], 0, 1)
        departure = pltpu.make_async_copy(turned.at[at], out_ref.at[at], sems.at[piece])
        departure.start()
        departures.append(departure)
    for departure in departures:
        departure.wait()


def collect(by_head):
    heads, rows, size = by_head.shape
    return pl.pallas_call(
        collect_kernel,
        in_specs=[pl.BlockSpec(memory_space=pltpu.VMEM)],
        out_specs=pl.BlockSpec(memory_space=pltpu.HBM),
        out_shape=pltpu.HBM((rows, heads, size), by_head.dtype),
        scratch_shapes=[
            pltpu.VMEM((rows, heads, size), by_head.dtype),
            pltpu.SemaphoreType.DMA((rows // PIECE,)),
        ],
        compiler_params=params(),
        name="collect",
    )(by_head)


def video_kernel(
    rows, slots, scale, group, pairs_ref, counts_ref, where_ref,
    video_ref, own_ref, core_ref, chip_ref, out_ref,
    near_keys, near_values, keys_ref, values_ref, queries_ref, result_ref,
):
    block = pl.program_id(0)
    heads, unused, size = own_ref.shape

    @pl.when(block == 0)
    def _():
        for ref, place in ((own_ref, rows), (core_ref, where_ref[1]), (chip_ref, where_ref[2])):
            at = pl.ds(pl.multiple_of(place, rows), rows)
            near_keys[:, at] = ref[:, :rows]
            near_values[:, at] = ref[:, rows:]
        values_ref[:, :, size:] = jnp.ones((heads, slots * ABLK, size), jnp.bfloat16)

    queries_ref[...] = jnp.swapaxes(video_ref[...], 0, 1)
    for slot in range(slots):
        start = pl.multiple_of((pairs_ref[block, slot] - where_ref[0]) * ABLK, ABLK)
        here = slice(slot * ABLK, (slot + 1) * ABLK)
        keys_ref[:, here] = near_keys[:, pl.ds(start, ABLK)]
        values_ref[:, here, :size] = near_values[:, pl.ds(start, ABLK)]
    column = lax.broadcasted_iota(jnp.int32, (VBLK, slots * ABLK), 1)
    live = column < counts_ref[block] * ABLK
    factor = scale * LOG2E
    for first in range(0, heads, group):
        members = range(first, first + group)
        scores = [
            lax.dot_general(
                queries_ref[head], keys_ref[head], (((1,), (1,)), ((), ())),
                preferred_element_type=jnp.float32,
            )
            for head in members
        ]
        scores = jnp.stack([jnp.where(live, one, LOWEST) for one in scores])
        top = jnp.max(scores, axis=2, keepdims=True)
        weights = jnp.exp2((scores - top) * factor).astype(jnp.bfloat16)
        summed = [
            jnp.dot(weights[head - first], values_ref[head], preferred_element_type=jnp.float32)
            for head in members
        ]
        for head in members:
            both = summed[head - first]
            result_ref[head] = (both[:, :size] / both[:, size:]).astype(jnp.bfloat16)
    out_ref[...] = jnp.swapaxes(result_ref[...], 0, 1)


def video(video_q, own, core, chip, pairs, counts, where, scale):
    total, heads, size = video_q.shape
    rows = own.shape[1] // 2
    slots = pairs.shape[1]
    blocks = total // VBLK
    block_spec = pl.BlockSpec((VBLK, heads, size), lambda i, *unused: (i, 0, 0))
    work = total * heads * slots * ABLK
    return pl.pallas_call(
        functools.partial(video_kernel, rows, slots, scale, 4),
        grid_spec=pltpu.PrefetchScalarGridSpec(
            num_scalar_prefetch=3,
            grid=(blocks,),
            in_specs=[block_spec] + [whole(own.shape)] * 3,
            out_specs=block_spec,
            scratch_shapes=[
                pltpu.VMEM((heads, 3 * rows, size), jnp.bfloat16),
                pltpu.VMEM((heads, 3 * rows, size), jnp.bfloat16),
                pltpu.VMEM((heads, slots * ABLK, size), jnp.bfloat16),
                pltpu.VMEM((heads, slots * ABLK, 2 * size), jnp.bfloat16),
                pltpu.VMEM((heads, VBLK, size), jnp.bfloat16),
                pltpu.VMEM((heads, VBLK, size), jnp.bfloat16),
            ],
        ),
        out_shape=jax.ShapeDtypeStruct(video_q.shape, jnp.bfloat16),
        compiler_params=params(),
        cost_estimate=pl.CostEstimate(
            flops=4 * work * size, bytes_accessed=32 * total * heads * size, transcendentals=work
        ),
        name="video",
    )(pairs, counts, where, video_q, own, core, chip)


def local(audio_qkv, video_q, pairs, counts):
    devices = lax.axis_size("seq")
    rows, unused, heads, size = audio_qkv.shape
    bands = devices // heads
    band_rows = rows // bands
    scale = size ** (-0.5)
    send, kv = arrange(audio_qkv)
    core_pairs = [(i, i ^ 1) for i in range(devices)]
    chip_pairs = [(i, ((i + 1) ^ 1) - 1) for i in range(1, devices - 1)]

    chip = lax.ppermute(kv, "seq", chip_pairs)

    def exchange(value):
        return lax.all_to_all(value, "seq", split_axis=0, concat_axis=0, tiled=True)

    core = lax.ppermute(kv, "seq", core_pairs)
    me = lax.axis_index("seq")
    odd = me & 1
    where = jnp.stack([(me - 1) * (rows // ABLK), 2 * (1 - odd) * rows, 2 * odd * rows])
    video_cross = video(
        video_q, kv, core, chip, pairs, counts, where.astype(jnp.int32), scale
    )
    if bands == 1:
        head_out = attend(exchange(send), scale)
    else:
        queries = exchange(send[:, :, :PIECE].reshape(devices, band_rows, size))
        spread = jnp.broadcast_to(kv[:, None], (heads, bands, 2 * rows, size))
        recv = exchange(spread.reshape(devices, 2 * rows, size))
        head_out = attend_band(queries, recv, scale)
    returned, video_cross = lax.optimization_barrier((exchange(head_out), video_cross))
    audio_attn = collect(returned.reshape(heads, rows, size))
    return audio_attn, video_cross


def solution(mesh):
    in_specs = (
        P(("groups", "seq"), None, None, None),
        P(("groups", "seq"), None, None),
        P(("groups", "seq"), None),
        P(("groups", "seq")),
    )
    out_specs = (P(("groups", "seq"), None, None), P(("groups", "seq"), None, None))
    return jax.shard_map(local, mesh=mesh, in_specs=in_specs, out_specs=out_specs, check_vma=False)
```

```python
import functools

import jax
import jax.numpy as jnp
from jax import lax
from jax.experimental import pallas as pl
from jax.experimental.pallas import tpu as pltpu
from jax.sharding import PartitionSpec as P

ABLK = 32
VBLK = 128
LOG2E = 1.4426950408889634
LOWEST = -1e30
VMEM_LIMIT = 48 * 1024 * 1024


def params():
    return pltpu.CompilerParams(vmem_limit_bytes=VMEM_LIMIT)


def whole(shape):
    return pl.BlockSpec(shape, lambda *unused: (0,) * len(shape))


PIECE = 16


def arrange_kernel(pieces, qkv_ref, send_ref, kv_ref, came, turned, in_sems, out_sems):
    rows = pieces * PIECE
    arrivals = [
        pltpu.make_async_copy(
            qkv_ref.at[pl.ds(piece * PIECE, PIECE)], came.at[piece], in_sems.at[piece]
        )
        for piece in range(pieces)
    ]
    for arrival in arrivals:
        arrival.start()
    departures = []
    for piece, arrival in enumerate(arrivals):
        arrival.wait()
        for part in range(3):
            by_head = jnp.swapaxes(came[piece, :, part], 0, 1)
            turned[piece, :, part * PIECE : (part + 1) * PIECE] = by_head
            if part:
                at = (part - 1) * rows + piece * PIECE
                kv_ref[:, at : at + PIECE] = by_head
        departure = pltpu.make_async_copy(
            turned.at[piece], send_ref.at[:, piece], out_sems.at[piece]
        )
        departure.start()
        departures.append(departure)
    for departure in departures:
        departure.wait()


def arrange(audio_qkv):
    rows, parts, heads, size = audio_qkv.shape
    dtype = audio_qkv.dtype
    pieces = rows // PIECE
    return pl.pallas_call(
        functools.partial(arrange_kernel, pieces),
        in_specs=[pl.BlockSpec(memory_space=pltpu.HBM)],
        out_specs=(
            pl.BlockSpec(memory_space=pltpu.HBM),
            pl.BlockSpec(memory_space=pltpu.VMEM),
        ),
        out_shape=(
            pltpu.HBM((heads, pieces, parts * PIECE, size), dtype),
            jax.ShapeDtypeStruct((heads, 2 * rows, size), dtype),
        ),
        scratch_shapes=[
            pltpu.VMEM((pieces, PIECE, parts, heads, size), dtype),
            pltpu.VMEM((pieces, heads, parts * PIECE, size), dtype),
            pltpu.SemaphoreType.DMA((pieces,)),
            pltpu.SemaphoreType.DMA((pieces,)),
        ],
        compiler_params=params(),
        name="arrange",
    )(pltpu.with_memory_space_constraint(audio_qkv, pltpu.HBM))


def scores_of(queries, keys):
    return lax.dot_general(
        queries, keys, (((1,), (1,)), ((), ())), preferred_element_type=jnp.float32
    )


def attend_kernel(scale, recv_ref, out_ref, held, sems):
    sources, pieces, unused, size = recv_ref.shape
    total = sources * pieces * PIECE
    chunk = total // sems.shape[0]
    group = chunk // (pieces * PIECE)
    factor = scale * LOG2E
    keys = recv_ref[:, :, PIECE : 2 * PIECE].reshape(total, size)
    values = recv_ref[:, :, 2 * PIECE :].reshape(total, size)
    chunks = total // chunk
    scores, weights, sums, departures = {}, {}, {}, []
    for step in range(chunks + 2):
        if step < chunks:
            first = step * group
            queries = recv_ref[first : first + group, :, :PIECE].reshape(chunk, size)
            scores[step] = scores_of(queries, keys)
        if 0 <= step - 1 < chunks:
            now = scores.pop(step - 1)
            top = jnp.max(now, axis=1, keepdims=True)
            exact = jnp.exp2((now - top) * factor)
            sums[step - 1] = jnp.sum(exact, axis=1, keepdims=True)
            weights[step - 1] = exact.astype(jnp.bfloat16)
        if step >= 2:
            summed = jnp.dot(
                weights.pop(step - 2), values, preferred_element_type=jnp.float32
            )
            result = (summed / sums.pop(step - 2)).astype(jnp.bfloat16)
            at = (step - 2) * group
            held[at : at + group] = result.reshape(group, pieces * PIECE, size)
            departure = pltpu.make_async_copy(
                held.at[pl.ds(at, group)], out_ref.at[pl.ds(at, group)], sems.at[step - 2]
            )
            departure.start()
            departures.append(departure)
    for departure in departures:
        departure.wait()


def attend(recv, scale):
    sources, pieces, unused, size = recv.shape
    rows = pieces * PIECE
    total = sources * rows
    return pl.pallas_call(
        functools.partial(attend_kernel, scale),
        in_specs=[pl.BlockSpec(memory_space=pltpu.VMEM)],
        out_specs=pl.BlockSpec(memory_space=pltpu.HBM),
        out_shape=pltpu.HBM((sources, rows, size), jnp.bfloat16),
        scratch_shapes=[
            pltpu.VMEM((sources, rows, size), jnp.bfloat16),
            pltpu.SemaphoreType.DMA((total // 128,)),
        ],
        compiler_params=params(),
        cost_estimate=pl.CostEstimate(
            flops=4 * total * total * size, bytes_accessed=8 * total * size,
            transcendentals=total * total,
        ),
        name="attend",
    )(recv)


def attend_band_kernel(query_rows, scale, query_ref, recv_ref, out_ref):
    sources, both, size = recv_ref.shape
    rows = both // 2
    group = 256 // query_rows
    factor = scale * LOG2E
    for first in range(0, sources, group):
        queries = query_ref[first : first + group].reshape(group * query_rows, size)

        def advance(step, state):
            top, total, summed = state
            at = pl.ds(step * PIECE, PIECE)
            keys = recv_ref[at, :rows].reshape(PIECE * rows, size)
            values = recv_ref[at, rows:].reshape(PIECE * rows, size)
            scores = scores_of(queries, keys)
            new_top = jnp.maximum(top, jnp.max(scores, axis=1, keepdims=True))
            weights = jnp.exp2((scores - new_top) * factor)
            rescale = jnp.exp2((top - new_top) * factor)
            new_total = total * rescale + jnp.sum(weights, axis=1, keepdims=True)
            new_summed = summed * rescale + jnp.dot(
                weights.astype(jnp.bfloat16), values, preferred_element_type=jnp.float32
            )
            return new_top, new_total, new_summed

        start = (
            jnp.full((group * query_rows, 1), LOWEST, jnp.float32),
            jnp.zeros((group * query_rows, 1), jnp.float32),
            jnp.zeros((group * query_rows, size), jnp.float32),
        )
        state = lax.fori_loop(0, sources // PIECE, advance, start)
        result = (state[2] / state[1]).astype(jnp.bfloat16)
        out_ref[first : first + group] = result.reshape(group, query_rows, size)


def attend_band(queries, recv, scale):
    return pl.pallas_call(
        functools.partial(attend_band_kernel, queries.shape[1], scale),
        out_shape=jax.ShapeDtypeStruct(queries.shape, jnp.bfloat16),
        compiler_params=params(),
        name="attend_band",
    )(queries, recv)


def collect_kernel(by_head_ref, out_ref, turned, sems):
    departures = []
    for piece in range(by_head_ref.shape[1] // PIECE):
        at = pl.ds(piece * PIECE, PIECE)
        turned[at] = jnp.swapaxes(by_head_ref[:, at], 0, 1)
        departure = pltpu.make_async_copy(turned.at[at], out_ref.at[at], sems.at[piece])
        departure.start()
        departures.append(departure)
    for departure in departures:
        departure.wait()


def collect(by_head):
    heads, rows, size = by_head.shape
    return pl.pallas_call(
        collect_kernel,
        in_specs=[pl.BlockSpec(memory_space=pltpu.VMEM)],
        out_specs=pl.BlockSpec(memory_space=pltpu.HBM),
        out_shape=pltpu.HBM((rows, heads, size), by_head.dtype),
        scratch_shapes=[
            pltpu.VMEM((rows, heads, size), by_head.dtype),
            pltpu.SemaphoreType.DMA((rows // PIECE,)),
        ],
        compiler_params=params(),
        name="collect",
    )(by_head)


def video_kernel(
    rows, slots, scale, group, pairs_ref, counts_ref, where_ref,
    video_ref, own_ref, core_ref, chip_ref, out_ref,
    near_keys, near_values, keys_ref, values_ref, queries_ref, result_ref,
):
    block = pl.program_id(0)
    heads, unused, size = own_ref.shape

    @pl.when(block == 0)
    def _():
        for ref, place in ((own_ref, rows), (core_ref, where_ref[1]), (chip_ref, where_ref[2])):
            at = pl.ds(pl.multiple_of(place, rows), rows)
            near_keys[:, at] = ref[:, :rows]
            near_values[:, at] = ref[:, rows:]
        values_ref[:, :, size:] = jnp.ones((heads, slots * ABLK, size), jnp.bfloat16)

    queries_ref[...] = jnp.swapaxes(video_ref[...], 0, 1)
    for slot in range(slots):
        start = pl.multiple_of((pairs_ref[block, slot] - where_ref[0]) * ABLK, ABLK)
        here = slice(slot * ABLK, (slot + 1) * ABLK)
        keys_ref[:, here] = near_keys[:, pl.ds(start, ABLK)]
        values_ref[:, here, :size] = near_values[:, pl.ds(start, ABLK)]
    column = lax.broadcasted_iota(jnp.int32, (VBLK, slots * ABLK), 1)
    live = column < counts_ref[block] * ABLK
    factor = scale * LOG2E
    for first in range(0, heads, group):
        members = range(first, first + group)
        scores = [
            lax.dot_general(
                queries_ref[head], keys_ref[head], (((1,), (1,)), ((), ())),
                preferred_element_type=jnp.float32,
            )
            for head in members
        ]
        scores = jnp.stack([jnp.where(live, one, LOWEST) for one in scores])
        top = jnp.max(scores, axis=2, keepdims=True)
        weights = jnp.exp2((scores - top) * factor).astype(jnp.bfloat16)
        summed = [
            jnp.dot(weights[head - first], values_ref[head], preferred_element_type=jnp.float32)
            for head in members
        ]
        for head in members:
            both = summed[head - first]
            result_ref[head] = (both[:, :size] / both[:, size:]).astype(jnp.bfloat16)
    out_ref[...] = jnp.swapaxes(result_ref[...], 0, 1)


def video(video_q, own, core, chip, pairs, counts, where, scale):
    total, heads, size = video_q.shape
    rows = own.shape[1] // 2
    slots = pairs.shape[1]
    blocks = total // VBLK
    block_spec = pl.BlockSpec((VBLK, heads, size), lambda i, *unused: (i, 0, 0))
    work = total * heads * slots * ABLK
    return pl.pallas_call(
        functools.partial(video_kernel, rows, slots, scale, 4),
        grid_spec=pltpu.PrefetchScalarGridSpec(
            num_scalar_prefetch=3,
            grid=(blocks,),
            in_specs=[block_spec] + [whole(own.shape)] * 3,
            out_specs=block_spec,
            scratch_shapes=[
                pltpu.VMEM((heads, 3 * rows, size), jnp.bfloat16),
                pltpu.VMEM((heads, 3 * rows, size), jnp.bfloat16),
                pltpu.VMEM((heads, slots * ABLK, size), jnp.bfloat16),
                pltpu.VMEM((heads, slots * ABLK, 2 * size), jnp.bfloat16),
                pltpu.VMEM((heads, VBLK, size), jnp.bfloat16),
                pltpu.VMEM((heads, VBLK, size), jnp.bfloat16),
            ],
        ),
        out_shape=jax.ShapeDtypeStruct(video_q.shape, jnp.bfloat16),
        compiler_params=params(),
        cost_estimate=pl.CostEstimate(
            flops=4 * work * size, bytes_accessed=32 * total * heads * size, transcendentals=work
        ),
        name="video",
    )(pairs, counts, where, video_q, own, core, chip)


def local(audio_qkv, video_q, pairs, counts):
    devices = lax.axis_size("seq")
    rows, unused, heads, size = audio_qkv.shape
    bands = devices // heads
    band_rows = rows // bands
    scale = size ** (-0.5)
    send, kv = arrange(audio_qkv)
    core_pairs = [(i, i ^ 1) for i in range(devices)]
    chip_pairs = [(i, ((i + 1) ^ 1) - 1) for i in range(1, devices - 1)]

    chip = lax.ppermute(kv, "seq", chip_pairs)

    planes = 4
    spread_out = [(p % planes) * (devices // planes) + p // planes for p in range(devices)]

    def exchange(value):
        return lax.all_to_all(
            value, "seq", split_axis=0, concat_axis=0, tiled=True, axis_index_groups=[spread_out]
        )

    core = lax.ppermute(kv, "seq", core_pairs)
    me = lax.axis_index("seq")
    odd = me & 1
    where = jnp.stack([(me - 1) * (rows // ABLK), 2 * (1 - odd) * rows, 2 * odd * rows])
    video_cross = video(
        video_q, kv, core, chip, pairs, counts, where.astype(jnp.int32), scale
    )
    if bands == 1:
        head_out = attend(exchange(send), scale)
    else:
        queries = exchange(send[:, :, :PIECE].reshape(devices, band_rows, size))
        spread = jnp.broadcast_to(kv[:, None], (heads, bands, 2 * rows, size))
        recv = exchange(spread.reshape(devices, 2 * rows, size))
        head_out = attend_band(queries, recv, scale)
    returned, video_cross = lax.optimization_barrier((exchange(head_out), video_cross))
    audio_attn = collect(returned.reshape(heads, rows, size))
    return audio_attn, video_cross


def solution(mesh):
    in_specs = (
        P(("groups", "seq"), None, None, None),
        P(("groups", "seq"), None, None),
        P(("groups", "seq"), None),
        P(("groups", "seq")),
    )
    out_specs = (P(("groups", "seq"), None, None), P(("groups", "seq"), None, None))
    return jax.shard_map(local, mesh=mesh, in_specs=in_specs, out_specs=out_specs, check_vma=False)
```

```python
import functools

import jax
import jax.numpy as jnp
from jax import lax
from jax.experimental import pallas as pl
from jax.experimental.pallas import tpu as pltpu
from jax.sharding import PartitionSpec as P

ABLK = 32
VBLK = 128
LOG2E = 1.4426950408889634
LOWEST = -1e30
VMEM_LIMIT = 48 * 1024 * 1024


def params():
    return pltpu.CompilerParams(vmem_limit_bytes=VMEM_LIMIT)


def whole(shape):
    return pl.BlockSpec(shape, lambda *unused: (0,) * len(shape))


PIECE = 16


def arrange_kernel(pieces, qkv_ref, send_ref, kv_ref, came, turned, in_sems, out_sems):
    rows = pieces * PIECE
    arrivals = [
        pltpu.make_async_copy(
            qkv_ref.at[pl.ds(piece * PIECE, PIECE)], came.at[piece], in_sems.at[piece]
        )
        for piece in range(pieces)
    ]
    for arrival in arrivals:
        arrival.start()
    departures = []
    for piece, arrival in enumerate(arrivals):
        arrival.wait()
        for part in range(3):
            by_head = jnp.swapaxes(came[piece, :, part], 0, 1)
            turned[piece, :, part * PIECE : (part + 1) * PIECE] = by_head
            if part:
                at = (part - 1) * rows + piece * PIECE
                kv_ref[:, at : at + PIECE] = by_head
        departure = pltpu.make_async_copy(
            turned.at[piece], send_ref.at[:, piece], out_sems.at[piece]
        )
        departure.start()
        departures.append(departure)
    for departure in departures:
        departure.wait()


def arrange(audio_qkv):
    rows, parts, heads, size = audio_qkv.shape
    dtype = audio_qkv.dtype
    pieces = rows // PIECE
    return pl.pallas_call(
        functools.partial(arrange_kernel, pieces),
        in_specs=[pl.BlockSpec(memory_space=pltpu.HBM)],
        out_specs=(
            pl.BlockSpec(memory_space=pltpu.HBM),
            pl.BlockSpec(memory_space=pltpu.VMEM),
        ),
        out_shape=(
            pltpu.HBM((heads, pieces, parts * PIECE, size), dtype),
            jax.ShapeDtypeStruct((heads, 2 * rows, size), dtype),
        ),
        scratch_shapes=[
            pltpu.VMEM((pieces, PIECE, parts, heads, size), dtype),
            pltpu.VMEM((pieces, heads, parts * PIECE, size), dtype),
            pltpu.SemaphoreType.DMA((pieces,)),
            pltpu.SemaphoreType.DMA((pieces,)),
        ],
        compiler_params=params(),
        name="arrange",
    )(pltpu.with_memory_space_constraint(audio_qkv, pltpu.HBM))


def scores_of(queries, keys):
    return lax.dot_general(
        queries, keys, (((1,), (1,)), ((), ())), preferred_element_type=jnp.float32
    )


def attend_kernel(scale, recv_ref, out_ref, held, sems):
    sources, pieces, unused, size = recv_ref.shape
    total = sources * pieces * PIECE
    chunk = total // sems.shape[0]
    group = chunk // (pieces * PIECE)
    factor = scale * LOG2E
    keys = recv_ref[:, :, PIECE : 2 * PIECE].reshape(total, size)
    values = recv_ref[:, :, 2 * PIECE :].reshape(total, size)
    chunks = total // chunk
    scores, weights, sums, departures = {}, {}, {}, []
    for step in range(chunks + 2):
        if step < chunks:
            first = step * group
            queries = recv_ref[first : first + group, :, :PIECE].reshape(chunk, size)
            scores[step] = scores_of(queries, keys)
        if 0 <= step - 1 < chunks:
            now = scores.pop(step - 1)
            top = jnp.max(now, axis=1, keepdims=True)
            exact = jnp.exp2((now - top) * factor)
            sums[step - 1] = jnp.sum(exact, axis=1, keepdims=True)
            weights[step - 1] = exact.astype(jnp.bfloat16)
        if step >= 2:
            summed = jnp.dot(
                weights.pop(step - 2), values, preferred_element_type=jnp.float32
            )
            result = (summed / sums.pop(step - 2)).astype(jnp.bfloat16)
            at = (step - 2) * group
            held[at : at + group] = result.reshape(group, pieces * PIECE, size)
            departure = pltpu.make_async_copy(
                held.at[pl.ds(at, group)], out_ref.at[pl.ds(at, group)], sems.at[step - 2]
            )
            departure.start()
            departures.append(departure)
    for departure in departures:
        departure.wait()


def attend(recv, scale):
    sources, pieces, unused, size = recv.shape
    rows = pieces * PIECE
    total = sources * rows
    return pl.pallas_call(
        functools.partial(attend_kernel, scale),
        in_specs=[pl.BlockSpec(memory_space=pltpu.VMEM)],
        out_specs=pl.BlockSpec(memory_space=pltpu.HBM),
        out_shape=pltpu.HBM((sources, rows, size), jnp.bfloat16),
        scratch_shapes=[
            pltpu.VMEM((sources, rows, size), jnp.bfloat16),
            pltpu.SemaphoreType.DMA((total // 128,)),
        ],
        compiler_params=params(),
        cost_estimate=pl.CostEstimate(
            flops=4 * total * total * size, bytes_accessed=8 * total * size,
            transcendentals=total * total,
        ),
        name="attend",
    )(recv)


def attend_band_kernel(query_rows, scale, query_ref, recv_ref, out_ref):
    sources, both, size = recv_ref.shape
    rows = both // 2
    group = 256 // query_rows
    factor = scale * LOG2E
    for first in range(0, sources, group):
        queries = query_ref[first : first + group].reshape(group * query_rows, size)

        def advance(step, state):
            top, total, summed = state
            at = pl.ds(step * PIECE, PIECE)
            keys = recv_ref[at, :rows].reshape(PIECE * rows, size)
            values = recv_ref[at, rows:].reshape(PIECE * rows, size)
            scores = scores_of(queries, keys)
            new_top = jnp.maximum(top, jnp.max(scores, axis=1, keepdims=True))
            weights = jnp.exp2((scores - new_top) * factor)
            rescale = jnp.exp2((top - new_top) * factor)
            new_total = total * rescale + jnp.sum(weights, axis=1, keepdims=True)
            new_summed = summed * rescale + jnp.dot(
                weights.astype(jnp.bfloat16), values, preferred_element_type=jnp.float32
            )
            return new_top, new_total, new_summed

        start = (
            jnp.full((group * query_rows, 1), LOWEST, jnp.float32),
            jnp.zeros((group * query_rows, 1), jnp.float32),
            jnp.zeros((group * query_rows, size), jnp.float32),
        )
        state = lax.fori_loop(0, sources // PIECE, advance, start)
        result = (state[2] / state[1]).astype(jnp.bfloat16)
        out_ref[first : first + group] = result.reshape(group, query_rows, size)


def attend_band(queries, recv, scale):
    return pl.pallas_call(
        functools.partial(attend_band_kernel, queries.shape[1], scale),
        out_shape=jax.ShapeDtypeStruct(queries.shape, jnp.bfloat16),
        compiler_params=params(),
        name="attend_band",
    )(queries, recv)


def collect_kernel(by_head_ref, out_ref, turned, sems):
    departures = []
    for piece in range(by_head_ref.shape[1] // PIECE):
        at = pl.ds(piece * PIECE, PIECE)
        turned[at] = jnp.swapaxes(by_head_ref[:, at], 0, 1)
        departure = pltpu.make_async_copy(turned.at[at], out_ref.at[at], sems.at[piece])
        departure.start()
        departures.append(departure)
    for departure in departures:
        departure.wait()


def collect(by_head):
    heads, rows, size = by_head.shape
    return pl.pallas_call(
        collect_kernel,
        in_specs=[pl.BlockSpec(memory_space=pltpu.VMEM)],
        out_specs=pl.BlockSpec(memory_space=pltpu.HBM),
        out_shape=pltpu.HBM((rows, heads, size), by_head.dtype),
        scratch_shapes=[
            pltpu.VMEM((rows, heads, size), by_head.dtype),
            pltpu.SemaphoreType.DMA((rows // PIECE,)),
        ],
        compiler_params=params(),
        name="collect",
    )(by_head)


def video_kernel(
    rows, slots, scale, group, pairs_ref, counts_ref, where_ref,
    video_ref, own_ref, core_ref, chip_ref, out_ref,
    near_keys, near_values, keys_ref, values_ref, queries_ref, result_ref,
):
    block = pl.program_id(0)
    heads, unused, size = own_ref.shape

    @pl.when(block == 0)
    def _():
        for ref, place in ((own_ref, rows), (core_ref, where_ref[1]), (chip_ref, where_ref[2])):
            at = pl.ds(pl.multiple_of(place, rows), rows)
            near_keys[:, at] = ref[:, :rows]
            near_values[:, at] = ref[:, rows:]
        values_ref[:, :, size:] = jnp.ones((heads, slots * ABLK, size), jnp.bfloat16)

    queries_ref[...] = jnp.swapaxes(video_ref[...], 0, 1)
    for slot in range(slots):
        start = pl.multiple_of((pairs_ref[block, slot] - where_ref[0]) * ABLK, ABLK)
        here = slice(slot * ABLK, (slot + 1) * ABLK)
        keys_ref[:, here] = near_keys[:, pl.ds(start, ABLK)]
        values_ref[:, here, :size] = near_values[:, pl.ds(start, ABLK)]
    column = lax.broadcasted_iota(jnp.int32, (VBLK, slots * ABLK), 1)
    live = column < counts_ref[block] * ABLK
    factor = scale * LOG2E
    for first in range(0, heads, group):
        members = range(first, first + group)
        scores = [
            lax.dot_general(
                queries_ref[head], keys_ref[head], (((1,), (1,)), ((), ())),
                preferred_element_type=jnp.float32,
            )
            for head in members
        ]
        scores = jnp.stack([jnp.where(live, one, LOWEST) for one in scores])
        top = jnp.max(scores, axis=2, keepdims=True)
        weights = jnp.exp2((scores - top) * factor).astype(jnp.bfloat16)
        summed = [
            jnp.dot(weights[head - first], values_ref[head], preferred_element_type=jnp.float32)
            for head in members
        ]
        for head in members:
            both = summed[head - first]
            result_ref[head] = (both[:, :size] / both[:, size:]).astype(jnp.bfloat16)
    out_ref[...] = jnp.swapaxes(result_ref[...], 0, 1)


def video(video_q, own, core, chip, pairs, counts, where, scale):
    total, heads, size = video_q.shape
    rows = own.shape[1] // 2
    slots = pairs.shape[1]
    blocks = total // VBLK
    block_spec = pl.BlockSpec((VBLK, heads, size), lambda i, *unused: (i, 0, 0))
    work = total * heads * slots * ABLK
    return pl.pallas_call(
        functools.partial(video_kernel, rows, slots, scale, 4),
        grid_spec=pltpu.PrefetchScalarGridSpec(
            num_scalar_prefetch=3,
            grid=(blocks,),
            in_specs=[block_spec] + [whole(own.shape)] * 3,
            out_specs=block_spec,
            scratch_shapes=[
                pltpu.VMEM((heads, 3 * rows, size), jnp.bfloat16),
                pltpu.VMEM((heads, 3 * rows, size), jnp.bfloat16),
                pltpu.VMEM((heads, slots * ABLK, size), jnp.bfloat16),
                pltpu.VMEM((heads, slots * ABLK, 2 * size), jnp.bfloat16),
                pltpu.VMEM((heads, VBLK, size), jnp.bfloat16),
                pltpu.VMEM((heads, VBLK, size), jnp.bfloat16),
            ],
        ),
        out_shape=jax.ShapeDtypeStruct(video_q.shape, jnp.bfloat16),
        compiler_params=params(),
        cost_estimate=pl.CostEstimate(
            flops=4 * work * size, bytes_accessed=32 * total * heads * size, transcendentals=work
        ),
        name="video",
    )(pairs, counts, where, video_q, own, core, chip)


def local(audio_qkv, video_q, pairs, counts):
    devices = lax.axis_size("seq")
    rows, unused, heads, size = audio_qkv.shape
    bands = devices // heads
    band_rows = rows // bands
    scale = size ** (-0.5)
    send, kv = arrange(audio_qkv)
    core_pairs = [(i, i ^ 1) for i in range(devices)]
    chip_pairs = [(i, ((i + 1) ^ 1) - 1) for i in range(1, devices - 1)]

    chip = lax.ppermute(kv, "seq", chip_pairs)

    order = list(range(devices))[::-1]

    def exchange(value):
        return lax.all_to_all(
            value, "seq", split_axis=0, concat_axis=0, tiled=True, axis_index_groups=[order]
        )

    core = lax.ppermute(kv, "seq", core_pairs)
    me = lax.axis_index("seq")
    odd = me & 1
    where = jnp.stack([(me - 1) * (rows // ABLK), 2 * (1 - odd) * rows, 2 * odd * rows])
    video_cross = video(
        video_q, kv, core, chip, pairs, counts, where.astype(jnp.int32), scale
    )
    if bands == 1:
        head_out = attend(exchange(send), scale)
    else:
        queries = exchange(send[:, :, :PIECE].reshape(devices, band_rows, size))
        spread = jnp.broadcast_to(kv[:, None], (heads, bands, 2 * rows, size))
        recv = exchange(spread.reshape(devices, 2 * rows, size))
        head_out = attend_band(queries, recv, scale)
    returned, video_cross = lax.optimization_barrier((exchange(head_out), video_cross))
    audio_attn = collect(returned.reshape(heads, rows, size))
    return audio_attn, video_cross


def solution(mesh):
    in_specs = (
        P(("groups", "seq"), None, None, None),
        P(("groups", "seq"), None, None),
        P(("groups", "seq"), None),
        P(("groups", "seq")),
    )
    out_specs = (P(("groups", "seq"), None, None), P(("groups", "seq"), None, None))
    return jax.shard_map(local, mesh=mesh, in_specs=in_specs, out_specs=out_specs, check_vma=False)
```

```python
import functools

import jax
import jax.numpy as jnp
from jax import lax
from jax.experimental import pallas as pl
from jax.experimental.pallas import tpu as pltpu
from jax.sharding import PartitionSpec as P

ABLK = 32
VBLK = 128
LOG2E = 1.4426950408889634
LOWEST = -1e30
VMEM_LIMIT = 48 * 1024 * 1024


def params():
    return pltpu.CompilerParams(vmem_limit_bytes=VMEM_LIMIT)


def whole(shape):
    return pl.BlockSpec(shape, lambda *unused: (0,) * len(shape))


PIECE = 16


def arrange_kernel(pieces, qkv_ref, send_ref, kv_ref, came, turned, in_sems, out_sems):
    rows = pieces * PIECE
    arrivals = [
        pltpu.make_async_copy(
            qkv_ref.at[pl.ds(piece * PIECE, PIECE)], came.at[piece], in_sems.at[piece]
        )
        for piece in range(pieces)
    ]
    for arrival in arrivals:
        arrival.start()
    departures = []
    for piece, arrival in enumerate(arrivals):
        arrival.wait()
        for part in range(3):
            by_head = jnp.swapaxes(came[piece, :, part], 0, 1)
            turned[piece, :, part * PIECE : (part + 1) * PIECE] = by_head
            if part:
                at = (part - 1) * rows + piece * PIECE
                kv_ref[:, at : at + PIECE] = by_head
        departure = pltpu.make_async_copy(
            turned.at[piece], send_ref.at[:, piece], out_sems.at[piece]
        )
        departure.start()
        departures.append(departure)
    for departure in departures:
        departure.wait()


def arrange(audio_qkv):
    rows, parts, heads, size = audio_qkv.shape
    dtype = audio_qkv.dtype
    pieces = rows // PIECE
    return pl.pallas_call(
        functools.partial(arrange_kernel, pieces),
        in_specs=[pl.BlockSpec(memory_space=pltpu.HBM)],
        out_specs=(
            pl.BlockSpec(memory_space=pltpu.HBM),
            pl.BlockSpec(memory_space=pltpu.VMEM),
        ),
        out_shape=(
            pltpu.HBM((heads, pieces, parts * PIECE, size), dtype),
            jax.ShapeDtypeStruct((heads, 2 * rows, size), dtype),
        ),
        scratch_shapes=[
            pltpu.VMEM((pieces, PIECE, parts, heads, size), dtype),
            pltpu.VMEM((pieces, heads, parts * PIECE, size), dtype),
            pltpu.SemaphoreType.DMA((pieces,)),
            pltpu.SemaphoreType.DMA((pieces,)),
        ],
        compiler_params=params(),
        name="arrange",
    )(pltpu.with_memory_space_constraint(audio_qkv, pltpu.HBM))


def scores_of(queries, keys):
    return lax.dot_general(
        queries, keys, (((1,), (1,)), ((), ())), preferred_element_type=jnp.float32
    )


def attend_kernel(scale, recv_ref, out_ref, held, sems):
    sources, pieces, unused, size = recv_ref.shape
    total = sources * pieces * PIECE
    chunk = total // sems.shape[0]
    group = chunk // (pieces * PIECE)
    factor = scale * LOG2E
    keys = recv_ref[:, :, PIECE : 2 * PIECE].reshape(total, size)
    values = recv_ref[:, :, 2 * PIECE :].reshape(total, size)
    chunks = total // chunk
    scores, weights, sums, departures = {}, {}, {}, []
    for step in range(chunks + 2):
        if step < chunks:
            first = step * group
            queries = recv_ref[first : first + group, :, :PIECE].reshape(chunk, size)
            scores[step] = scores_of(queries, keys)
        if 0 <= step - 1 < chunks:
            now = scores.pop(step - 1)
            top = jnp.max(now, axis=1, keepdims=True)
            exact = jnp.exp2((now - top) * factor)
            sums[step - 1] = jnp.sum(exact, axis=1, keepdims=True)
            weights[step - 1] = exact.astype(jnp.bfloat16)
        if step >= 2:
            summed = jnp.dot(
                weights.pop(step - 2), values, preferred_element_type=jnp.float32
            )
            result = (summed / sums.pop(step - 2)).astype(jnp.bfloat16)
            at = (step - 2) * group
            held[at : at + group] = result.reshape(group, pieces * PIECE, size)
            departure = pltpu.make_async_copy(
                held.at[pl.ds(at, group)], out_ref.at[pl.ds(at, group)], sems.at[step - 2]
            )
            departure.start()
            departures.append(departure)
    for departure in departures:
        departure.wait()


def attend(recv, scale):
    sources, pieces, unused, size = recv.shape
    rows = pieces * PIECE
    total = sources * rows
    return pl.pallas_call(
        functools.partial(attend_kernel, scale),
        in_specs=[pl.BlockSpec(memory_space=pltpu.VMEM)],
        out_specs=pl.BlockSpec(memory_space=pltpu.HBM),
        out_shape=pltpu.HBM((sources, rows, size), jnp.bfloat16),
        scratch_shapes=[
            pltpu.VMEM((sources, rows, size), jnp.bfloat16),
            pltpu.SemaphoreType.DMA((total // 128,)),
        ],
        compiler_params=params(),
        cost_estimate=pl.CostEstimate(
            flops=4 * total * total * size, bytes_accessed=8 * total * size,
            transcendentals=total * total,
        ),
        name="attend",
    )(recv)


def attend_band_kernel(query_rows, scale, query_ref, recv_ref, out_ref):
    sources, both, size = recv_ref.shape
    rows = both // 2
    group = 256 // query_rows
    factor = scale * LOG2E
    for first in range(0, sources, group):
        queries = query_ref[first : first + group].reshape(group * query_rows, size)

        def advance(step, state):
            top, total, summed = state
            at = pl.ds(step * PIECE, PIECE)
            keys = recv_ref[at, :rows].reshape(PIECE * rows, size)
            values = recv_ref[at, rows:].reshape(PIECE * rows, size)
            scores = scores_of(queries, keys)
            new_top = jnp.maximum(top, jnp.max(scores, axis=1, keepdims=True))
            weights = jnp.exp2((scores - new_top) * factor)
            rescale = jnp.exp2((top - new_top) * factor)
            new_total = total * rescale + jnp.sum(weights, axis=1, keepdims=True)
            new_summed = summed * rescale + jnp.dot(
                weights.astype(jnp.bfloat16), values, preferred_element_type=jnp.float32
            )
            return new_top, new_total, new_summed

        start = (
            jnp.full((group * query_rows, 1), LOWEST, jnp.float32),
            jnp.zeros((group * query_rows, 1), jnp.float32),
            jnp.zeros((group * query_rows, size), jnp.float32),
        )
        state = lax.fori_loop(0, sources // PIECE, advance, start)
        result = (state[2] / state[1]).astype(jnp.bfloat16)
        out_ref[first : first + group] = result.reshape(group, query_rows, size)


def attend_band(queries, recv, scale):
    return pl.pallas_call(
        functools.partial(attend_band_kernel, queries.shape[1], scale),
        out_shape=jax.ShapeDtypeStruct(queries.shape, jnp.bfloat16),
        compiler_params=params(),
        name="attend_band",
    )(queries, recv)


def collect_kernel(by_head_ref, out_ref, turned, sems):
    departures = []
    for piece in range(by_head_ref.shape[1] // PIECE):
        at = pl.ds(piece * PIECE, PIECE)
        turned[at] = jnp.swapaxes(by_head_ref[:, at], 0, 1)
        departure = pltpu.make_async_copy(turned.at[at], out_ref.at[at], sems.at[piece])
        departure.start()
        departures.append(departure)
    for departure in departures:
        departure.wait()


def collect(by_head):
    heads, rows, size = by_head.shape
    return pl.pallas_call(
        collect_kernel,
        in_specs=[pl.BlockSpec(memory_space=pltpu.VMEM)],
        out_specs=pl.BlockSpec(memory_space=pltpu.HBM),
        out_shape=pltpu.HBM((rows, heads, size), by_head.dtype),
        scratch_shapes=[
            pltpu.VMEM((rows, heads, size), by_head.dtype),
            pltpu.SemaphoreType.DMA((rows // PIECE,)),
        ],
        compiler_params=params(),
        name="collect",
    )(by_head)


def video_kernel(
    rows, slots, scale, group, pairs_ref, counts_ref, where_ref,
    video_ref, own_ref, core_ref, chip_ref, out_ref,
    near_keys, near_values, keys_ref, values_ref, queries_ref, result_ref, identity_ref,
):
    block = pl.program_id(0)
    heads, unused, size = own_ref.shape

    @pl.when(block == 0)
    def _():
        for ref, place in ((own_ref, rows), (core_ref, where_ref[1]), (chip_ref, where_ref[2])):
            at = pl.ds(pl.multiple_of(place, rows), rows)
            near_keys[:, at] = ref[:, :rows]
            near_values[:, at] = ref[:, rows:]
        row = lax.broadcasted_iota(jnp.int32, (VBLK, VBLK), 0)
        column = lax.broadcasted_iota(jnp.int32, (VBLK, VBLK), 1)
        identity_ref[...] = jnp.where(row == column, 1.0, 0.0).astype(jnp.bfloat16)

    queries_ref[...] = jnp.swapaxes(video_ref[...], 0, 1)
    for slot in range(slots):
        start = pl.multiple_of((pairs_ref[block, slot] - where_ref[0]) * ABLK, ABLK)
        here = slice(slot * ABLK, (slot + 1) * ABLK)
        keys_ref[:, here] = near_keys[:, pl.ds(start, ABLK)]
        values_ref[:, here] = near_values[:, pl.ds(start, ABLK)]
    key_row = lax.broadcasted_iota(jnp.int32, (slots * ABLK, VBLK), 0)
    live = key_row < counts_ref[block] * ABLK
    factor = scale * LOG2E
    for first in range(0, heads, group):
        members = range(first, first + group)
        scores = [scores_of(keys_ref[head], queries_ref[head]) for head in members]
        scores = jnp.stack([jnp.where(live, one, LOWEST) for one in scores])
        top = jnp.max(scores, axis=1, keepdims=True)
        exact = jnp.exp2((scores - top) * factor)
        share = 1.0 / jnp.sum(exact, axis=1, keepdims=True)
        weights = (exact * share).astype(jnp.bfloat16)
        turned = [
            scores_of(identity_ref[...], weights[i]).astype(jnp.bfloat16) for i in range(group)
        ]
        for i, head in enumerate(members):
            result_ref[head] = jnp.dot(
                turned[i], values_ref[head], preferred_element_type=jnp.float32
            ).astype(jnp.bfloat16)
    out_ref[...] = jnp.swapaxes(result_ref[...], 0, 1)


def video(video_q, own, core, chip, pairs, counts, where, scale):
    total, heads, size = video_q.shape
    rows = own.shape[1] // 2
    slots = pairs.shape[1]
    blocks = total // VBLK
    block_spec = pl.BlockSpec((VBLK, heads, size), lambda i, *unused: (i, 0, 0))
    work = total * heads * slots * ABLK
    return pl.pallas_call(
        functools.partial(video_kernel, rows, slots, scale, 4),
        grid_spec=pltpu.PrefetchScalarGridSpec(
            num_scalar_prefetch=3,
            grid=(blocks,),
            in_specs=[block_spec] + [whole(own.shape)] * 3,
            out_specs=block_spec,
            scratch_shapes=[
                pltpu.VMEM((heads, 3 * rows, size), jnp.bfloat16),
                pltpu.VMEM((heads, 3 * rows, size), jnp.bfloat16),
                pltpu.VMEM((heads, slots * ABLK, size), jnp.bfloat16),
                pltpu.VMEM((heads, slots * ABLK, size), jnp.bfloat16),
                pltpu.VMEM((heads, VBLK, size), jnp.bfloat16),
                pltpu.VMEM((heads, VBLK, size), jnp.bfloat16),
                pltpu.VMEM((VBLK, VBLK), jnp.bfloat16),
            ],
        ),
        out_shape=jax.ShapeDtypeStruct(video_q.shape, jnp.bfloat16),
        compiler_params=params(),
        cost_estimate=pl.CostEstimate(
            flops=4 * work * size, bytes_accessed=32 * total * heads * size, transcendentals=work
        ),
        name="video",
    )(pairs, counts, where, video_q, own, core, chip)


def local(audio_qkv, video_q, pairs, counts):
    devices = lax.axis_size("seq")
    rows, unused, heads, size = audio_qkv.shape
    bands = devices // heads
    band_rows = rows // bands
    scale = size ** (-0.5)
    send, kv = arrange(audio_qkv)
    core_pairs = [(i, i ^ 1) for i in range(devices)]
    chip_pairs = [(i, ((i + 1) ^ 1) - 1) for i in range(1, devices - 1)]

    chip = lax.ppermute(kv, "seq", chip_pairs)

    order = list(range(devices))[::-1]

    def exchange(value):
        return lax.all_to_all(
            value, "seq", split_axis=0, concat_axis=0, tiled=True, axis_index_groups=[order]
        )

    core = lax.ppermute(kv, "seq", core_pairs)
    me = lax.axis_index("seq")
    odd = me & 1
    where = jnp.stack([(me - 1) * (rows // ABLK), 2 * (1 - odd) * rows, 2 * odd * rows])
    video_cross = video(
        video_q, kv, core, chip, pairs, counts, where.astype(jnp.int32), scale
    )
    if bands == 1:
        head_out = attend(exchange(send), scale)
    else:
        queries = exchange(send[:, :, :PIECE].reshape(devices, band_rows, size))
        spread = jnp.broadcast_to(kv[:, None], (heads, bands, 2 * rows, size))
        recv = exchange(spread.reshape(devices, 2 * rows, size))
        head_out = attend_band(queries, recv, scale)
    returned, video_cross = lax.optimization_barrier((exchange(head_out), video_cross))
    audio_attn = collect(returned.reshape(heads, rows, size))
    return audio_attn, video_cross


def solution(mesh):
    in_specs = (
        P(("groups", "seq"), None, None, None),
        P(("groups", "seq"), None, None),
        P(("groups", "seq"), None),
        P(("groups", "seq")),
    )
    out_specs = (P(("groups", "seq"), None, None), P(("groups", "seq"), None, None))
    return jax.shard_map(local, mesh=mesh, in_specs=in_specs, out_specs=out_specs, check_vma=False)
```

```python
import functools

import jax
import jax.numpy as jnp
from jax import lax
from jax.experimental import pallas as pl
from jax.experimental.pallas import tpu as pltpu
from jax.sharding import PartitionSpec as P

ABLK = 32
VBLK = 128
LOG2E = 1.4426950408889634
LOWEST = -1e30
VMEM_LIMIT = 48 * 1024 * 1024


def params():
    return pltpu.CompilerParams(vmem_limit_bytes=VMEM_LIMIT)


PIECE = 16


def arrange_kernel(pieces, qkv_ref, send_ref, kv_ref, came, turned, in_sems, out_sems):
    rows = pieces * PIECE
    arrivals = [
        pltpu.make_async_copy(
            qkv_ref.at[pl.ds(piece * PIECE, PIECE)], came.at[piece], in_sems.at[piece]
        )
        for piece in range(pieces)
    ]
    for arrival in arrivals:
        arrival.start()
    departures = []
    for piece, arrival in enumerate(arrivals):
        arrival.wait()
        for part in range(3):
            by_head = jnp.swapaxes(came[piece, :, part], 0, 1)
            turned[piece, :, part * PIECE : (part + 1) * PIECE] = by_head
            if part:
                at = (part - 1) * rows + piece * PIECE
                kv_ref[:, at : at + PIECE] = by_head
        departure = pltpu.make_async_copy(
            turned.at[piece], send_ref.at[:, piece], out_sems.at[piece]
        )
        departure.start()
        departures.append(departure)
    for departure in departures:
        departure.wait()


def arrange(audio_qkv):
    rows, parts, heads, size = audio_qkv.shape
    dtype = audio_qkv.dtype
    pieces = rows // PIECE
    return pl.pallas_call(
        functools.partial(arrange_kernel, pieces),
        in_specs=[pl.BlockSpec(memory_space=pltpu.HBM)],
        out_specs=(
            pl.BlockSpec(memory_space=pltpu.HBM),
            pl.BlockSpec(memory_space=pltpu.VMEM),
        ),
        out_shape=(
            pltpu.HBM((heads, pieces, parts * PIECE, size), dtype),
            jax.ShapeDtypeStruct((heads, 2 * rows, size), dtype),
        ),
        scratch_shapes=[
            pltpu.VMEM((pieces, PIECE, parts, heads, size), dtype),
            pltpu.VMEM((pieces, heads, parts * PIECE, size), dtype),
            pltpu.SemaphoreType.DMA((pieces,)),
            pltpu.SemaphoreType.DMA((pieces,)),
        ],
        compiler_params=params(),
        name="arrange",
    )(pltpu.with_memory_space_constraint(audio_qkv, pltpu.HBM))


def scores_of(queries, keys):
    return lax.dot_general(
        queries, keys, (((1,), (1,)), ((), ())), preferred_element_type=jnp.float32
    )


def attend_kernel(scale, recv_ref, out_ref, held, sems):
    sources, pieces, unused, size = recv_ref.shape
    total = sources * pieces * PIECE
    chunk = total // sems.shape[0]
    group = chunk // (pieces * PIECE)
    factor = scale * LOG2E
    keys = recv_ref[:, :, PIECE : 2 * PIECE].reshape(total, size)
    values = recv_ref[:, :, 2 * PIECE :].reshape(total, size)
    chunks = total // chunk
    scores, weights, sums, departures = {}, {}, {}, []
    for step in range(chunks + 2):
        if step < chunks:
            first = step * group
            queries = recv_ref[first : first + group, :, :PIECE].reshape(chunk, size)
            scores[step] = scores_of(queries, keys)
        if 0 <= step - 1 < chunks:
            now = scores.pop(step - 1)
            top = jnp.max(now, axis=1, keepdims=True)
            exact = jnp.exp2((now - top) * factor)
            sums[step - 1] = jnp.sum(exact, axis=1, keepdims=True)
            weights[step - 1] = exact.astype(jnp.bfloat16)
        if step >= 2:
            summed = jnp.dot(
                weights.pop(step - 2), values, preferred_element_type=jnp.float32
            )
            result = (summed / sums.pop(step - 2)).astype(jnp.bfloat16)
            at = (step - 2) * group
            held[at : at + group] = result.reshape(group, pieces * PIECE, size)
            departure = pltpu.make_async_copy(
                held.at[pl.ds(at, group)], out_ref.at[pl.ds(at, group)], sems.at[step - 2]
            )
            departure.start()
            departures.append(departure)
    for departure in departures:
        departure.wait()


def attend(recv, scale):
    sources, pieces, unused, size = recv.shape
    rows = pieces * PIECE
    total = sources * rows
    return pl.pallas_call(
        functools.partial(attend_kernel, scale),
        in_specs=[pl.BlockSpec(memory_space=pltpu.VMEM)],
        out_specs=pl.BlockSpec(memory_space=pltpu.HBM),
        out_shape=pltpu.HBM((sources, rows, size), jnp.bfloat16),
        scratch_shapes=[
            pltpu.VMEM((sources, rows, size), jnp.bfloat16),
            pltpu.SemaphoreType.DMA((total // 128,)),
        ],
        compiler_params=params(),
        cost_estimate=pl.CostEstimate(
            flops=4 * total * total * size, bytes_accessed=8 * total * size,
            transcendentals=total * total,
        ),
        name="attend",
    )(recv)


def attend_band_kernel(query_rows, scale, query_ref, recv_ref, out_ref):
    sources, both, size = recv_ref.shape
    rows = both // 2
    group = 256 // query_rows
    factor = scale * LOG2E
    for first in range(0, sources, group):
        queries = query_ref[first : first + group].reshape(group * query_rows, size)

        def advance(step, state):
            top, total, summed = state
            at = pl.ds(step * PIECE, PIECE)
            keys = recv_ref[at, :rows].reshape(PIECE * rows, size)
            values = recv_ref[at, rows:].reshape(PIECE * rows, size)
            scores = scores_of(queries, keys)
            new_top = jnp.maximum(top, jnp.max(scores, axis=1, keepdims=True))
            weights = jnp.exp2((scores - new_top) * factor)
            rescale = jnp.exp2((top - new_top) * factor)
            new_total = total * rescale + jnp.sum(weights, axis=1, keepdims=True)
            new_summed = summed * rescale + jnp.dot(
                weights.astype(jnp.bfloat16), values, preferred_element_type=jnp.float32
            )
            return new_top, new_total, new_summed

        start = (
            jnp.full((group * query_rows, 1), LOWEST, jnp.float32),
            jnp.zeros((group * query_rows, 1), jnp.float32),
            jnp.zeros((group * query_rows, size), jnp.float32),
        )
        state = lax.fori_loop(0, sources // PIECE, advance, start)
        result = (state[2] / state[1]).astype(jnp.bfloat16)
        out_ref[first : first + group] = result.reshape(group, query_rows, size)


def attend_band(queries, recv, scale):
    return pl.pallas_call(
        functools.partial(attend_band_kernel, queries.shape[1], scale),
        out_shape=jax.ShapeDtypeStruct(queries.shape, jnp.bfloat16),
        compiler_params=params(),
        name="attend_band",
    )(queries, recv)


def collect_kernel(by_head_ref, out_ref, turned, sems):
    departures = []
    for piece in range(by_head_ref.shape[1] // PIECE):
        at = pl.ds(piece * PIECE, PIECE)
        turned[at] = jnp.swapaxes(by_head_ref[:, at], 0, 1)
        departure = pltpu.make_async_copy(turned.at[at], out_ref.at[at], sems.at[piece])
        departure.start()
        departures.append(departure)
    for departure in departures:
        departure.wait()


def collect(by_head):
    heads, rows, size = by_head.shape
    return pl.pallas_call(
        collect_kernel,
        in_specs=[pl.BlockSpec(memory_space=pltpu.VMEM)],
        out_specs=pl.BlockSpec(memory_space=pltpu.HBM),
        out_shape=pltpu.HBM((rows, heads, size), by_head.dtype),
        scratch_shapes=[
            pltpu.VMEM((rows, heads, size), by_head.dtype),
            pltpu.SemaphoreType.DMA((rows // PIECE,)),
        ],
        compiler_params=params(),
        name="collect",
    )(by_head)


def video_kernel(
    scale, group, pairs_ref, counts_ref, where_ref, video_ref, own_ref, core_ref, chip_ref, out_ref,
    near_keys, near_values, keys_ref, values_ref, queries_ref, result_ref, turned, sems,
):
    heads, both, size = own_ref.shape
    rows = both // 2
    blocks, slots = pairs_ref.shape
    for ref, place in ((own_ref, rows), (core_ref, where_ref[1]), (chip_ref, where_ref[2])):
        at = pl.ds(pl.multiple_of(place, rows), rows)
        near_keys[:, at] = ref[:, :rows]
        near_values[:, at] = ref[:, rows:]
    values_ref[:, :, size:] = jnp.ones((heads, slots * ABLK, size), jnp.bfloat16)
    column = lax.broadcasted_iota(jnp.int32, (VBLK, slots * ABLK), 1)
    factor = scale * LOG2E

    def departure(block):
        at = pl.ds(pl.multiple_of(block * VBLK, VBLK), VBLK)
        return pltpu.make_async_copy(turned.at[block], out_ref.at[at], sems.at[block])

    def one_block(block, carried):
        at = pl.ds(pl.multiple_of(block * VBLK, VBLK), VBLK)
        queries_ref[...] = jnp.swapaxes(video_ref[at], 0, 1)
        for slot in range(slots):
            start = pl.multiple_of((pairs_ref[block, slot] - where_ref[0]) * ABLK, ABLK)
            here = slice(slot * ABLK, (slot + 1) * ABLK)
            keys_ref[:, here] = near_keys[:, pl.ds(start, ABLK)]
            values_ref[:, here, :size] = near_values[:, pl.ds(start, ABLK)]
        live = column < counts_ref[block] * ABLK
        for first in range(0, heads, group):
            members = range(first, first + group)
            scores = [scores_of(queries_ref[head], keys_ref[head]) for head in members]
            scores = jnp.stack([jnp.where(live, one, LOWEST) for one in scores])
            top = jnp.max(scores, axis=2, keepdims=True)
            weights = jnp.exp2((scores - top) * factor).astype(jnp.bfloat16)
            summed = [
                jnp.dot(weights[i], values_ref[head], preferred_element_type=jnp.float32)
                for i, head in enumerate(members)
            ]
            for i, head in enumerate(members):
                result_ref[head] = (summed[i][:, :size] / summed[i][:, size:]).astype(jnp.bfloat16)
        turned[block] = jnp.swapaxes(result_ref[...], 0, 1)
        departure(block).start()
        return carried

    lax.fori_loop(0, blocks, one_block, 0)
    for block in range(blocks):
        departure(block).wait()


def video(video_q, own, core, chip, pairs, counts, where, scale):
    total, heads, size = video_q.shape
    rows = own.shape[1] // 2
    blocks, slots = pairs.shape
    work = total * heads * slots * ABLK
    in_smem = pl.BlockSpec(memory_space=pltpu.SMEM)
    in_vmem = pl.BlockSpec(memory_space=pltpu.VMEM)
    return pl.pallas_call(
        functools.partial(video_kernel, scale, 4),
        in_specs=[in_smem] * 3 + [in_vmem] * 4,
        out_specs=pl.BlockSpec(memory_space=pltpu.HBM),
        out_shape=pltpu.HBM(video_q.shape, jnp.bfloat16),
        scratch_shapes=[
            pltpu.VMEM((heads, 3 * rows, size), jnp.bfloat16),
            pltpu.VMEM((heads, 3 * rows, size), jnp.bfloat16),
            pltpu.VMEM((heads, slots * ABLK, size), jnp.bfloat16),
            pltpu.VMEM((heads, slots * ABLK, 2 * size), jnp.bfloat16),
            pltpu.VMEM((heads, VBLK, size), jnp.bfloat16),
            pltpu.VMEM((heads, VBLK, size), jnp.bfloat16),
            pltpu.VMEM((blocks, VBLK, heads, size), jnp.bfloat16),
            pltpu.SemaphoreType.DMA((blocks,)),
        ],
        compiler_params=params(),
        cost_estimate=pl.CostEstimate(
            flops=4 * work * size, bytes_accessed=32 * total * heads * size, transcendentals=work
        ),
        name="video",
    )(pairs, counts, where, video_q, own, core, chip)


def local(audio_qkv, video_q, pairs, counts):
    devices = lax.axis_size("seq")
    rows, unused, heads, size = audio_qkv.shape
    bands = devices // heads
    band_rows = rows // bands
    scale = size ** (-0.5)
    send, kv = arrange(audio_qkv)
    core_pairs = [(i, i ^ 1) for i in range(devices)]
    chip_pairs = [(i, ((i + 1) ^ 1) - 1) for i in range(1, devices - 1)]

    chip = lax.ppermute(kv, "seq", chip_pairs)

    order = list(range(devices))[::-1]

    def exchange(value):
        return lax.all_to_all(
            value, "seq", split_axis=0, concat_axis=0, tiled=True, axis_index_groups=[order]
        )

    core = lax.ppermute(kv, "seq", core_pairs)
    me = lax.axis_index("seq")
    odd = me & 1
    where = jnp.stack([(me - 1) * (rows // ABLK), 2 * (1 - odd) * rows, 2 * odd * rows])
    video_cross = video(
        video_q, kv, core, chip, pairs, counts, where.astype(jnp.int32), scale
    )
    if bands == 1:
        head_out = attend(exchange(send), scale)
    else:
        queries = exchange(send[:, :, :PIECE].reshape(devices, band_rows, size))
        spread = jnp.broadcast_to(kv[:, None], (heads, bands, 2 * rows, size))
        recv = exchange(spread.reshape(devices, 2 * rows, size))
        head_out = attend_band(queries, recv, scale)
    returned, video_cross = lax.optimization_barrier((exchange(head_out), video_cross))
    audio_attn = collect(returned.reshape(heads, rows, size))
    return audio_attn, video_cross


def solution(mesh):
    in_specs = (
        P(("groups", "seq"), None, None, None),
        P(("groups", "seq"), None, None),
        P(("groups", "seq"), None),
        P(("groups", "seq")),
    )
    out_specs = (P(("groups", "seq"), None, None), P(("groups", "seq"), None, None))
    return jax.shard_map(local, mesh=mesh, in_specs=in_specs, out_specs=out_specs, check_vma=False)
```

```python
import functools

import jax
import jax.numpy as jnp
from jax import lax
from jax.experimental import pallas as pl
from jax.experimental.pallas import tpu as pltpu
from jax.sharding import PartitionSpec as P

ABLK = 32
VBLK = 128
LOG2E = 1.4426950408889634
LOWEST = -1e30
VMEM_LIMIT = 48 * 1024 * 1024


def params():
    return pltpu.CompilerParams(vmem_limit_bytes=VMEM_LIMIT)


PIECE = 16


def arrange_kernel(pieces, qkv_ref, send_ref, kv_ref, came, turned, in_sems, out_sems):
    rows = pieces * PIECE
    arrivals = [
        pltpu.make_async_copy(
            qkv_ref.at[pl.ds(piece * PIECE, PIECE)], came.at[piece], in_sems.at[piece]
        )
        for piece in range(pieces)
    ]
    for arrival in arrivals:
        arrival.start()
    departures = []
    for piece, arrival in enumerate(arrivals):
        arrival.wait()
        for part in range(3):
            by_head = jnp.swapaxes(came[piece, :, part], 0, 1)
            turned[piece, :, part * PIECE : (part + 1) * PIECE] = by_head
            if part:
                at = (part - 1) * rows + piece * PIECE
                kv_ref[:, at : at + PIECE] = by_head
        departure = pltpu.make_async_copy(
            turned.at[piece], send_ref.at[:, piece], out_sems.at[piece]
        )
        departure.start()
        departures.append(departure)
    for departure in departures:
        departure.wait()


def arrange(audio_qkv):
    rows, parts, heads, size = audio_qkv.shape
    dtype = audio_qkv.dtype
    pieces = rows // PIECE
    return pl.pallas_call(
        functools.partial(arrange_kernel, pieces),
        in_specs=[pl.BlockSpec(memory_space=pltpu.HBM)],
        out_specs=(
            pl.BlockSpec(memory_space=pltpu.HBM),
            pl.BlockSpec(memory_space=pltpu.VMEM),
        ),
        out_shape=(
            pltpu.HBM((heads, pieces, parts * PIECE, size), dtype),
            jax.ShapeDtypeStruct((heads, 2 * rows, size), dtype),
        ),
        scratch_shapes=[
            pltpu.VMEM((pieces, PIECE, parts, heads, size), dtype),
            pltpu.VMEM((pieces, heads, parts * PIECE, size), dtype),
            pltpu.SemaphoreType.DMA((pieces,)),
            pltpu.SemaphoreType.DMA((pieces,)),
        ],
        compiler_params=params(),
        name="arrange",
    )(pltpu.with_memory_space_constraint(audio_qkv, pltpu.HBM))


def scores_of(queries, keys):
    return lax.dot_general(
        queries, keys, (((1,), (1,)), ((), ())), preferred_element_type=jnp.float32
    )


def attend_kernel(scale, recv_ref, out_ref, held, sems):
    sources, pieces, unused, size = recv_ref.shape
    total = sources * pieces * PIECE
    chunk = total // sems.shape[0]
    group = chunk // (pieces * PIECE)
    factor = scale * LOG2E
    keys = recv_ref[:, :, PIECE : 2 * PIECE].reshape(total, size)
    values = recv_ref[:, :, 2 * PIECE :].reshape(total, size)
    chunks = total // chunk
    scores, weights, sums, departures = {}, {}, {}, []
    for step in range(chunks + 2):
        if step < chunks:
            first = step * group
            queries = recv_ref[first : first + group, :, :PIECE].reshape(chunk, size)
            scores[step] = scores_of(queries, keys)
        if 0 <= step - 1 < chunks:
            now = scores.pop(step - 1)
            top = jnp.max(now, axis=1, keepdims=True)
            exact = jnp.exp2((now - top) * factor)
            sums[step - 1] = jnp.sum(exact, axis=1, keepdims=True)
            weights[step - 1] = exact.astype(jnp.bfloat16)
        if step >= 2:
            summed = jnp.dot(
                weights.pop(step - 2), values, preferred_element_type=jnp.float32
            )
            result = (summed / sums.pop(step - 2)).astype(jnp.bfloat16)
            at = (step - 2) * group
            held[at : at + group] = result.reshape(group, pieces * PIECE, size)
            departure = pltpu.make_async_copy(
                held.at[pl.ds(at, group)], out_ref.at[pl.ds(at, group)], sems.at[step - 2]
            )
            departure.start()
            departures.append(departure)
    for departure in departures:
        departure.wait()


def attend(recv, scale):
    sources, pieces, unused, size = recv.shape
    rows = pieces * PIECE
    total = sources * rows
    return pl.pallas_call(
        functools.partial(attend_kernel, scale),
        in_specs=[pl.BlockSpec(memory_space=pltpu.VMEM)],
        out_specs=pl.BlockSpec(memory_space=pltpu.HBM),
        out_shape=pltpu.HBM((sources, rows, size), jnp.bfloat16),
        scratch_shapes=[
            pltpu.VMEM((sources, rows, size), jnp.bfloat16),
            pltpu.SemaphoreType.DMA((total // 128,)),
        ],
        compiler_params=params(),
        cost_estimate=pl.CostEstimate(
            flops=4 * total * total * size, bytes_accessed=8 * total * size,
            transcendentals=total * total,
        ),
        name="attend",
    )(recv)


def attend_band_kernel(query_rows, scale, query_ref, recv_ref, out_ref):
    sources, both, size = recv_ref.shape
    rows = both // 2
    group = 256 // query_rows
    factor = scale * LOG2E
    for first in range(0, sources, group):
        queries = query_ref[first : first + group].reshape(group * query_rows, size)

        def advance(step, state):
            top, total, summed = state
            at = pl.ds(step * PIECE, PIECE)
            keys = recv_ref[at, :rows].reshape(PIECE * rows, size)
            values = recv_ref[at, rows:].reshape(PIECE * rows, size)
            scores = scores_of(queries, keys)
            new_top = jnp.maximum(top, jnp.max(scores, axis=1, keepdims=True))
            weights = jnp.exp2((scores - new_top) * factor)
            rescale = jnp.exp2((top - new_top) * factor)
            new_total = total * rescale + jnp.sum(weights, axis=1, keepdims=True)
            new_summed = summed * rescale + jnp.dot(
                weights.astype(jnp.bfloat16), values, preferred_element_type=jnp.float32
            )
            return new_top, new_total, new_summed

        start = (
            jnp.full((group * query_rows, 1), LOWEST, jnp.float32),
            jnp.zeros((group * query_rows, 1), jnp.float32),
            jnp.zeros((group * query_rows, size), jnp.float32),
        )
        state = lax.fori_loop(0, sources // PIECE, advance, start)
        result = (state[2] / state[1]).astype(jnp.bfloat16)
        out_ref[first : first + group] = result.reshape(group, query_rows, size)


def attend_band(queries, recv, scale):
    return pl.pallas_call(
        functools.partial(attend_band_kernel, queries.shape[1], scale),
        out_shape=jax.ShapeDtypeStruct(queries.shape, jnp.bfloat16),
        compiler_params=params(),
        name="attend_band",
    )(queries, recv)


def collect_kernel(by_head_ref, out_ref, turned, sems):
    departures = []
    for piece in range(by_head_ref.shape[1] // PIECE):
        at = pl.ds(piece * PIECE, PIECE)
        turned[at] = jnp.swapaxes(by_head_ref[:, at], 0, 1)
        departure = pltpu.make_async_copy(turned.at[at], out_ref.at[at], sems.at[piece])
        departure.start()
        departures.append(departure)
    for departure in departures:
        departure.wait()


def collect(by_head):
    heads, rows, size = by_head.shape
    return pl.pallas_call(
        collect_kernel,
        in_specs=[pl.BlockSpec(memory_space=pltpu.VMEM)],
        out_specs=pl.BlockSpec(memory_space=pltpu.HBM),
        out_shape=pltpu.HBM((rows, heads, size), by_head.dtype),
        scratch_shapes=[
            pltpu.VMEM((rows, heads, size), by_head.dtype),
            pltpu.SemaphoreType.DMA((rows // PIECE,)),
        ],
        compiler_params=params(),
        name="collect",
    )(by_head)


def video_kernel(
    scale, group, pairs_ref, counts_ref, where_ref, video_ref, own_ref, core_ref, chip_ref, out_ref,
    near_keys, near_values, keys_ref, values_ref, queries_ref, result_ref, turned, sems,
):
    heads, both, size = own_ref.shape
    rows = both // 2
    blocks, slots = pairs_ref.shape
    for ref, place in ((own_ref, rows), (core_ref, where_ref[1]), (chip_ref, where_ref[2])):
        at = pl.ds(pl.multiple_of(place, rows), rows)
        near_keys[:, at] = ref[:, :rows]
        near_values[:, at] = ref[:, rows:]
    values_ref[:, :, :, size:] = jnp.ones((blocks, heads, slots * ABLK, size), jnp.bfloat16)
    column = lax.broadcasted_iota(jnp.int32, (VBLK, slots * ABLK), 1)
    factor = scale * LOG2E

    def prepare(block):
        queries_ref[block] = jnp.swapaxes(video_ref[block * VBLK : (block + 1) * VBLK], 0, 1)
        for slot in range(slots):
            start = pl.multiple_of((pairs_ref[block, slot] - where_ref[0]) * ABLK, ABLK)
            here = slice(slot * ABLK, (slot + 1) * ABLK)
            keys_ref[block, :, here] = near_keys[:, pl.ds(start, ABLK)]
            values_ref[block, :, here, :size] = near_values[:, pl.ds(start, ABLK)]

    def departure(block):
        at = pl.ds(block * VBLK, VBLK)
        return pltpu.make_async_copy(turned.at[block], out_ref.at[at], sems.at[block])

    units = [(block, first) for block in range(blocks) for first in range(0, heads, group)]
    scores, weights = {}, {}
    for step in range(len(units) + 2):
        if step < len(units):
            block, first = units[step]
            if first == 0:
                prepare(block)
            live = column < counts_ref[block] * ABLK
            scores[step] = [
                jnp.where(live, scores_of(queries_ref[block, head], keys_ref[block, head]), LOWEST)
                for head in range(first, first + group)
            ]
        if 1 <= step <= len(units):
            now = jnp.stack(scores.pop(step - 1))
            top = jnp.max(now, axis=2, keepdims=True)
            weights[step - 1] = jnp.exp2((now - top) * factor).astype(jnp.bfloat16)
        if step >= 2:
            block, first = units[step - 2]
            now = weights.pop(step - 2)
            for i in range(group):
                summed = jnp.dot(
                    now[i], values_ref[block, first + i], preferred_element_type=jnp.float32
                )
                result_ref[block, first + i] = (summed[:, :size] / summed[:, size:]).astype(
                    jnp.bfloat16
                )
            if first + group == heads:
                turned[block] = jnp.swapaxes(result_ref[block], 0, 1)
                departure(block).start()
    for block in range(blocks):
        departure(block).wait()


def video(video_q, own, core, chip, pairs, counts, where, scale):
    total, heads, size = video_q.shape
    rows = own.shape[1] // 2
    blocks, slots = pairs.shape
    work = total * heads * slots * ABLK
    in_smem = pl.BlockSpec(memory_space=pltpu.SMEM)
    in_vmem = pl.BlockSpec(memory_space=pltpu.VMEM)
    return pl.pallas_call(
        functools.partial(video_kernel, scale, 4),
        in_specs=[in_smem] * 3 + [in_vmem] * 4,
        out_specs=pl.BlockSpec(memory_space=pltpu.HBM),
        out_shape=pltpu.HBM(video_q.shape, jnp.bfloat16),
        scratch_shapes=[
            pltpu.VMEM((heads, 3 * rows, size), jnp.bfloat16),
            pltpu.VMEM((heads, 3 * rows, size), jnp.bfloat16),
            pltpu.VMEM((blocks, heads, slots * ABLK, size), jnp.bfloat16),
            pltpu.VMEM((blocks, heads, slots * ABLK, 2 * size), jnp.bfloat16),
            pltpu.VMEM((blocks, heads, VBLK, size), jnp.bfloat16),
            pltpu.VMEM((blocks, heads, VBLK, size), jnp.bfloat16),
            pltpu.VMEM((blocks, VBLK, heads, size), jnp.bfloat16),
            pltpu.SemaphoreType.DMA((blocks,)),
        ],
        compiler_params=params(),
        cost_estimate=pl.CostEstimate(
            flops=4 * work * size, bytes_accessed=32 * total * heads * size, transcendentals=work
        ),
        name="video",
    )(pairs, counts, where, video_q, own, core, chip)


def local(audio_qkv, video_q, pairs, counts):
    devices = lax.axis_size("seq")
    rows, unused, heads, size = audio_qkv.shape
    bands = devices // heads
    band_rows = rows // bands
    scale = size ** (-0.5)
    send, kv = arrange(audio_qkv)
    core_pairs = [(i, i ^ 1) for i in range(devices)]
    chip_pairs = [(i, ((i + 1) ^ 1) - 1) for i in range(1, devices - 1)]

    chip = lax.ppermute(kv, "seq", chip_pairs)

    order = list(range(devices))[::-1]

    def exchange(value):
        return lax.all_to_all(
            value, "seq", split_axis=0, concat_axis=0, tiled=True, axis_index_groups=[order]
        )

    core = lax.ppermute(kv, "seq", core_pairs)
    me = lax.axis_index("seq")
    odd = me & 1
    where = jnp.stack([(me - 1) * (rows // ABLK), 2 * (1 - odd) * rows, 2 * odd * rows])
    video_cross = video(
        video_q, kv, core, chip, pairs, counts, where.astype(jnp.int32), scale
    )
    if bands == 1:
        head_out = attend(exchange(send), scale)
    else:
        queries = exchange(send[:, :, :PIECE].reshape(devices, band_rows, size))
        spread = jnp.broadcast_to(kv[:, None], (heads, bands, 2 * rows, size))
        recv = exchange(spread.reshape(devices, 2 * rows, size))
        head_out = attend_band(queries, recv, scale)
    returned, video_cross = lax.optimization_barrier((exchange(head_out), video_cross))
    audio_attn = collect(returned.reshape(heads, rows, size))
    return audio_attn, video_cross


def solution(mesh):
    in_specs = (
        P(("groups", "seq"), None, None, None),
        P(("groups", "seq"), None, None),
        P(("groups", "seq"), None),
        P(("groups", "seq")),
    )
    out_specs = (P(("groups", "seq"), None, None), P(("groups", "seq"), None, None))
    return jax.shard_map(local, mesh=mesh, in_specs=in_specs, out_specs=out_specs, check_vma=False)
```

```python
import functools

import jax
import jax.numpy as jnp
from jax import lax
from jax.experimental import pallas as pl
from jax.experimental.pallas import tpu as pltpu
from jax.sharding import PartitionSpec as P

ABLK = 32
VBLK = 128
LOG2E = 1.4426950408889634
LOWEST = -1e30
VMEM_LIMIT = 48 * 1024 * 1024


def params():
    return pltpu.CompilerParams(vmem_limit_bytes=VMEM_LIMIT)


PIECE = 16


def arrange_kernel(pieces, qkv_ref, send_ref, kv_ref, came, turned, in_sems, out_sems):
    rows = pieces * PIECE
    heads = turned.shape[1]
    halves = 2
    arrivals = []
    for piece in range(pieces):
        for half in range(halves):
            count = PIECE // halves
            arrivals.append(
                pltpu.make_async_copy(
                    qkv_ref.at[pl.ds(piece * PIECE + half * count, count)],
                    came.at[piece, pl.ds(half * count, count)],
                    in_sems.at[piece, half],
                )
            )
    for arrival in arrivals:
        arrival.start()
    departures = []
    for piece in range(pieces):
        for half in range(halves):
            arrivals[piece * halves + half].wait()
        for part in range(3):
            by_head = jnp.swapaxes(came[piece, :, part], 0, 1)
            turned[piece, :, part * PIECE : (part + 1) * PIECE] = by_head
            if part:
                at = (part - 1) * rows + piece * PIECE
                kv_ref[:, at : at + PIECE] = by_head
        for half in range(halves):
            at = pl.ds(half * (heads // halves), heads // halves)
            departure = pltpu.make_async_copy(
                turned.at[piece, at], send_ref.at[at, piece], out_sems.at[piece, half]
            )
            departure.start()
            departures.append(departure)
    for departure in departures:
        departure.wait()


def arrange(audio_qkv):
    rows, parts, heads, size = audio_qkv.shape
    dtype = audio_qkv.dtype
    pieces = rows // PIECE
    return pl.pallas_call(
        functools.partial(arrange_kernel, pieces),
        in_specs=[pl.BlockSpec(memory_space=pltpu.HBM)],
        out_specs=(
            pl.BlockSpec(memory_space=pltpu.HBM),
            pl.BlockSpec(memory_space=pltpu.VMEM),
        ),
        out_shape=(
            pltpu.HBM((heads, pieces, parts * PIECE, size), dtype),
            jax.ShapeDtypeStruct((heads, 2 * rows, size), dtype),
        ),
        scratch_shapes=[
            pltpu.VMEM((pieces, PIECE, parts, heads, size), dtype),
            pltpu.VMEM((pieces, heads, parts * PIECE, size), dtype),
            pltpu.SemaphoreType.DMA((pieces, 2)),
            pltpu.SemaphoreType.DMA((pieces, 2)),
        ],
        compiler_params=params(),
        name="arrange",
    )(pltpu.with_memory_space_constraint(audio_qkv, pltpu.HBM))


def scores_of(queries, keys):
    return lax.dot_general(
        queries, keys, (((1,), (1,)), ((), ())), preferred_element_type=jnp.float32
    )


def attend_kernel(scale, recv_ref, out_ref, held, sems):
    sources, pieces, unused, size = recv_ref.shape
    total = sources * pieces * PIECE
    chunk = total // sems.shape[0]
    group = chunk // (pieces * PIECE)
    factor = scale * LOG2E
    keys = recv_ref[:, :, PIECE : 2 * PIECE].reshape(total, size)
    values = recv_ref[:, :, 2 * PIECE :].reshape(total, size)
    chunks = total // chunk
    scores, weights, sums, departures = {}, {}, {}, []
    for step in range(chunks + 2):
        if step < chunks:
            first = step * group
            queries = recv_ref[first : first + group, :, :PIECE].reshape(chunk, size)
            scores[step] = scores_of(queries, keys)
        if 0 <= step - 1 < chunks:
            now = scores.pop(step - 1)
            top = jnp.max(now, axis=1, keepdims=True)
            exact = jnp.exp2((now - top) * factor)
            sums[step - 1] = jnp.sum(exact, axis=1, keepdims=True)
            weights[step - 1] = exact.astype(jnp.bfloat16)
        if step >= 2:
            summed = jnp.dot(
                weights.pop(step - 2), values, preferred_element_type=jnp.float32
            )
            result = (summed / sums.pop(step - 2)).astype(jnp.bfloat16)
            at = (step - 2) * group
            held[at : at + group] = result.reshape(group, pieces * PIECE, size)
            departure = pltpu.make_async_copy(
                held.at[pl.ds(at, group)], out_ref.at[pl.ds(at, group)], sems.at[step - 2]
            )
            departure.start()
            departures.append(departure)
    for departure in departures:
        departure.wait()


def attend(recv, scale):
    sources, pieces, unused, size = recv.shape
    rows = pieces * PIECE
    total = sources * rows
    return pl.pallas_call(
        functools.partial(attend_kernel, scale),
        in_specs=[pl.BlockSpec(memory_space=pltpu.VMEM)],
        out_specs=pl.BlockSpec(memory_space=pltpu.HBM),
        out_shape=pltpu.HBM((sources, rows, size), jnp.bfloat16),
        scratch_shapes=[
            pltpu.VMEM((sources, rows, size), jnp.bfloat16),
            pltpu.SemaphoreType.DMA((total // 256,)),
        ],
        compiler_params=params(),
        cost_estimate=pl.CostEstimate(
            flops=4 * total * total * size, bytes_accessed=8 * total * size,
            transcendentals=total * total,
        ),
        name="attend",
    )(recv)


def attend_band_kernel(query_rows, scale, query_ref, recv_ref, out_ref):
    sources, both, size = recv_ref.shape
    rows = both // 2
    group = 256 // query_rows
    factor = scale * LOG2E
    for first in range(0, sources, group):
        queries = query_ref[first : first + group].reshape(group * query_rows, size)

        def advance(step, state):
            top, total, summed = state
            at = pl.ds(step * PIECE, PIECE)
            keys = recv_ref[at, :rows].reshape(PIECE * rows, size)
            values = recv_ref[at, rows:].reshape(PIECE * rows, size)
            scores = scores_of(queries, keys)
            new_top = jnp.maximum(top, jnp.max(scores, axis=1, keepdims=True))
            weights = jnp.exp2((scores - new_top) * factor)
            rescale = jnp.exp2((top - new_top) * factor)
            new_total = total * rescale + jnp.sum(weights, axis=1, keepdims=True)
            new_summed = summed * rescale + jnp.dot(
                weights.astype(jnp.bfloat16), values, preferred_element_type=jnp.float32
            )
            return new_top, new_total, new_summed

        start = (
            jnp.full((group * query_rows, 1), LOWEST, jnp.float32),
            jnp.zeros((group * query_rows, 1), jnp.float32),
            jnp.zeros((group * query_rows, size), jnp.float32),
        )
        state = lax.fori_loop(0, sources // PIECE, advance, start)
        result = (state[2] / state[1]).astype(jnp.bfloat16)
        out_ref[first : first + group] = result.reshape(group, query_rows, size)


def attend_band(queries, recv, scale):
    return pl.pallas_call(
        functools.partial(attend_band_kernel, queries.shape[1], scale),
        out_shape=jax.ShapeDtypeStruct(queries.shape, jnp.bfloat16),
        compiler_params=params(),
        name="attend_band",
    )(queries, recv)


def collect_kernel(by_head_ref, out_ref, turned, sems):
    departures = []
    for piece in range(by_head_ref.shape[1] // PIECE):
        at = pl.ds(piece * PIECE, PIECE)
        turned[at] = jnp.swapaxes(by_head_ref[:, at], 0, 1)
        departure = pltpu.make_async_copy(turned.at[at], out_ref.at[at], sems.at[piece])
        departure.start()
        departures.append(departure)
    for departure in departures:
        departure.wait()


def collect(by_head):
    heads, rows, size = by_head.shape
    return pl.pallas_call(
        collect_kernel,
        in_specs=[pl.BlockSpec(memory_space=pltpu.VMEM)],
        out_specs=pl.BlockSpec(memory_space=pltpu.HBM),
        out_shape=pltpu.HBM((rows, heads, size), by_head.dtype),
        scratch_shapes=[
            pltpu.VMEM((rows, heads, size), by_head.dtype),
            pltpu.SemaphoreType.DMA((rows // PIECE,)),
        ],
        compiler_params=params(),
        name="collect",
    )(by_head)


def video_kernel(
    scale, group, pairs_ref, counts_ref, where_ref, video_ref, own_ref, core_ref, chip_ref, out_ref,
    near_keys, near_values, keys_ref, values_ref, queries_ref, result_ref, turned, sems,
):
    heads, both, size = own_ref.shape
    rows = both // 2
    blocks, slots = pairs_ref.shape
    for ref, place in ((own_ref, rows), (core_ref, where_ref[1]), (chip_ref, where_ref[2])):
        at = pl.ds(pl.multiple_of(place, rows), rows)
        near_keys[:, at] = ref[:, :rows]
        near_values[:, at] = ref[:, rows:]
    values_ref[:, :, :, size:] = jnp.ones((blocks, heads, slots * ABLK, size), jnp.bfloat16)
    column = lax.broadcasted_iota(jnp.int32, (VBLK, slots * ABLK), 1)
    factor = scale * LOG2E

    def prepare(block):
        queries_ref[block] = jnp.swapaxes(video_ref[block * VBLK : (block + 1) * VBLK], 0, 1)
        for slot in range(slots):
            start = pl.multiple_of((pairs_ref[block, slot] - where_ref[0]) * ABLK, ABLK)
            here = slice(slot * ABLK, (slot + 1) * ABLK)
            keys_ref[block, :, here] = near_keys[:, pl.ds(start, ABLK)]
            values_ref[block, :, here, :size] = near_values[:, pl.ds(start, ABLK)]

    def departure(block):
        at = pl.ds(block * VBLK, VBLK)
        return pltpu.make_async_copy(turned.at[block], out_ref.at[at], sems.at[block])

    units = [(block, first) for block in range(blocks) for first in range(0, heads, group)]
    scores, weights = {}, {}
    for step in range(len(units) + 2):
        if step < len(units):
            block, first = units[step]
            if first == 0:
                prepare(block)
            live = column < counts_ref[block] * ABLK
            scores[step] = [
                jnp.where(live, scores_of(queries_ref[block, head], keys_ref[block, head]), LOWEST)
                for head in range(first, first + group)
            ]
        if 1 <= step <= len(units):
            now = jnp.stack(scores.pop(step - 1))
            top = jnp.max(now, axis=2, keepdims=True)
            weights[step - 1] = jnp.exp2((now - top) * factor).astype(jnp.bfloat16)
        if step >= 2:
            block, first = units[step - 2]
            now = weights.pop(step - 2)
            for i in range(group):
                summed = jnp.dot(
                    now[i], values_ref[block, first + i], preferred_element_type=jnp.float32
                )
                result_ref[block, first + i] = (summed[:, :size] / summed[:, size:]).astype(
                    jnp.bfloat16
                )
            if first + group == heads:
                turned[block] = jnp.swapaxes(result_ref[block], 0, 1)
                departure(block).start()
    for block in range(blocks):
        departure(block).wait()


def video(video_q, own, core, chip, pairs, counts, where, scale):
    total, heads, size = video_q.shape
    rows = own.shape[1] // 2
    blocks, slots = pairs.shape
    work = total * heads * slots * ABLK
    in_smem = pl.BlockSpec(memory_space=pltpu.SMEM)
    in_vmem = pl.BlockSpec(memory_space=pltpu.VMEM)
    return pl.pallas_call(
        functools.partial(video_kernel, scale, 4),
        in_specs=[in_smem] * 3 + [in_vmem] * 4,
        out_specs=pl.BlockSpec(memory_space=pltpu.HBM),
        out_shape=pltpu.HBM(video_q.shape, jnp.bfloat16),
        scratch_shapes=[
            pltpu.VMEM((heads, 3 * rows, size), jnp.bfloat16),
            pltpu.VMEM((heads, 3 * rows, size), jnp.bfloat16),
            pltpu.VMEM((blocks, heads, slots * ABLK, size), jnp.bfloat16),
            pltpu.VMEM((blocks, heads, slots * ABLK, 2 * size), jnp.bfloat16),
            pltpu.VMEM((blocks, heads, VBLK, size), jnp.bfloat16),
            pltpu.VMEM((blocks, heads, VBLK, size), jnp.bfloat16),
            pltpu.VMEM((blocks, VBLK, heads, size), jnp.bfloat16),
            pltpu.SemaphoreType.DMA((blocks,)),
        ],
        compiler_params=params(),
        cost_estimate=pl.CostEstimate(
            flops=4 * work * size, bytes_accessed=32 * total * heads * size, transcendentals=work
        ),
        name="video",
    )(pairs, counts, where, video_q, own, core, chip)


def local(audio_qkv, video_q, pairs, counts):
    devices = lax.axis_size("seq")
    rows, unused, heads, size = audio_qkv.shape
    bands = devices // heads
    band_rows = rows // bands
    scale = size ** (-0.5)
    send, kv = arrange(audio_qkv)
    core_pairs = [(i, i ^ 1) for i in range(devices)]
    chip_pairs = [(i, ((i + 1) ^ 1) - 1) for i in range(1, devices - 1)]

    chip = lax.ppermute(kv, "seq", chip_pairs)

    order = list(range(devices))[::-1]

    def exchange(value):
        return lax.all_to_all(
            value, "seq", split_axis=0, concat_axis=0, tiled=True, axis_index_groups=[order]
        )

    core = lax.ppermute(kv, "seq", core_pairs)
    me = lax.axis_index("seq")
    odd = me & 1
    where = jnp.stack([(me - 1) * (rows // ABLK), 2 * (1 - odd) * rows, 2 * odd * rows])
    video_cross = video(
        video_q, kv, core, chip, pairs, counts, where.astype(jnp.int32), scale
    )
    if bands == 1:
        head_out = attend(exchange(send), scale)
    else:
        queries = exchange(send[:, :, :PIECE].reshape(devices, band_rows, size))
        spread = jnp.broadcast_to(kv[:, None], (heads, bands, 2 * rows, size))
        recv = exchange(spread.reshape(devices, 2 * rows, size))
        head_out = attend_band(queries, recv, scale)
    returned, video_cross = lax.optimization_barrier((exchange(head_out), video_cross))
    audio_attn = collect(returned.reshape(heads, rows, size))
    return audio_attn, video_cross


def solution(mesh):
    in_specs = (
        P(("groups", "seq"), None, None, None),
        P(("groups", "seq"), None, None),
        P(("groups", "seq"), None),
        P(("groups", "seq")),
    )
    out_specs = (P(("groups", "seq"), None, None), P(("groups", "seq"), None, None))
    return jax.shard_map(local, mesh=mesh, in_specs=in_specs, out_specs=out_specs, check_vma=False)
```

```python
import functools

import jax
import jax.numpy as jnp
from jax import lax
from jax.experimental import pallas as pl
from jax.experimental.pallas import tpu as pltpu
from jax.sharding import PartitionSpec as P

ABLK = 32
VBLK = 128
LOG2E = 1.4426950408889634
LOWEST = -1e30
VMEM_LIMIT = 48 * 1024 * 1024


def params():
    return pltpu.CompilerParams(vmem_limit_bytes=VMEM_LIMIT)


PIECE = 16


def arrange_kernel(pieces, qkv_ref, send_ref, kv_ref, came, turned, in_sems, out_sems):
    rows = pieces * PIECE
    arrivals = [
        pltpu.make_async_copy(
            qkv_ref.at[pl.ds(piece * PIECE, PIECE)], came.at[piece], in_sems.at[piece]
        )
        for piece in range(pieces)
    ]
    for arrival in arrivals:
        arrival.start()
    departures = []
    for piece, arrival in enumerate(arrivals):
        arrival.wait()
        for part in range(3):
            by_head = jnp.swapaxes(came[piece, :, part], 0, 1)
            turned[piece, :, part * PIECE : (part + 1) * PIECE] = by_head
            if part:
                at = (part - 1) * rows + piece * PIECE
                kv_ref[:, at : at + PIECE] = by_head
        departure = pltpu.make_async_copy(
            turned.at[piece], send_ref.at[:, piece], out_sems.at[piece]
        )
        departure.start()
        departures.append(departure)
    for departure in departures:
        departure.wait()


def arrange(audio_qkv):
    rows, parts, heads, size = audio_qkv.shape
    dtype = audio_qkv.dtype
    pieces = rows // PIECE
    return pl.pallas_call(
        functools.partial(arrange_kernel, pieces),
        in_specs=[pl.BlockSpec(memory_space=pltpu.HBM)],
        out_specs=(
            pl.BlockSpec(memory_space=pltpu.HBM),
            pl.BlockSpec(memory_space=pltpu.VMEM),
        ),
        out_shape=(
            pltpu.HBM((heads, pieces, parts * PIECE, size), dtype),
            jax.ShapeDtypeStruct((heads, 2 * rows, size), dtype),
        ),
        scratch_shapes=[
            pltpu.VMEM((pieces, PIECE, parts, heads, size), dtype),
            pltpu.VMEM((pieces, heads, parts * PIECE, size), dtype),
            pltpu.SemaphoreType.DMA((pieces,)),
            pltpu.SemaphoreType.DMA((pieces,)),
        ],
        compiler_params=params(),
        name="arrange",
    )(pltpu.with_memory_space_constraint(audio_qkv, pltpu.HBM))


def scores_of(queries, keys):
    return lax.dot_general(
        queries, keys, (((1,), (1,)), ((), ())), preferred_element_type=jnp.float32
    )


def attend_kernel(scale, recv_ref, out_ref, held, sems):
    sources, pieces, unused, size = recv_ref.shape
    total = sources * pieces * PIECE
    chunk = total // sems.shape[0]
    group = chunk // (pieces * PIECE)
    factor = scale * LOG2E
    keys = recv_ref[:, :, PIECE : 2 * PIECE].reshape(total, size)
    values = recv_ref[:, :, 2 * PIECE :].reshape(total, size)
    chunks = total // chunk
    scores, weights, sums, departures = {}, {}, {}, []
    for step in range(chunks + 2):
        if step < chunks:
            first = step * group
            queries = recv_ref[first : first + group, :, :PIECE].reshape(chunk, size)
            scores[step] = scores_of(queries, keys)
        if 0 <= step - 1 < chunks:
            now = scores.pop(step - 1)
            top = jnp.max(now, axis=1, keepdims=True)
            exact = jnp.exp2((now - top) * factor)
            sums[step - 1] = jnp.sum(exact, axis=1, keepdims=True)
            weights[step - 1] = exact.astype(jnp.bfloat16)
        if step >= 2:
            summed = jnp.dot(
                weights.pop(step - 2), values, preferred_element_type=jnp.float32
            )
            result = (summed / sums.pop(step - 2)).astype(jnp.bfloat16)
            at = (step - 2) * group
            held[at : at + group] = result.reshape(group, pieces * PIECE, size)
            departure = pltpu.make_async_copy(
                held.at[pl.ds(at, group)], out_ref.at[pl.ds(at, group)], sems.at[step - 2]
            )
            departure.start()
            departures.append(departure)
    for departure in departures:
        departure.wait()


def attend(recv, scale):
    sources, pieces, unused, size = recv.shape
    rows = pieces * PIECE
    total = sources * rows
    return pl.pallas_call(
        functools.partial(attend_kernel, scale),
        in_specs=[pl.BlockSpec(memory_space=pltpu.VMEM)],
        out_specs=pl.BlockSpec(memory_space=pltpu.HBM),
        out_shape=pltpu.HBM((sources, rows, size), jnp.bfloat16),
        scratch_shapes=[
            pltpu.VMEM((sources, rows, size), jnp.bfloat16),
            pltpu.SemaphoreType.DMA((total // 128,)),
        ],
        compiler_params=params(),
        cost_estimate=pl.CostEstimate(
            flops=4 * total * total * size, bytes_accessed=8 * total * size,
            transcendentals=total * total,
        ),
        name="attend",
    )(recv)


def attend_band_kernel(query_rows, scale, query_ref, recv_ref, out_ref):
    sources, both, size = recv_ref.shape
    rows = both // 2
    group = 256 // query_rows
    factor = scale * LOG2E
    for first in range(0, sources, group):
        queries = query_ref[first : first + group].reshape(group * query_rows, size)

        def advance(step, state):
            top, total, summed = state
            at = pl.ds(step * PIECE, PIECE)
            keys = recv_ref[at, :rows].reshape(PIECE * rows, size)
            values = recv_ref[at, rows:].reshape(PIECE * rows, size)
            scores = scores_of(queries, keys)
            new_top = jnp.maximum(top, jnp.max(scores, axis=1, keepdims=True))
            weights = jnp.exp2((scores - new_top) * factor)
            rescale = jnp.exp2((top - new_top) * factor)
            new_total = total * rescale + jnp.sum(weights, axis=1, keepdims=True)
            new_summed = summed * rescale + jnp.dot(
                weights.astype(jnp.bfloat16), values, preferred_element_type=jnp.float32
            )
            return new_top, new_total, new_summed

        start = (
            jnp.full((group * query_rows, 1), LOWEST, jnp.float32),
            jnp.zeros((group * query_rows, 1), jnp.float32),
            jnp.zeros((group * query_rows, size), jnp.float32),
        )
        state = lax.fori_loop(0, sources // PIECE, advance, start)
        result = (state[2] / state[1]).astype(jnp.bfloat16)
        out_ref[first : first + group] = result.reshape(group, query_rows, size)


def attend_band(queries, recv, scale):
    return pl.pallas_call(
        functools.partial(attend_band_kernel, queries.shape[1], scale),
        out_shape=jax.ShapeDtypeStruct(queries.shape, jnp.bfloat16),
        compiler_params=params(),
        name="attend_band",
    )(queries, recv)


def collect_kernel(by_head_ref, out_ref, turned, sems):
    departures = []
    for piece in range(by_head_ref.shape[1] // PIECE):
        at = pl.ds(piece * PIECE, PIECE)
        turned[at] = jnp.swapaxes(by_head_ref[:, at], 0, 1)
        departure = pltpu.make_async_copy(turned.at[at], out_ref.at[at], sems.at[piece])
        departure.start()
        departures.append(departure)
    for departure in departures:
        departure.wait()


def collect(by_head):
    heads, rows, size = by_head.shape
    return pl.pallas_call(
        collect_kernel,
        in_specs=[pl.BlockSpec(memory_space=pltpu.VMEM)],
        out_specs=pl.BlockSpec(memory_space=pltpu.HBM),
        out_shape=pltpu.HBM((rows, heads, size), by_head.dtype),
        scratch_shapes=[
            pltpu.VMEM((rows, heads, size), by_head.dtype),
            pltpu.SemaphoreType.DMA((rows // PIECE,)),
        ],
        compiler_params=params(),
        name="collect",
    )(by_head)


def video_kernel(
    scale, group, pairs_ref, counts_ref, where_ref, video_ref, own_ref, core_ref, chip_ref, out_ref,
    near_keys, near_values, keys_ref, values_ref, queries_ref, result_ref, turned, sems,
):
    heads, both, size = own_ref.shape
    rows = both // 2
    blocks, slots = pairs_ref.shape
    for ref, place in ((own_ref, rows), (core_ref, where_ref[1]), (chip_ref, where_ref[2])):
        at = pl.ds(pl.multiple_of(place, rows), rows)
        near_keys[:, at] = ref[:, :rows]
        near_values[:, at] = ref[:, rows:]
    values_ref[:, :, :, size:] = jnp.ones((blocks, heads, slots * ABLK, size), jnp.bfloat16)
    column = lax.broadcasted_iota(jnp.int32, (VBLK, slots * ABLK), 1)
    factor = scale * LOG2E

    def prepare(block):
        queries_ref[block] = jnp.swapaxes(video_ref[block * VBLK : (block + 1) * VBLK], 0, 1)
        for slot in range(slots):
            start = pl.multiple_of((pairs_ref[block, slot] - where_ref[0]) * ABLK, ABLK)
            here = slice(slot * ABLK, (slot + 1) * ABLK)
            keys_ref[block, :, here] = near_keys[:, pl.ds(start, ABLK)]
            values_ref[block, :, here, :size] = near_values[:, pl.ds(start, ABLK)]

    def departure(block):
        at = pl.ds(block * VBLK, VBLK)
        return pltpu.make_async_copy(turned.at[block], out_ref.at[at], sems.at[block])

    units = [(block, first) for block in range(blocks) for first in range(0, heads, group)]
    scores, weights = {}, {}
    for step in range(len(units) + 2):
        if step < len(units):
            block, first = units[step]
            if first == 0:
                prepare(block)
            live = column < counts_ref[block] * ABLK
            scores[step] = [
                jnp.where(live, scores_of(queries_ref[block, head], keys_ref[block, head]), LOWEST)
                for head in range(first, first + group)
            ]
        if 1 <= step <= len(units):
            now = jnp.stack(scores.pop(step - 1))
            top = jnp.max(now, axis=2, keepdims=True)
            weights[step - 1] = jnp.exp2((now - top) * factor).astype(jnp.bfloat16)
        if step >= 2:
            block, first = units[step - 2]
            now = weights.pop(step - 2)
            for i in range(group):
                summed = jnp.dot(
                    now[i], values_ref[block, first + i], preferred_element_type=jnp.float32
                )
                result_ref[block, first + i] = (summed[:, :size] / summed[:, size:]).astype(
                    jnp.bfloat16
                )
            if first + group == heads:
                turned[block] = jnp.swapaxes(result_ref[block], 0, 1)
                departure(block).start()
    for block in range(blocks):
        departure(block).wait()


def video(video_q, own, core, chip, pairs, counts, where, scale):
    total, heads, size = video_q.shape
    rows = own.shape[1] // 2
    blocks, slots = pairs.shape
    work = total * heads * slots * ABLK
    in_smem = pl.BlockSpec(memory_space=pltpu.SMEM)
    in_vmem = pl.BlockSpec(memory_space=pltpu.VMEM)
    return pl.pallas_call(
        functools.partial(video_kernel, scale, 4),
        in_specs=[in_smem] * 3 + [in_vmem] * 4,
        out_specs=pl.BlockSpec(memory_space=pltpu.HBM),
        out_shape=pltpu.HBM(video_q.shape, jnp.bfloat16),
        scratch_shapes=[
            pltpu.VMEM((heads, 3 * rows, size), jnp.bfloat16),
            pltpu.VMEM((heads, 3 * rows, size), jnp.bfloat16),
            pltpu.VMEM((blocks, heads, slots * ABLK, size), jnp.bfloat16),
            pltpu.VMEM((blocks, heads, slots * ABLK, 2 * size), jnp.bfloat16),
            pltpu.VMEM((blocks, heads, VBLK, size), jnp.bfloat16),
            pltpu.VMEM((blocks, heads, VBLK, size), jnp.bfloat16),
            pltpu.VMEM((blocks, VBLK, heads, size), jnp.bfloat16),
            pltpu.SemaphoreType.DMA((blocks,)),
        ],
        compiler_params=params(),
        cost_estimate=pl.CostEstimate(
            flops=4 * work * size, bytes_accessed=32 * total * heads * size, transcendentals=work
        ),
        name="video",
    )(pairs, counts, where, video_q, own, core, chip)


def local(audio_qkv, video_q, pairs, counts):
    devices = lax.axis_size("seq")
    rows, unused, heads, size = audio_qkv.shape
    bands = devices // heads
    band_rows = rows // bands
    scale = size ** (-0.5)
    send, kv = arrange(audio_qkv)
    core_pairs = [(i, i ^ 1) for i in range(devices)]
    chip_pairs = [(i, ((i + 1) ^ 1) - 1) for i in range(1, devices - 1)]

    chip = lax.ppermute(kv, "seq", chip_pairs)

    order = [(devices - 1 - devices // 4 - p) % devices for p in range(devices)]

    def exchange(value):
        return lax.all_to_all(
            value, "seq", split_axis=0, concat_axis=0, tiled=True, axis_index_groups=[order]
        )

    core = lax.ppermute(kv, "seq", core_pairs)
    me = lax.axis_index("seq")
    odd = me & 1
    where = jnp.stack([(me - 1) * (rows // ABLK), 2 * (1 - odd) * rows, 2 * odd * rows])
    video_cross = video(
        video_q, kv, core, chip, pairs, counts, where.astype(jnp.int32), scale
    )
    if bands == 1:
        head_out = attend(exchange(send), scale)
    else:
        queries = exchange(send[:, :, :PIECE].reshape(devices, band_rows, size))
        spread = jnp.broadcast_to(kv[:, None], (heads, bands, 2 * rows, size))
        recv = exchange(spread.reshape(devices, 2 * rows, size))
        head_out = attend_band(queries, recv, scale)
    returned, video_cross = lax.optimization_barrier((exchange(head_out), video_cross))
    audio_attn = collect(returned.reshape(heads, rows, size))
    return audio_attn, video_cross


def solution(mesh):
    in_specs = (
        P(("groups", "seq"), None, None, None),
        P(("groups", "seq"), None, None),
        P(("groups", "seq"), None),
        P(("groups", "seq")),
    )
    out_specs = (P(("groups", "seq"), None, None), P(("groups", "seq"), None, None))
    return jax.shard_map(local, mesh=mesh, in_specs=in_specs, out_specs=out_specs, check_vma=False)
```

```python
import functools

import jax
import jax.numpy as jnp
from jax import lax
from jax.experimental import pallas as pl
from jax.experimental.pallas import tpu as pltpu
from jax.sharding import PartitionSpec as P

ABLK = 32
VBLK = 128
LOG2E = 1.4426950408889634
LOWEST = -1e30
VMEM_LIMIT = 48 * 1024 * 1024


def params():
    return pltpu.CompilerParams(vmem_limit_bytes=VMEM_LIMIT)


PIECE = 16


def arrange_kernel(pieces, qkv_ref, send_ref, kv_ref, came, turned, in_sems, out_sems):
    rows = pieces * PIECE
    arrivals = [
        pltpu.make_async_copy(
            qkv_ref.at[pl.ds(piece * PIECE, PIECE)], came.at[piece], in_sems.at[piece]
        )
        for piece in range(pieces)
    ]
    for arrival in arrivals:
        arrival.start()
    departures = []
    for piece, arrival in enumerate(arrivals):
        arrival.wait()
        for part in range(3):
            by_head = jnp.swapaxes(came[piece, :, part], 0, 1)
            turned[piece, :, part * PIECE : (part + 1) * PIECE] = by_head
            if part:
                at = (part - 1) * rows + piece * PIECE
                kv_ref[:, at : at + PIECE] = by_head
        departure = pltpu.make_async_copy(
            turned.at[piece], send_ref.at[:, piece], out_sems.at[piece]
        )
        departure.start()
        departures.append(departure)
    for departure in departures:
        departure.wait()


def arrange(audio_qkv):
    rows, parts, heads, size = audio_qkv.shape
    dtype = audio_qkv.dtype
    pieces = rows // PIECE
    return pl.pallas_call(
        functools.partial(arrange_kernel, pieces),
        in_specs=[pl.BlockSpec(memory_space=pltpu.HBM)],
        out_specs=(
            pl.BlockSpec(memory_space=pltpu.HBM),
            pl.BlockSpec(memory_space=pltpu.VMEM),
        ),
        out_shape=(
            pltpu.HBM((heads, pieces, parts * PIECE, size), dtype),
            jax.ShapeDtypeStruct((heads, 2 * rows, size), dtype),
        ),
        scratch_shapes=[
            pltpu.VMEM((pieces, PIECE, parts, heads, size), dtype),
            pltpu.VMEM((pieces, heads, parts * PIECE, size), dtype),
            pltpu.SemaphoreType.DMA((pieces,)),
            pltpu.SemaphoreType.DMA((pieces,)),
        ],
        compiler_params=params(),
        name="arrange",
    )(pltpu.with_memory_space_constraint(audio_qkv, pltpu.HBM))


def scores_of(queries, keys):
    return lax.dot_general(
        queries, keys, (((1,), (1,)), ((), ())), preferred_element_type=jnp.float32
    )


def attend_kernel(scale, recv_ref, out_ref, held, sems):
    sources, pieces, unused, size = recv_ref.shape
    total = sources * pieces * PIECE
    chunk = total // sems.shape[0]
    group = chunk // (pieces * PIECE)
    factor = scale * LOG2E
    keys = recv_ref[:, :, PIECE : 2 * PIECE].reshape(total, size)
    values = recv_ref[:, :, 2 * PIECE :].reshape(total, size)
    chunks = total // chunk
    scores, weights, sums, departures = {}, {}, {}, []
    for step in range(chunks + 2):
        if step < chunks:
            first = step * group
            queries = recv_ref[first : first + group, :, :PIECE].reshape(chunk, size)
            scores[step] = scores_of(queries, keys)
        if 0 <= step - 1 < chunks:
            now = scores.pop(step - 1)
            top = jnp.max(now, axis=1, keepdims=True)
            exact = jnp.exp2((now - top) * factor)
            sums[step - 1] = jnp.sum(exact, axis=1, keepdims=True)
            weights[step - 1] = exact.astype(jnp.bfloat16)
        if step >= 2:
            summed = jnp.dot(
                weights.pop(step - 2), values, preferred_element_type=jnp.float32
            )
            result = (summed / sums.pop(step - 2)).astype(jnp.bfloat16)
            at = (step - 2) * group
            held[at : at + group] = result.reshape(group, pieces * PIECE, size)
            departure = pltpu.make_async_copy(
                held.at[pl.ds(at, group)], out_ref.at[pl.ds(at, group)], sems.at[step - 2]
            )
            departure.start()
            departures.append(departure)
    for departure in departures:
        departure.wait()


def attend(recv, scale):
    sources, pieces, unused, size = recv.shape
    rows = pieces * PIECE
    total = sources * rows
    return pl.pallas_call(
        functools.partial(attend_kernel, scale),
        in_specs=[pl.BlockSpec(memory_space=pltpu.VMEM)],
        out_specs=pl.BlockSpec(memory_space=pltpu.HBM),
        out_shape=pltpu.HBM((sources, rows, size), jnp.bfloat16),
        scratch_shapes=[
            pltpu.VMEM((sources, rows, size), jnp.bfloat16),
            pltpu.SemaphoreType.DMA((total // 128,)),
        ],
        compiler_params=params(),
        cost_estimate=pl.CostEstimate(
            flops=4 * total * total * size, bytes_accessed=8 * total * size,
            transcendentals=total * total,
        ),
        name="attend",
    )(recv)


def attend_band_kernel(query_rows, scale, query_ref, recv_ref, out_ref):
    sources, both, size = recv_ref.shape
    rows = both // 2
    group = 256 // query_rows
    factor = scale * LOG2E
    for first in range(0, sources, group):
        queries = query_ref[first : first + group].reshape(group * query_rows, size)

        def advance(step, state):
            top, total, summed = state
            at = pl.ds(step * PIECE, PIECE)
            keys = recv_ref[at, :rows].reshape(PIECE * rows, size)
            values = recv_ref[at, rows:].reshape(PIECE * rows, size)
            scores = scores_of(queries, keys)
            new_top = jnp.maximum(top, jnp.max(scores, axis=1, keepdims=True))
            weights = jnp.exp2((scores - new_top) * factor)
            rescale = jnp.exp2((top - new_top) * factor)
            new_total = total * rescale + jnp.sum(weights, axis=1, keepdims=True)
            new_summed = summed * rescale + jnp.dot(
                weights.astype(jnp.bfloat16), values, preferred_element_type=jnp.float32
            )
            return new_top, new_total, new_summed

        start = (
            jnp.full((group * query_rows, 1), LOWEST, jnp.float32),
            jnp.zeros((group * query_rows, 1), jnp.float32),
            jnp.zeros((group * query_rows, size), jnp.float32),
        )
        state = lax.fori_loop(0, sources // PIECE, advance, start)
        result = (state[2] / state[1]).astype(jnp.bfloat16)
        out_ref[first : first + group] = result.reshape(group, query_rows, size)


def attend_band(queries, recv, scale):
    return pl.pallas_call(
        functools.partial(attend_band_kernel, queries.shape[1], scale),
        out_shape=jax.ShapeDtypeStruct(queries.shape, jnp.bfloat16),
        compiler_params=params(),
        name="attend_band",
    )(queries, recv)


def collect_kernel(by_head_ref, out_ref, turned, sems):
    departures = []
    for piece in range(by_head_ref.shape[1] // PIECE):
        at = pl.ds(piece * PIECE, PIECE)
        turned[at] = jnp.swapaxes(by_head_ref[:, at], 0, 1)
        departure = pltpu.make_async_copy(turned.at[at], out_ref.at[at], sems.at[piece])
        departure.start()
        departures.append(departure)
    for departure in departures:
        departure.wait()


def collect(by_head):
    heads, rows, size = by_head.shape
    return pl.pallas_call(
        collect_kernel,
        in_specs=[pl.BlockSpec(memory_space=pltpu.VMEM)],
        out_specs=pl.BlockSpec(memory_space=pltpu.HBM),
        out_shape=pltpu.HBM((rows, heads, size), by_head.dtype),
        scratch_shapes=[
            pltpu.VMEM((rows, heads, size), by_head.dtype),
            pltpu.SemaphoreType.DMA((rows // PIECE,)),
        ],
        compiler_params=params(),
        name="collect",
    )(by_head)


def video_kernel(
    scale, group, pairs_ref, counts_ref, where_ref, video_ref, own_ref, core_ref, chip_ref, out_ref,
    near_keys, near_values, keys_ref, values_ref, queries_ref, result_ref, turned, sems,
):
    heads, both, size = own_ref.shape
    rows = both // 2
    blocks, slots = pairs_ref.shape
    for ref, place in ((own_ref, rows), (core_ref, where_ref[1]), (chip_ref, where_ref[2])):
        at = pl.ds(pl.multiple_of(place, rows), rows)
        near_keys[:, at] = ref[:, :rows]
        near_values[:, at] = ref[:, rows:]
    values_ref[:, :, :, size:] = jnp.ones((blocks, heads, slots * ABLK, size), jnp.bfloat16)
    column = lax.broadcasted_iota(jnp.int32, (VBLK, slots * ABLK), 1)
    factor = scale * LOG2E

    def prepare(block):
        queries_ref[block] = jnp.swapaxes(video_ref[block * VBLK : (block + 1) * VBLK], 0, 1)
        for slot in range(slots):
            start = pl.multiple_of((pairs_ref[block, slot] - where_ref[0]) * ABLK, ABLK)
            here = slice(slot * ABLK, (slot + 1) * ABLK)
            keys_ref[block, :, here] = near_keys[:, pl.ds(start, ABLK)]
            values_ref[block, :, here, :size] = near_values[:, pl.ds(start, ABLK)]

    def departure(block):
        at = pl.ds(block * VBLK, VBLK)
        return pltpu.make_async_copy(turned.at[block], out_ref.at[at], sems.at[block])

    units = [(block, first) for block in range(blocks) for first in range(0, heads, group)]
    scores, weights = {}, {}
    for step in range(len(units) + 2):
        if step < len(units):
            block, first = units[step]
            if first == 0:
                prepare(block)
            live = column < counts_ref[block] * ABLK
            scores[step] = [
                jnp.where(live, scores_of(queries_ref[block, head], keys_ref[block, head]), LOWEST)
                for head in range(first, first + group)
            ]
        if 1 <= step <= len(units):
            now = jnp.stack(scores.pop(step - 1))
            top = jnp.max(now, axis=2, keepdims=True)
            weights[step - 1] = jnp.exp2((now - top) * factor).astype(jnp.bfloat16)
        if step >= 2:
            block, first = units[step - 2]
            now = weights.pop(step - 2)
            for i in range(group):
                summed = jnp.dot(
                    now[i], values_ref[block, first + i], preferred_element_type=jnp.float32
                )
                result_ref[block, first + i] = (summed[:, :size] / summed[:, size:]).astype(
                    jnp.bfloat16
                )
            if first + group == heads:
                turned[block] = jnp.swapaxes(result_ref[block], 0, 1)
                departure(block).start()
    for block in range(blocks):
        departure(block).wait()


def video(video_q, own, core, chip, pairs, counts, where, scale):
    total, heads, size = video_q.shape
    rows = own.shape[1] // 2
    blocks, slots = pairs.shape
    work = total * heads * slots * ABLK
    in_smem = pl.BlockSpec(memory_space=pltpu.SMEM)
    in_vmem = pl.BlockSpec(memory_space=pltpu.VMEM)
    return pl.pallas_call(
        functools.partial(video_kernel, scale, 4),
        in_specs=[in_smem] * 3 + [in_vmem] * 4,
        out_specs=pl.BlockSpec(memory_space=pltpu.HBM),
        out_shape=pltpu.HBM(video_q.shape, jnp.bfloat16),
        scratch_shapes=[
            pltpu.VMEM((heads, 3 * rows, size), jnp.bfloat16),
            pltpu.VMEM((heads, 3 * rows, size), jnp.bfloat16),
            pltpu.VMEM((blocks, heads, slots * ABLK, size), jnp.bfloat16),
            pltpu.VMEM((blocks, heads, slots * ABLK, 2 * size), jnp.bfloat16),
            pltpu.VMEM((blocks, heads, VBLK, size), jnp.bfloat16),
            pltpu.VMEM((blocks, heads, VBLK, size), jnp.bfloat16),
            pltpu.VMEM((blocks, VBLK, heads, size), jnp.bfloat16),
            pltpu.SemaphoreType.DMA((blocks,)),
        ],
        compiler_params=params(),
        cost_estimate=pl.CostEstimate(
            flops=4 * work * size, bytes_accessed=32 * total * heads * size, transcendentals=work
        ),
        name="video",
    )(pairs, counts, where, video_q, own, core, chip)


def local(audio_qkv, video_q, pairs, counts):
    devices = lax.axis_size("seq")
    rows, unused, heads, size = audio_qkv.shape
    bands = devices // heads
    band_rows = rows // bands
    scale = size ** (-0.5)
    send, kv = arrange(audio_qkv)
    core_pairs = [(i, i ^ 1) for i in range(devices)]
    chip_pairs = [(i, ((i + 1) ^ 1) - 1) for i in range(1, devices - 1)]

    chip = lax.ppermute(kv, "seq", chip_pairs)

    order = [(devices - 1 - devices // 2 - p) % devices for p in range(devices)]

    def exchange(value):
        return lax.all_to_all(
            value, "seq", split_axis=0, concat_axis=0, tiled=True, axis_index_groups=[order]
        )

    core = lax.ppermute(kv, "seq", core_pairs)
    me = lax.axis_index("seq")
    odd = me & 1
    where = jnp.stack([(me - 1) * (rows // ABLK), 2 * (1 - odd) * rows, 2 * odd * rows])
    video_cross = video(
        video_q, kv, core, chip, pairs, counts, where.astype(jnp.int32), scale
    )
    if bands == 1:
        head_out = attend(exchange(send), scale)
    else:
        queries = exchange(send[:, :, :PIECE].reshape(devices, band_rows, size))
        spread = jnp.broadcast_to(kv[:, None], (heads, bands, 2 * rows, size))
        recv = exchange(spread.reshape(devices, 2 * rows, size))
        head_out = attend_band(queries, recv, scale)
    returned, video_cross = lax.optimization_barrier((exchange(head_out), video_cross))
    audio_attn = collect(returned.reshape(heads, rows, size))
    return audio_attn, video_cross


def solution(mesh):
    in_specs = (
        P(("groups", "seq"), None, None, None),
        P(("groups", "seq"), None, None),
        P(("groups", "seq"), None),
        P(("groups", "seq")),
    )
    out_specs = (P(("groups", "seq"), None, None), P(("groups", "seq"), None, None))
    return jax.shard_map(local, mesh=mesh, in_specs=in_specs, out_specs=out_specs, check_vma=False)
```

```python
import functools

import jax
import jax.numpy as jnp
from jax import lax
from jax.experimental import pallas as pl
from jax.experimental.pallas import tpu as pltpu
from jax.sharding import PartitionSpec as P

ABLK = 32
VBLK = 128
LOG2E = 1.4426950408889634
LOWEST = -1e30
VMEM_LIMIT = 48 * 1024 * 1024


def params():
    return pltpu.CompilerParams(vmem_limit_bytes=VMEM_LIMIT)


PIECE = 16


def arrange_kernel(pieces, qkv_ref, send_ref, kv_ref, came, turned, in_sems, out_sems):
    rows = pieces * PIECE
    arrivals = [
        pltpu.make_async_copy(
            qkv_ref.at[pl.ds(piece * PIECE, PIECE)], came.at[piece], in_sems.at[piece]
        )
        for piece in range(pieces)
    ]
    for arrival in arrivals:
        arrival.start()
    departures = []
    for piece, arrival in enumerate(arrivals):
        arrival.wait()
        for part in range(3):
            by_head = jnp.swapaxes(came[piece, :, part], 0, 1)
            turned[piece, :, part * PIECE : (part + 1) * PIECE] = by_head
            if part:
                at = (part - 1) * rows + piece * PIECE
                kv_ref[:, at : at + PIECE] = by_head
        departure = pltpu.make_async_copy(
            turned.at[piece], send_ref.at[:, piece], out_sems.at[piece]
        )
        departure.start()
        departures.append(departure)
    for departure in departures:
        departure.wait()


def arrange(audio_qkv):
    rows, parts, heads, size = audio_qkv.shape
    dtype = audio_qkv.dtype
    pieces = rows // PIECE
    return pl.pallas_call(
        functools.partial(arrange_kernel, pieces),
        in_specs=[pl.BlockSpec(memory_space=pltpu.HBM)],
        out_specs=(
            pl.BlockSpec(memory_space=pltpu.HBM),
            pl.BlockSpec(memory_space=pltpu.VMEM),
        ),
        out_shape=(
            pltpu.HBM((heads, pieces, parts * PIECE, size), dtype),
            jax.ShapeDtypeStruct((heads, 2 * rows, size), dtype),
        ),
        scratch_shapes=[
            pltpu.VMEM((pieces, PIECE, parts, heads, size), dtype),
            pltpu.VMEM((pieces, heads, parts * PIECE, size), dtype),
            pltpu.SemaphoreType.DMA((pieces,)),
            pltpu.SemaphoreType.DMA((pieces,)),
        ],
        compiler_params=params(),
        name="arrange",
    )(pltpu.with_memory_space_constraint(audio_qkv, pltpu.HBM))


def scores_of(queries, keys):
    return lax.dot_general(
        queries, keys, (((1,), (1,)), ((), ())), preferred_element_type=jnp.float32
    )


def attend_kernel(scale, recv_ref, out_ref, held, sems):
    sources, pieces, unused, size = recv_ref.shape
    total = sources * pieces * PIECE
    chunk = total // sems.shape[0]
    group = chunk // (pieces * PIECE)
    factor = scale * LOG2E
    keys = recv_ref[:, :, PIECE : 2 * PIECE].reshape(total, size)
    values = recv_ref[:, :, 2 * PIECE :].reshape(total, size)
    chunks = total // chunk
    scores, weights, sums, departures = {}, {}, {}, []
    for step in range(chunks + 2):
        if step < chunks:
            first = step * group
            queries = recv_ref[first : first + group, :, :PIECE].reshape(chunk, size)
            scores[step] = scores_of(queries, keys)
        if 0 <= step - 1 < chunks:
            now = scores.pop(step - 1)
            top = jnp.max(now, axis=1, keepdims=True)
            exact = jnp.exp2((now - top) * factor)
            sums[step - 1] = jnp.sum(exact, axis=1, keepdims=True)
            weights[step - 1] = exact.astype(jnp.bfloat16)
        if step >= 2:
            summed = jnp.dot(
                weights.pop(step - 2), values, preferred_element_type=jnp.float32
            )
            result = (summed / sums.pop(step - 2)).astype(jnp.bfloat16)
            at = (step - 2) * group
            held[at : at + group] = result.reshape(group, pieces * PIECE, size)
            departure = pltpu.make_async_copy(
                held.at[pl.ds(at, group)], out_ref.at[pl.ds(at, group)], sems.at[step - 2]
            )
            departure.start()
            departures.append(departure)
    for departure in departures:
        departure.wait()


def attend(recv, scale):
    sources, pieces, unused, size = recv.shape
    rows = pieces * PIECE
    total = sources * rows
    return pl.pallas_call(
        functools.partial(attend_kernel, scale),
        in_specs=[pl.BlockSpec(memory_space=pltpu.VMEM)],
        out_specs=pl.BlockSpec(memory_space=pltpu.HBM),
        out_shape=pltpu.HBM((sources, rows, size), jnp.bfloat16),
        scratch_shapes=[
            pltpu.VMEM((sources, rows, size), jnp.bfloat16),
            pltpu.SemaphoreType.DMA((total // 128,)),
        ],
        compiler_params=params(),
        cost_estimate=pl.CostEstimate(
            flops=4 * total * total * size, bytes_accessed=8 * total * size,
            transcendentals=total * total,
        ),
        name="attend",
    )(recv)


def attend_band_kernel(query_rows, scale, query_ref, recv_ref, out_ref):
    sources, both, size = recv_ref.shape
    rows = both // 2
    group = 256 // query_rows
    factor = scale * LOG2E
    for first in range(0, sources, group):
        queries = query_ref[first : first + group].reshape(group * query_rows, size)

        def advance(step, state):
            top, total, summed = state
            at = pl.ds(step * PIECE, PIECE)
            keys = recv_ref[at, :rows].reshape(PIECE * rows, size)
            values = recv_ref[at, rows:].reshape(PIECE * rows, size)
            scores = scores_of(queries, keys)
            new_top = jnp.maximum(top, jnp.max(scores, axis=1, keepdims=True))
            weights = jnp.exp2((scores - new_top) * factor)
            rescale = jnp.exp2((top - new_top) * factor)
            new_total = total * rescale + jnp.sum(weights, axis=1, keepdims=True)
            new_summed = summed * rescale + jnp.dot(
                weights.astype(jnp.bfloat16), values, preferred_element_type=jnp.float32
            )
            return new_top, new_total, new_summed

        start = (
            jnp.full((group * query_rows, 1), LOWEST, jnp.float32),
            jnp.zeros((group * query_rows, 1), jnp.float32),
            jnp.zeros((group * query_rows, size), jnp.float32),
        )
        state = lax.fori_loop(0, sources // PIECE, advance, start)
        result = (state[2] / state[1]).astype(jnp.bfloat16)
        out_ref[first : first + group] = result.reshape(group, query_rows, size)


def attend_band(queries, recv, scale):
    return pl.pallas_call(
        functools.partial(attend_band_kernel, queries.shape[1], scale),
        out_shape=jax.ShapeDtypeStruct(queries.shape, jnp.bfloat16),
        compiler_params=params(),
        name="attend_band",
    )(queries, recv)


def collect_kernel(by_head_ref, out_ref, turned, sems):
    departures = []
    for piece in range(by_head_ref.shape[1] // PIECE):
        at = pl.ds(piece * PIECE, PIECE)
        turned[at] = jnp.swapaxes(by_head_ref[:, at], 0, 1)
        departure = pltpu.make_async_copy(turned.at[at], out_ref.at[at], sems.at[piece])
        departure.start()
        departures.append(departure)
    for departure in departures:
        departure.wait()


def collect(by_head):
    heads, rows, size = by_head.shape
    return pl.pallas_call(
        collect_kernel,
        in_specs=[pl.BlockSpec(memory_space=pltpu.VMEM)],
        out_specs=pl.BlockSpec(memory_space=pltpu.HBM),
        out_shape=pltpu.HBM((rows, heads, size), by_head.dtype),
        scratch_shapes=[
            pltpu.VMEM((rows, heads, size), by_head.dtype),
            pltpu.SemaphoreType.DMA((rows // PIECE,)),
        ],
        compiler_params=params(),
        name="collect",
    )(by_head)


def video_kernel(
    scale, group, pairs_ref, counts_ref, where_ref, video_ref, own_ref, core_ref, chip_ref, out_ref,
    near_keys, near_values, keys_ref, values_ref, queries_ref, result_ref, turned, sems,
):
    heads, both, size = own_ref.shape
    rows = both // 2
    blocks, slots = pairs_ref.shape
    for ref, place in ((own_ref, rows), (core_ref, where_ref[1]), (chip_ref, where_ref[2])):
        at = pl.ds(pl.multiple_of(place, rows), rows)
        near_keys[:, at] = ref[:, :rows]
        near_values[:, at] = ref[:, rows:]
    values_ref[:, :, :, size:] = jnp.ones((blocks, heads, slots * ABLK, size), jnp.bfloat16)
    column = lax.broadcasted_iota(jnp.int32, (VBLK, slots * ABLK), 1)
    factor = scale * LOG2E

    def prepare(block):
        queries_ref[block] = jnp.swapaxes(video_ref[block * VBLK : (block + 1) * VBLK], 0, 1)
        for slot in range(slots):
            start = pl.multiple_of((pairs_ref[block, slot] - where_ref[0]) * ABLK, ABLK)
            here = slice(slot * ABLK, (slot + 1) * ABLK)
            keys_ref[block, :, here] = near_keys[:, pl.ds(start, ABLK)]
            values_ref[block, :, here, :size] = near_values[:, pl.ds(start, ABLK)]

    def departure(block):
        at = pl.ds(block * VBLK, VBLK)
        return pltpu.make_async_copy(turned.at[block], out_ref.at[at], sems.at[block])

    units = [(block, first) for block in range(blocks) for first in range(0, heads, group)]
    scores, weights = {}, {}
    for step in range(len(units) + 2):
        if step < len(units):
            block, first = units[step]
            if first == 0:
                prepare(block)
            live = column < counts_ref[block] * ABLK
            scores[step] = [
                jnp.where(live, scores_of(queries_ref[block, head], keys_ref[block, head]), LOWEST)
                for head in range(first, first + group)
            ]
        if 1 <= step <= len(units):
            now = jnp.stack(scores.pop(step - 1))
            top = jnp.max(now, axis=2, keepdims=True)
            weights[step - 1] = jnp.exp2((now - top) * factor).astype(jnp.bfloat16)
        if step >= 2:
            block, first = units[step - 2]
            now = weights.pop(step - 2)
            for i in range(group):
                summed = jnp.dot(
                    now[i], values_ref[block, first + i], preferred_element_type=jnp.float32
                )
                result_ref[block, first + i] = (summed[:, :size] / summed[:, size:]).astype(
                    jnp.bfloat16
                )
            if first + group == heads:
                turned[block] = jnp.swapaxes(result_ref[block], 0, 1)
                departure(block).start()
    for block in range(blocks):
        departure(block).wait()


def video(video_q, own, core, chip, pairs, counts, where, scale):
    total, heads, size = video_q.shape
    rows = own.shape[1] // 2
    blocks, slots = pairs.shape
    work = total * heads * slots * ABLK
    in_smem = pl.BlockSpec(memory_space=pltpu.SMEM)
    in_vmem = pl.BlockSpec(memory_space=pltpu.VMEM)
    return pl.pallas_call(
        functools.partial(video_kernel, scale, 4),
        in_specs=[in_smem] * 3 + [in_vmem] * 4,
        out_specs=pl.BlockSpec(memory_space=pltpu.HBM),
        out_shape=pltpu.HBM(video_q.shape, jnp.bfloat16),
        scratch_shapes=[
            pltpu.VMEM((heads, 3 * rows, size), jnp.bfloat16),
            pltpu.VMEM((heads, 3 * rows, size), jnp.bfloat16),
            pltpu.VMEM((blocks, heads, slots * ABLK, size), jnp.bfloat16),
            pltpu.VMEM((blocks, heads, slots * ABLK, 2 * size), jnp.bfloat16),
            pltpu.VMEM((blocks, heads, VBLK, size), jnp.bfloat16),
            pltpu.VMEM((blocks, heads, VBLK, size), jnp.bfloat16),
            pltpu.VMEM((blocks, VBLK, heads, size), jnp.bfloat16),
            pltpu.SemaphoreType.DMA((blocks,)),
        ],
        compiler_params=params(),
        cost_estimate=pl.CostEstimate(
            flops=4 * work * size, bytes_accessed=32 * total * heads * size, transcendentals=work
        ),
        name="video",
    )(pairs, counts, where, video_q, own, core, chip)


def local(audio_qkv, video_q, pairs, counts):
    devices = lax.axis_size("seq")
    rows, unused, heads, size = audio_qkv.shape
    bands = devices // heads
    band_rows = rows // bands
    scale = size ** (-0.5)
    send, kv = arrange(audio_qkv)
    core_pairs = [(i, i ^ 1) for i in range(devices)]
    chip_pairs = [(i, ((i + 1) ^ 1) - 1) for i in range(1, devices - 1)]

    chip = lax.ppermute(kv, "seq", chip_pairs)

    order = [(devices // 2 + p) % devices for p in range(devices)]

    def exchange(value):
        return lax.all_to_all(
            value, "seq", split_axis=0, concat_axis=0, tiled=True, axis_index_groups=[order]
        )

    core = lax.ppermute(kv, "seq", core_pairs)
    me = lax.axis_index("seq")
    odd = me & 1
    where = jnp.stack([(me - 1) * (rows // ABLK), 2 * (1 - odd) * rows, 2 * odd * rows])
    video_cross = video(
        video_q, kv, core, chip, pairs, counts, where.astype(jnp.int32), scale
    )
    if bands == 1:
        head_out = attend(exchange(send), scale)
    else:
        queries = exchange(send[:, :, :PIECE].reshape(devices, band_rows, size))
        spread = jnp.broadcast_to(kv[:, None], (heads, bands, 2 * rows, size))
        recv = exchange(spread.reshape(devices, 2 * rows, size))
        head_out = attend_band(queries, recv, scale)
    returned, video_cross = lax.optimization_barrier((exchange(head_out), video_cross))
    audio_attn = collect(returned.reshape(heads, rows, size))
    return audio_attn, video_cross


def solution(mesh):
    in_specs = (
        P(("groups", "seq"), None, None, None),
        P(("groups", "seq"), None, None),
        P(("groups", "seq"), None),
        P(("groups", "seq")),
    )
    out_specs = (P(("groups", "seq"), None, None), P(("groups", "seq"), None, None))
    return jax.shard_map(local, mesh=mesh, in_specs=in_specs, out_specs=out_specs, check_vma=False)
```

```python
import functools

import jax
import jax.numpy as jnp
from jax import lax
from jax.experimental import pallas as pl
from jax.experimental.pallas import tpu as pltpu
from jax.sharding import PartitionSpec as P

ABLK = 32
VBLK = 128
LOG2E = 1.4426950408889634
LOWEST = -1e30
VMEM_LIMIT = 48 * 1024 * 1024


def params():
    return pltpu.CompilerParams(vmem_limit_bytes=VMEM_LIMIT)


PIECE = 16


def arrange_kernel(pieces, qkv_ref, send_ref, kv_ref, came, turned, in_sems, out_sems):
    rows = pieces * PIECE
    arrivals = [
        pltpu.make_async_copy(
            qkv_ref.at[pl.ds(piece * PIECE, PIECE)], came.at[piece], in_sems.at[piece]
        )
        for piece in range(pieces)
    ]
    for arrival in arrivals:
        arrival.start()
    departures = []
    for piece, arrival in enumerate(arrivals):
        arrival.wait()
        for part in range(3):
            by_head = jnp.swapaxes(came[piece, :, part], 0, 1)
            turned[piece, :, part * PIECE : (part + 1) * PIECE] = by_head
            if part:
                at = (part - 1) * rows + piece * PIECE
                kv_ref[:, at : at + PIECE] = by_head
        departure = pltpu.make_async_copy(
            turned.at[piece], send_ref.at[:, piece], out_sems.at[piece]
        )
        departure.start()
        departures.append(departure)
    for departure in departures:
        departure.wait()


def arrange(audio_qkv):
    rows, parts, heads, size = audio_qkv.shape
    dtype = audio_qkv.dtype
    pieces = rows // PIECE
    return pl.pallas_call(
        functools.partial(arrange_kernel, pieces),
        in_specs=[pl.BlockSpec(memory_space=pltpu.HBM)],
        out_specs=(
            pl.BlockSpec(memory_space=pltpu.HBM),
            pl.BlockSpec(memory_space=pltpu.VMEM),
        ),
        out_shape=(
            pltpu.HBM((heads, pieces, parts * PIECE, size), dtype),
            jax.ShapeDtypeStruct((heads, 2 * rows, size), dtype),
        ),
        scratch_shapes=[
            pltpu.VMEM((pieces, PIECE, parts, heads, size), dtype),
            pltpu.VMEM((pieces, heads, parts * PIECE, size), dtype),
            pltpu.SemaphoreType.DMA((pieces,)),
            pltpu.SemaphoreType.DMA((pieces,)),
        ],
        compiler_params=params(),
        name="arrange",
    )(pltpu.with_memory_space_constraint(audio_qkv, pltpu.HBM))


def scores_of(queries, keys):
    return lax.dot_general(
        queries, keys, (((1,), (1,)), ((), ())), preferred_element_type=jnp.float32
    )


def attend_kernel(scale, recv_ref, out_ref, held, sems):
    sources, pieces, unused, size = recv_ref.shape
    total = sources * pieces * PIECE
    chunk = total // sems.shape[0]
    group = chunk // (pieces * PIECE)
    factor = scale * LOG2E
    keys = recv_ref[:, :, PIECE : 2 * PIECE].reshape(total, size)
    values = recv_ref[:, :, 2 * PIECE :].reshape(total, size)
    chunks = total // chunk
    scores, weights, sums, departures = {}, {}, {}, []
    for step in range(chunks + 2):
        if step < chunks:
            first = step * group
            queries = recv_ref[first : first + group, :, :PIECE].reshape(chunk, size)
            scores[step] = scores_of(queries, keys)
        if 0 <= step - 1 < chunks:
            now = scores.pop(step - 1)
            top = jnp.max(now, axis=1, keepdims=True)
            exact = jnp.exp2((now - top) * factor)
            sums[step - 1] = jnp.sum(exact, axis=1, keepdims=True)
            weights[step - 1] = exact.astype(jnp.bfloat16)
        if step >= 2:
            summed = jnp.dot(
                weights.pop(step - 2), values, preferred_element_type=jnp.float32
            )
            result = (summed / sums.pop(step - 2)).astype(jnp.bfloat16)
            at = (step - 2) * group
            held[at : at + group] = result.reshape(group, pieces * PIECE, size)
            departure = pltpu.make_async_copy(
                held.at[pl.ds(at, group)], out_ref.at[pl.ds(at, group)], sems.at[step - 2]
            )
            departure.start()
            departures.append(departure)
    for departure in departures:
        departure.wait()


def attend(recv, scale):
    sources, pieces, unused, size = recv.shape
    rows = pieces * PIECE
    total = sources * rows
    return pl.pallas_call(
        functools.partial(attend_kernel, scale),
        in_specs=[pl.BlockSpec(memory_space=pltpu.VMEM)],
        out_specs=pl.BlockSpec(memory_space=pltpu.HBM),
        out_shape=pltpu.HBM((sources, rows, size), jnp.bfloat16),
        scratch_shapes=[
            pltpu.VMEM((sources, rows, size), jnp.bfloat16),
            pltpu.SemaphoreType.DMA((total // 128,)),
        ],
        compiler_params=params(),
        cost_estimate=pl.CostEstimate(
            flops=4 * total * total * size, bytes_accessed=8 * total * size,
            transcendentals=total * total,
        ),
        name="attend",
    )(recv)


def attend_band_kernel(query_rows, scale, query_ref, recv_ref, out_ref):
    sources, both, size = recv_ref.shape
    rows = both // 2
    group = 256 // query_rows
    factor = scale * LOG2E
    for first in range(0, sources, group):
        queries = query_ref[first : first + group].reshape(group * query_rows, size)

        def advance(step, state):
            top, total, summed = state
            at = pl.ds(step * PIECE, PIECE)
            keys = recv_ref[at, :rows].reshape(PIECE * rows, size)
            values = recv_ref[at, rows:].reshape(PIECE * rows, size)
            scores = scores_of(queries, keys)
            new_top = jnp.maximum(top, jnp.max(scores, axis=1, keepdims=True))
            weights = jnp.exp2((scores - new_top) * factor)
            rescale = jnp.exp2((top - new_top) * factor)
            new_total = total * rescale + jnp.sum(weights, axis=1, keepdims=True)
            new_summed = summed * rescale + jnp.dot(
                weights.astype(jnp.bfloat16), values, preferred_element_type=jnp.float32
            )
            return new_top, new_total, new_summed

        start = (
            jnp.full((group * query_rows, 1), LOWEST, jnp.float32),
            jnp.zeros((group * query_rows, 1), jnp.float32),
            jnp.zeros((group * query_rows, size), jnp.float32),
        )
        state = lax.fori_loop(0, sources // PIECE, advance, start)
        result = (state[2] / state[1]).astype(jnp.bfloat16)
        out_ref[first : first + group] = result.reshape(group, query_rows, size)


def attend_band(queries, recv, scale):
    return pl.pallas_call(
        functools.partial(attend_band_kernel, queries.shape[1], scale),
        out_shape=jax.ShapeDtypeStruct(queries.shape, jnp.bfloat16),
        compiler_params=params(),
        name="attend_band",
    )(queries, recv)


def collect_kernel(by_head_ref, out_ref, turned, sems):
    departures = []
    for piece in range(by_head_ref.shape[1] // PIECE):
        at = pl.ds(piece * PIECE, PIECE)
        turned[at] = jnp.swapaxes(by_head_ref[:, at], 0, 1)
        departure = pltpu.make_async_copy(turned.at[at], out_ref.at[at], sems.at[piece])
        departure.start()
        departures.append(departure)
    for departure in departures:
        departure.wait()


def collect(by_head):
    heads, rows, size = by_head.shape
    return pl.pallas_call(
        collect_kernel,
        in_specs=[pl.BlockSpec(memory_space=pltpu.VMEM)],
        out_specs=pl.BlockSpec(memory_space=pltpu.HBM),
        out_shape=pltpu.HBM((rows, heads, size), by_head.dtype),
        scratch_shapes=[
            pltpu.VMEM((rows, heads, size), by_head.dtype),
            pltpu.SemaphoreType.DMA((rows // PIECE,)),
        ],
        compiler_params=params(),
        name="collect",
    )(by_head)


def video_kernel(
    scale, group, pairs_ref, counts_ref, where_ref, video_ref, own_ref, core_ref, chip_ref, out_ref,
    near_keys, near_values, keys_ref, values_ref, queries_ref, result_ref, turned, sems,
):
    heads, both, size = own_ref.shape
    rows = both // 2
    blocks, slots = pairs_ref.shape
    for ref, place in ((own_ref, rows), (core_ref, where_ref[1]), (chip_ref, where_ref[2])):
        at = pl.ds(pl.multiple_of(place, rows), rows)
        near_keys[:, at] = ref[:, :rows]
        near_values[:, at] = ref[:, rows:]
    values_ref[:, :, :, size:] = jnp.ones((blocks, heads, slots * ABLK, size), jnp.bfloat16)
    column = lax.broadcasted_iota(jnp.int32, (VBLK, slots * ABLK), 1)
    factor = scale * LOG2E

    def prepare(block):
        queries_ref[block] = jnp.swapaxes(video_ref[block * VBLK : (block + 1) * VBLK], 0, 1)
        for slot in range(slots):
            start = pl.multiple_of((pairs_ref[block, slot] - where_ref[0]) * ABLK, ABLK)
            here = slice(slot * ABLK, (slot + 1) * ABLK)
            keys_ref[block, :, here] = near_keys[:, pl.ds(start, ABLK)]
            values_ref[block, :, here, :size] = near_values[:, pl.ds(start, ABLK)]

    def departure(block):
        at = pl.ds(block * VBLK, VBLK)
        return pltpu.make_async_copy(turned.at[block], out_ref.at[at], sems.at[block])

    units = [(block, first) for block in range(blocks) for first in range(0, heads, group)]
    scores, weights = {}, {}
    for step in range(len(units) + 2):
        if step < len(units):
            block, first = units[step]
            if first == 0:
                prepare(block)
            live = column < counts_ref[block] * ABLK
            scores[step] = [
                jnp.where(live, scores_of(queries_ref[block, head], keys_ref[block, head]), LOWEST)
                for head in range(first, first + group)
            ]
        if 1 <= step <= len(units):
            now = jnp.stack(scores.pop(step - 1))
            top = jnp.max(now, axis=2, keepdims=True)
            weights[step - 1] = jnp.exp2((now - top) * factor).astype(jnp.bfloat16)
        if step >= 2:
            block, first = units[step - 2]
            now = weights.pop(step - 2)
            for i in range(group):
                summed = jnp.dot(
                    now[i], values_ref[block, first + i], preferred_element_type=jnp.float32
                )
                result_ref[block, first + i] = (summed[:, :size] / summed[:, size:]).astype(
                    jnp.bfloat16
                )
            if first + group == heads:
                turned[block] = jnp.swapaxes(result_ref[block], 0, 1)
                departure(block).start()
    for block in range(blocks):
        departure(block).wait()


def video(video_q, own, core, chip, pairs, counts, where, scale):
    total, heads, size = video_q.shape
    rows = own.shape[1] // 2
    blocks, slots = pairs.shape
    work = total * heads * slots * ABLK
    in_smem = pl.BlockSpec(memory_space=pltpu.SMEM)
    in_vmem = pl.BlockSpec(memory_space=pltpu.VMEM)
    return pl.pallas_call(
        functools.partial(video_kernel, scale, 4),
        in_specs=[in_smem] * 3 + [in_vmem] * 4,
        out_specs=pl.BlockSpec(memory_space=pltpu.HBM),
        out_shape=pltpu.HBM(video_q.shape, jnp.bfloat16),
        scratch_shapes=[
            pltpu.VMEM((heads, 3 * rows, size), jnp.bfloat16),
            pltpu.VMEM((heads, 3 * rows, size), jnp.bfloat16),
            pltpu.VMEM((blocks, heads, slots * ABLK, size), jnp.bfloat16),
            pltpu.VMEM((blocks, heads, slots * ABLK, 2 * size), jnp.bfloat16),
            pltpu.VMEM((blocks, heads, VBLK, size), jnp.bfloat16),
            pltpu.VMEM((blocks, heads, VBLK, size), jnp.bfloat16),
            pltpu.VMEM((blocks, VBLK, heads, size), jnp.bfloat16),
            pltpu.SemaphoreType.DMA((blocks,)),
        ],
        compiler_params=params(),
        cost_estimate=pl.CostEstimate(
            flops=4 * work * size, bytes_accessed=32 * total * heads * size, transcendentals=work
        ),
        name="video",
    )(pairs, counts, where, video_q, own, core, chip)


def local(audio_qkv, video_q, pairs, counts):
    devices = lax.axis_size("seq")
    rows, unused, heads, size = audio_qkv.shape
    bands = devices // heads
    band_rows = rows // bands
    scale = size ** (-0.5)
    send, kv = arrange(audio_qkv)
    core_pairs = [(i, i ^ 1) for i in range(devices)]
    chip_pairs = [(i, ((i + 1) ^ 1) - 1) for i in range(1, devices - 1)]

    chip = lax.ppermute(kv, "seq", chip_pairs)

    plane = devices // 4
    order = [z * plane + plane - 1 - r for z in (1, 3, 0, 2) for r in range(plane)]

    def exchange(value):
        return lax.all_to_all(
            value, "seq", split_axis=0, concat_axis=0, tiled=True, axis_index_groups=[order]
        )

    core = lax.ppermute(kv, "seq", core_pairs)
    me = lax.axis_index("seq")
    odd = me & 1
    where = jnp.stack([(me - 1) * (rows // ABLK), 2 * (1 - odd) * rows, 2 * odd * rows])
    video_cross = video(
        video_q, kv, core, chip, pairs, counts, where.astype(jnp.int32), scale
    )
    if bands == 1:
        head_out = attend(exchange(send), scale)
    else:
        queries = exchange(send[:, :, :PIECE].reshape(devices, band_rows, size))
        spread = jnp.broadcast_to(kv[:, None], (heads, bands, 2 * rows, size))
        recv = exchange(spread.reshape(devices, 2 * rows, size))
        head_out = attend_band(queries, recv, scale)
    returned, video_cross = lax.optimization_barrier((exchange(head_out), video_cross))
    audio_attn = collect(returned.reshape(heads, rows, size))
    return audio_attn, video_cross


def solution(mesh):
    in_specs = (
        P(("groups", "seq"), None, None, None),
        P(("groups", "seq"), None, None),
        P(("groups", "seq"), None),
        P(("groups", "seq")),
    )
    out_specs = (P(("groups", "seq"), None, None), P(("groups", "seq"), None, None))
    return jax.shard_map(local, mesh=mesh, in_specs=in_specs, out_specs=out_specs, check_vma=False)
```

```python
import functools

import jax
import jax.numpy as jnp
from jax import lax
from jax.experimental import pallas as pl
from jax.experimental.pallas import tpu as pltpu
from jax.sharding import PartitionSpec as P

ABLK = 32
VBLK = 128
LOG2E = 1.4426950408889634
LOWEST = -1e30
VMEM_LIMIT = 48 * 1024 * 1024


def params():
    return pltpu.CompilerParams(vmem_limit_bytes=VMEM_LIMIT)


PIECE = 16


def arrange_kernel(pieces, qkv_ref, send_ref, kv_ref, came, turned, in_sems, out_sems):
    rows = pieces * PIECE
    arrivals = [
        pltpu.make_async_copy(
            qkv_ref.at[pl.ds(piece * PIECE, PIECE)], came.at[piece], in_sems.at[piece]
        )
        for piece in range(pieces)
    ]
    for arrival in arrivals:
        arrival.start()
    departures = []
    for piece, arrival in enumerate(arrivals):
        arrival.wait()
        for part in range(3):
            by_head = jnp.swapaxes(came[piece, :, part], 0, 1)
            turned[piece, :, part * PIECE : (part + 1) * PIECE] = by_head
            if part:
                at = (part - 1) * rows + piece * PIECE
                kv_ref[:, at : at + PIECE] = by_head
        departure = pltpu.make_async_copy(
            turned.at[piece], send_ref.at[:, piece], out_sems.at[piece]
        )
        departure.start()
        departures.append(departure)
    for departure in departures:
        departure.wait()


def arrange(audio_qkv):
    rows, parts, heads, size = audio_qkv.shape
    dtype = audio_qkv.dtype
    pieces = rows // PIECE
    return pl.pallas_call(
        functools.partial(arrange_kernel, pieces),
        in_specs=[pl.BlockSpec(memory_space=pltpu.HBM)],
        out_specs=(
            pl.BlockSpec(memory_space=pltpu.HBM),
            pl.BlockSpec(memory_space=pltpu.VMEM),
        ),
        out_shape=(
            pltpu.HBM((heads, pieces, parts * PIECE, size), dtype),
            jax.ShapeDtypeStruct((heads, 2 * rows, size), dtype),
        ),
        scratch_shapes=[
            pltpu.VMEM((pieces, PIECE, parts, heads, size), dtype),
            pltpu.VMEM((pieces, heads, parts * PIECE, size), dtype),
            pltpu.SemaphoreType.DMA((pieces,)),
            pltpu.SemaphoreType.DMA((pieces,)),
        ],
        compiler_params=params(),
        name="arrange",
    )(pltpu.with_memory_space_constraint(audio_qkv, pltpu.HBM))


def scores_of(queries, keys):
    return lax.dot_general(
        queries, keys, (((1,), (1,)), ((), ())), preferred_element_type=jnp.float32
    )


def attend_kernel(scale, recv_ref, out_ref, held, sems):
    sources, pieces, unused, size = recv_ref.shape
    total = sources * pieces * PIECE
    chunk = total // sems.shape[0]
    group = chunk // (pieces * PIECE)
    factor = scale * LOG2E
    keys = recv_ref[:, :, PIECE : 2 * PIECE].reshape(total, size)
    values = recv_ref[:, :, 2 * PIECE :].reshape(total, size)
    chunks = total // chunk
    scores, weights, sums, departures = {}, {}, {}, []
    for step in range(chunks + 2):
        if step < chunks:
            first = step * group
            queries = recv_ref[first : first + group, :, :PIECE].reshape(chunk, size)
            scores[step] = scores_of(queries, keys)
        if 0 <= step - 1 < chunks:
            now = scores.pop(step - 1)
            top = jnp.max(now, axis=1, keepdims=True)
            exact = jnp.exp2((now - top) * factor)
            sums[step - 1] = jnp.sum(exact, axis=1, keepdims=True)
            weights[step - 1] = exact.astype(jnp.bfloat16)
        if step >= 2:
            summed = jnp.dot(
                weights.pop(step - 2), values, preferred_element_type=jnp.float32
            )
            result = (summed / sums.pop(step - 2)).astype(jnp.bfloat16)
            at = (step - 2) * group
            held[at : at + group] = result.reshape(group, pieces * PIECE, size)
            departure = pltpu.make_async_copy(
                held.at[pl.ds(at, group)], out_ref.at[pl.ds(at, group)], sems.at[step - 2]
            )
            departure.start()
            departures.append(departure)
    for departure in departures:
        departure.wait()


def attend(recv, scale):
    sources, pieces, unused, size = recv.shape
    rows = pieces * PIECE
    total = sources * rows
    return pl.pallas_call(
        functools.partial(attend_kernel, scale),
        in_specs=[pl.BlockSpec(memory_space=pltpu.VMEM)],
        out_specs=pl.BlockSpec(memory_space=pltpu.HBM),
        out_shape=pltpu.HBM((sources, rows, size), jnp.bfloat16),
        scratch_shapes=[
            pltpu.VMEM((sources, rows, size), jnp.bfloat16),
            pltpu.SemaphoreType.DMA((total // 128,)),
        ],
        compiler_params=params(),
        cost_estimate=pl.CostEstimate(
            flops=4 * total * total * size, bytes_accessed=8 * total * size,
            transcendentals=total * total,
        ),
        name="attend",
    )(recv)


def attend_band_kernel(query_rows, scale, query_ref, recv_ref, out_ref):
    sources, both, size = recv_ref.shape
    rows = both // 2
    group = 256 // query_rows
    factor = scale * LOG2E
    for first in range(0, sources, group):
        queries = query_ref[first : first + group].reshape(group * query_rows, size)

        def advance(step, state):
            top, total, summed = state
            at = pl.ds(step * PIECE, PIECE)
            keys = recv_ref[at, :rows].reshape(PIECE * rows, size)
            values = recv_ref[at, rows:].reshape(PIECE * rows, size)
            scores = scores_of(queries, keys)
            new_top = jnp.maximum(top, jnp.max(scores, axis=1, keepdims=True))
            weights = jnp.exp2((scores - new_top) * factor)
            rescale = jnp.exp2((top - new_top) * factor)
            new_total = total * rescale + jnp.sum(weights, axis=1, keepdims=True)
            new_summed = summed * rescale + jnp.dot(
                weights.astype(jnp.bfloat16), values, preferred_element_type=jnp.float32
            )
            return new_top, new_total, new_summed

        start = (
            jnp.full((group * query_rows, 1), LOWEST, jnp.float32),
            jnp.zeros((group * query_rows, 1), jnp.float32),
            jnp.zeros((group * query_rows, size), jnp.float32),
        )
        state = lax.fori_loop(0, sources // PIECE, advance, start)
        result = (state[2] / state[1]).astype(jnp.bfloat16)
        out_ref[first : first + group] = result.reshape(group, query_rows, size)


def attend_band(queries, recv, scale):
    return pl.pallas_call(
        functools.partial(attend_band_kernel, queries.shape[1], scale),
        out_shape=jax.ShapeDtypeStruct(queries.shape, jnp.bfloat16),
        compiler_params=params(),
        name="attend_band",
    )(queries, recv)


def collect_kernel(by_head_ref, out_ref, turned, sems):
    departures = []
    for piece in range(by_head_ref.shape[1] // PIECE):
        at = pl.ds(piece * PIECE, PIECE)
        turned[at] = jnp.swapaxes(by_head_ref[:, at], 0, 1)
        departure = pltpu.make_async_copy(turned.at[at], out_ref.at[at], sems.at[piece])
        departure.start()
        departures.append(departure)
    for departure in departures:
        departure.wait()


def collect(by_head):
    heads, rows, size = by_head.shape
    return pl.pallas_call(
        collect_kernel,
        in_specs=[pl.BlockSpec(memory_space=pltpu.VMEM)],
        out_specs=pl.BlockSpec(memory_space=pltpu.HBM),
        out_shape=pltpu.HBM((rows, heads, size), by_head.dtype),
        scratch_shapes=[
            pltpu.VMEM((rows, heads, size), by_head.dtype),
            pltpu.SemaphoreType.DMA((rows // PIECE,)),
        ],
        compiler_params=params(),
        name="collect",
    )(by_head)


def video_kernel(
    scale, group, pairs_ref, counts_ref, where_ref, video_ref, own_ref, core_ref, chip_ref, out_ref,
    near_keys, near_values, keys_ref, values_ref, queries_ref, result_ref, turned, sems,
):
    heads, both, size = own_ref.shape
    rows = both // 2
    blocks, slots = pairs_ref.shape
    for ref, place in ((own_ref, rows), (core_ref, where_ref[1]), (chip_ref, where_ref[2])):
        at = pl.ds(pl.multiple_of(place, rows), rows)
        near_keys[:, at] = ref[:, :rows]
        near_values[:, at] = ref[:, rows:]
    values_ref[:, :, :, size:] = jnp.ones((blocks, heads, slots * ABLK, size), jnp.bfloat16)
    column = lax.broadcasted_iota(jnp.int32, (VBLK, slots * ABLK), 1)
    factor = scale * LOG2E

    def prepare(block):
        queries_ref[block] = jnp.swapaxes(video_ref[block * VBLK : (block + 1) * VBLK], 0, 1)
        for slot in range(slots):
            start = pl.multiple_of((pairs_ref[block, slot] - where_ref[0]) * ABLK, ABLK)
            here = slice(slot * ABLK, (slot + 1) * ABLK)
            keys_ref[block, :, here] = near_keys[:, pl.ds(start, ABLK)]
            values_ref[block, :, here, :size] = near_values[:, pl.ds(start, ABLK)]

    def departure(block):
        at = pl.ds(block * VBLK, VBLK)
        return pltpu.make_async_copy(turned.at[block], out_ref.at[at], sems.at[block])

    units = [(block, first) for block in range(blocks) for first in range(0, heads, group)]
    scores, weights = {}, {}
    for step in range(len(units) + 2):
        if step < len(units):
            block, first = units[step]
            if first == 0:
                prepare(block)
            live = column < counts_ref[block] * ABLK
            scores[step] = [
                jnp.where(live, scores_of(queries_ref[block, head], keys_ref[block, head]), LOWEST)
                for head in range(first, first + group)
            ]
        if 1 <= step <= len(units):
            now = jnp.stack(scores.pop(step - 1))
            top = jnp.max(now, axis=2, keepdims=True)
            weights[step - 1] = jnp.exp2((now - top) * factor).astype(jnp.bfloat16)
        if step >= 2:
            block, first = units[step - 2]
            now = weights.pop(step - 2)
            for i in range(group):
                summed = jnp.dot(
                    now[i], values_ref[block, first + i], preferred_element_type=jnp.float32
                )
                result_ref[block, first + i] = (summed[:, :size] / summed[:, size:]).astype(
                    jnp.bfloat16
                )
            if first + group == heads:
                turned[block] = jnp.swapaxes(result_ref[block], 0, 1)
                departure(block).start()
    for block in range(blocks):
        departure(block).wait()


def video(video_q, own, core, chip, pairs, counts, where, scale):
    total, heads, size = video_q.shape
    rows = own.shape[1] // 2
    blocks, slots = pairs.shape
    work = total * heads * slots * ABLK
    in_smem = pl.BlockSpec(memory_space=pltpu.SMEM)
    in_vmem = pl.BlockSpec(memory_space=pltpu.VMEM)
    return pl.pallas_call(
        functools.partial(video_kernel, scale, 4),
        in_specs=[in_smem] * 3 + [in_vmem] * 4,
        out_specs=pl.BlockSpec(memory_space=pltpu.HBM),
        out_shape=pltpu.HBM(video_q.shape, jnp.bfloat16),
        scratch_shapes=[
            pltpu.VMEM((heads, 3 * rows, size), jnp.bfloat16),
            pltpu.VMEM((heads, 3 * rows, size), jnp.bfloat16),
            pltpu.VMEM((blocks, heads, slots * ABLK, size), jnp.bfloat16),
            pltpu.VMEM((blocks, heads, slots * ABLK, 2 * size), jnp.bfloat16),
            pltpu.VMEM((blocks, heads, VBLK, size), jnp.bfloat16),
            pltpu.VMEM((blocks, heads, VBLK, size), jnp.bfloat16),
            pltpu.VMEM((blocks, VBLK, heads, size), jnp.bfloat16),
            pltpu.SemaphoreType.DMA((blocks,)),
        ],
        compiler_params=params(),
        cost_estimate=pl.CostEstimate(
            flops=4 * work * size, bytes_accessed=32 * total * heads * size, transcendentals=work
        ),
        name="video",
    )(pairs, counts, where, video_q, own, core, chip)


def local(audio_qkv, video_q, pairs, counts):
    devices = lax.axis_size("seq")
    rows, unused, heads, size = audio_qkv.shape
    bands = devices // heads
    band_rows = rows // bands
    scale = size ** (-0.5)
    send, kv = arrange(audio_qkv)
    core_pairs = [(i, i ^ 1) for i in range(devices)]
    chip_pairs = [(i, ((i + 1) ^ 1) - 1) for i in range(1, devices - 1)]

    chip = lax.ppermute(kv, "seq", chip_pairs)

    plane = devices // 4
    order = [z * plane + plane - 1 - r for r in range(plane) for z in (1, 0, 3, 2)]

    def exchange(value):
        return lax.all_to_all(
            value, "seq", split_axis=0, concat_axis=0, tiled=True, axis_index_groups=[order]
        )

    core = lax.ppermute(kv, "seq", core_pairs)
    me = lax.axis_index("seq")
    odd = me & 1
    where = jnp.stack([(me - 1) * (rows // ABLK), 2 * (1 - odd) * rows, 2 * odd * rows])
    video_cross = video(
        video_q, kv, core, chip, pairs, counts, where.astype(jnp.int32), scale
    )
    if bands == 1:
        head_out = attend(exchange(send), scale)
    else:
        queries = exchange(send[:, :, :PIECE].reshape(devices, band_rows, size))
        spread = jnp.broadcast_to(kv[:, None], (heads, bands, 2 * rows, size))
        recv = exchange(spread.reshape(devices, 2 * rows, size))
        head_out = attend_band(queries, recv, scale)
    returned, video_cross = lax.optimization_barrier((exchange(head_out), video_cross))
    audio_attn = collect(returned.reshape(heads, rows, size))
    return audio_attn, video_cross


def solution(mesh):
    in_specs = (
        P(("groups", "seq"), None, None, None),
        P(("groups", "seq"), None, None),
        P(("groups", "seq"), None),
        P(("groups", "seq")),
    )
    out_specs = (P(("groups", "seq"), None, None), P(("groups", "seq"), None, None))
    return jax.shard_map(local, mesh=mesh, in_specs=in_specs, out_specs=out_specs, check_vma=False)
```

```python
import functools

import jax
import jax.numpy as jnp
from jax import lax
from jax.experimental import pallas as pl
from jax.experimental.pallas import tpu as pltpu
from jax.sharding import PartitionSpec as P

ABLK = 32
VBLK = 128
LOG2E = 1.4426950408889634
LOWEST = -1e30
VMEM_LIMIT = 48 * 1024 * 1024


def params():
    return pltpu.CompilerParams(vmem_limit_bytes=VMEM_LIMIT)


PIECE = 16


def arrange_kernel(pieces, qkv_ref, send_ref, kv_ref, came, turned, in_sems, out_sems):
    rows = pieces * PIECE
    arrivals = [
        pltpu.make_async_copy(
            qkv_ref.at[pl.ds(piece * PIECE, PIECE)], came.at[piece], in_sems.at[piece]
        )
        for piece in range(pieces)
    ]
    for arrival in arrivals:
        arrival.start()
    departures = []
    for piece, arrival in enumerate(arrivals):
        arrival.wait()
        for part in range(3):
            by_head = jnp.swapaxes(came[piece, :, part], 0, 1)
            turned[piece, :, part * PIECE : (part + 1) * PIECE] = by_head
            if part:
                at = (part - 1) * rows + piece * PIECE
                kv_ref[:, at : at + PIECE] = by_head
        departure = pltpu.make_async_copy(
            turned.at[piece], send_ref.at[:, piece], out_sems.at[piece]
        )
        departure.start()
        departures.append(departure)
    for departure in departures:
        departure.wait()


def arrange(audio_qkv):
    rows, parts, heads, size = audio_qkv.shape
    dtype = audio_qkv.dtype
    pieces = rows // PIECE
    return pl.pallas_call(
        functools.partial(arrange_kernel, pieces),
        in_specs=[pl.BlockSpec(memory_space=pltpu.HBM)],
        out_specs=(
            pl.BlockSpec(memory_space=pltpu.HBM),
            pl.BlockSpec(memory_space=pltpu.VMEM),
        ),
        out_shape=(
            pltpu.HBM((heads, pieces, parts * PIECE, size), dtype),
            jax.ShapeDtypeStruct((heads, 2 * rows, size), dtype),
        ),
        scratch_shapes=[
            pltpu.VMEM((pieces, PIECE, parts, heads, size), dtype),
            pltpu.VMEM((pieces, heads, parts * PIECE, size), dtype),
            pltpu.SemaphoreType.DMA((pieces,)),
            pltpu.SemaphoreType.DMA((pieces,)),
        ],
        compiler_params=params(),
        name="arrange",
    )(pltpu.with_memory_space_constraint(audio_qkv, pltpu.HBM))


def scores_of(queries, keys):
    return lax.dot_general(
        queries, keys, (((1,), (1,)), ((), ())), preferred_element_type=jnp.float32
    )


def attend_kernel(scale, recv_ref, out_ref, held, values_ref, sems):
    sources, pieces, unused, size = recv_ref.shape
    total = sources * pieces * PIECE
    chunk = total // sems.shape[0]
    group = chunk // (pieces * PIECE)
    factor = scale * LOG2E
    keys = recv_ref[:, :, PIECE : 2 * PIECE].reshape(total, size)
    values_ref[:, :size] = recv_ref[:, :, 2 * PIECE :].reshape(total, size)
    values_ref[:, size:] = jnp.ones((total, size), jnp.bfloat16)
    chunks = total // chunk
    scores, weights, departures = {}, {}, []
    for step in range(chunks + 2):
        if step < chunks:
            first = step * group
            queries = recv_ref[first : first + group, :, :PIECE].reshape(chunk, size)
            scores[step] = scores_of(queries, keys)
        if 0 <= step - 1 < chunks:
            now = scores.pop(step - 1)
            top = jnp.max(now, axis=1, keepdims=True)
            weights[step - 1] = jnp.exp2((now - top) * factor).astype(jnp.bfloat16)
        if step >= 2:
            summed = jnp.dot(
                weights.pop(step - 2), values_ref[...], preferred_element_type=jnp.float32
            )
            result = (summed[:, :size] / summed[:, size:]).astype(jnp.bfloat16)
            at = (step - 2) * group
            held[at : at + group] = result.reshape(group, pieces * PIECE, size)
            departure = pltpu.make_async_copy(
                held.at[pl.ds(at, group)], out_ref.at[pl.ds(at, group)], sems.at[step - 2]
            )
            departure.start()
            departures.append(departure)
    for departure in departures:
        departure.wait()


def attend(recv, scale):
    sources, pieces, unused, size = recv.shape
    rows = pieces * PIECE
    total = sources * rows
    return pl.pallas_call(
        functools.partial(attend_kernel, scale),
        in_specs=[pl.BlockSpec(memory_space=pltpu.VMEM)],
        out_specs=pl.BlockSpec(memory_space=pltpu.HBM),
        out_shape=pltpu.HBM((sources, rows, size), jnp.bfloat16),
        scratch_shapes=[
            pltpu.VMEM((sources, rows, size), jnp.bfloat16),
            pltpu.VMEM((total, 2 * size), jnp.bfloat16),
            pltpu.SemaphoreType.DMA((total // 128,)),
        ],
        compiler_params=params(),
        cost_estimate=pl.CostEstimate(
            flops=4 * total * total * size, bytes_accessed=8 * total * size,
            transcendentals=total * total,
        ),
        name="attend",
    )(recv)


def attend_band_kernel(query_rows, scale, query_ref, recv_ref, out_ref):
    sources, both, size = recv_ref.shape
    rows = both // 2
    group = 256 // query_rows
    factor = scale * LOG2E
    for first in range(0, sources, group):
        queries = query_ref[first : first + group].reshape(group * query_rows, size)

        def advance(step, state):
            top, total, summed = state
            at = pl.ds(step * PIECE, PIECE)
            keys = recv_ref[at, :rows].reshape(PIECE * rows, size)
            values = recv_ref[at, rows:].reshape(PIECE * rows, size)
            scores = scores_of(queries, keys)
            new_top = jnp.maximum(top, jnp.max(scores, axis=1, keepdims=True))
            weights = jnp.exp2((scores - new_top) * factor)
            rescale = jnp.exp2((top - new_top) * factor)
            new_total = total * rescale + jnp.sum(weights, axis=1, keepdims=True)
            new_summed = summed * rescale + jnp.dot(
                weights.astype(jnp.bfloat16), values, preferred_element_type=jnp.float32
            )
            return new_top, new_total, new_summed

        start = (
            jnp.full((group * query_rows, 1), LOWEST, jnp.float32),
            jnp.zeros((group * query_rows, 1), jnp.float32),
            jnp.zeros((group * query_rows, size), jnp.float32),
        )
        state = lax.fori_loop(0, sources // PIECE, advance, start)
        result = (state[2] / state[1]).astype(jnp.bfloat16)
        out_ref[first : first + group] = result.reshape(group, query_rows, size)


def attend_band(queries, recv, scale):
    return pl.pallas_call(
        functools.partial(attend_band_kernel, queries.shape[1], scale),
        out_shape=jax.ShapeDtypeStruct(queries.shape, jnp.bfloat16),
        compiler_params=params(),
        name="attend_band",
    )(queries, recv)


def collect_kernel(by_head_ref, out_ref, turned, sems):
    departures = []
    for piece in range(by_head_ref.shape[1] // PIECE):
        at = pl.ds(piece * PIECE, PIECE)
        turned[at] = jnp.swapaxes(by_head_ref[:, at], 0, 1)
        departure = pltpu.make_async_copy(turned.at[at], out_ref.at[at], sems.at[piece])
        departure.start()
        departures.append(departure)
    for departure in departures:
        departure.wait()


def collect(by_head):
    heads, rows, size = by_head.shape
    return pl.pallas_call(
        collect_kernel,
        in_specs=[pl.BlockSpec(memory_space=pltpu.VMEM)],
        out_specs=pl.BlockSpec(memory_space=pltpu.HBM),
        out_shape=pltpu.HBM((rows, heads, size), by_head.dtype),
        scratch_shapes=[
            pltpu.VMEM((rows, heads, size), by_head.dtype),
            pltpu.SemaphoreType.DMA((rows // PIECE,)),
        ],
        compiler_params=params(),
        name="collect",
    )(by_head)


def video_kernel(
    scale, group, pairs_ref, counts_ref, where_ref, video_ref, own_ref, core_ref, chip_ref, out_ref,
    near_keys, near_values, keys_ref, values_ref, queries_ref, result_ref, turned, sems,
):
    heads, both, size = own_ref.shape
    rows = both // 2
    blocks, slots = pairs_ref.shape
    for ref, place in ((own_ref, rows), (core_ref, where_ref[1]), (chip_ref, where_ref[2])):
        at = pl.ds(pl.multiple_of(place, rows), rows)
        near_keys[:, at] = ref[:, :rows]
        near_values[:, at] = ref[:, rows:]
    values_ref[:, :, :, size:] = jnp.ones((blocks, heads, slots * ABLK, size), jnp.bfloat16)
    column = lax.broadcasted_iota(jnp.int32, (VBLK, slots * ABLK), 1)
    factor = scale * LOG2E

    def prepare(block):
        queries_ref[block] = jnp.swapaxes(video_ref[block * VBLK : (block + 1) * VBLK], 0, 1)
        for slot in range(slots):
            start = pl.multiple_of((pairs_ref[block, slot] - where_ref[0]) * ABLK, ABLK)
            here = slice(slot * ABLK, (slot + 1) * ABLK)
            keys_ref[block, :, here] = near_keys[:, pl.ds(start, ABLK)]
            values_ref[block, :, here, :size] = near_values[:, pl.ds(start, ABLK)]

    def departure(block):
        at = pl.ds(block * VBLK, VBLK)
        return pltpu.make_async_copy(turned.at[block], out_ref.at[at], sems.at[block])

    units = [(block, first) for block in range(blocks) for first in range(0, heads, group)]
    scores, weights = {}, {}
    for step in range(len(units) + 2):
        if step < len(units):
            block, first = units[step]
            if first == 0:
                prepare(block)
            live = column < counts_ref[block] * ABLK
            scores[step] = [
                jnp.where(live, scores_of(queries_ref[block, head], keys_ref[block, head]), LOWEST)
                for head in range(first, first + group)
            ]
        if 1 <= step <= len(units):
            now = jnp.stack(scores.pop(step - 1))
            top = jnp.max(now, axis=2, keepdims=True)
            weights[step - 1] = jnp.exp2((now - top) * factor).astype(jnp.bfloat16)
        if step >= 2:
            block, first = units[step - 2]
            now = weights.pop(step - 2)
            for i in range(group):
                summed = jnp.dot(
                    now[i], values_ref[block, first + i], preferred_element_type=jnp.float32
                )
                result_ref[block, first + i] = (summed[:, :size] / summed[:, size:]).astype(
                    jnp.bfloat16
                )
            if first + group == heads:
                turned[block] = jnp.swapaxes(result_ref[block], 0, 1)
                departure(block).start()
    for block in range(blocks):
        departure(block).wait()


def video(video_q, own, core, chip, pairs, counts, where, scale):
    total, heads, size = video_q.shape
    rows = own.shape[1] // 2
    blocks, slots = pairs.shape
    work = total * heads * slots * ABLK
    in_smem = pl.BlockSpec(memory_space=pltpu.SMEM)
    in_vmem = pl.BlockSpec(memory_space=pltpu.VMEM)
    return pl.pallas_call(
        functools.partial(video_kernel, scale, 4),
        in_specs=[in_smem] * 3 + [in_vmem] * 4,
        out_specs=pl.BlockSpec(memory_space=pltpu.HBM),
        out_shape=pltpu.HBM(video_q.shape, jnp.bfloat16),
        scratch_shapes=[
            pltpu.VMEM((heads, 3 * rows, size), jnp.bfloat16),
            pltpu.VMEM((heads, 3 * rows, size), jnp.bfloat16),
            pltpu.VMEM((blocks, heads, slots * ABLK, size), jnp.bfloat16),
            pltpu.VMEM((blocks, heads, slots * ABLK, 2 * size), jnp.bfloat16),
            pltpu.VMEM((blocks, heads, VBLK, size), jnp.bfloat16),
            pltpu.VMEM((blocks, heads, VBLK, size), jnp.bfloat16),
            pltpu.VMEM((blocks, VBLK, heads, size), jnp.bfloat16),
            pltpu.SemaphoreType.DMA((blocks,)),
        ],
        compiler_params=params(),
        cost_estimate=pl.CostEstimate(
            flops=4 * work * size, bytes_accessed=32 * total * heads * size, transcendentals=work
        ),
        name="video",
    )(pairs, counts, where, video_q, own, core, chip)


def local(audio_qkv, video_q, pairs, counts):
    devices = lax.axis_size("seq")
    rows, unused, heads, size = audio_qkv.shape
    bands = devices // heads
    band_rows = rows // bands
    scale = size ** (-0.5)
    send, kv = arrange(audio_qkv)
    core_pairs = [(i, i ^ 1) for i in range(devices)]
    chip_pairs = [(i, ((i + 1) ^ 1) - 1) for i in range(1, devices - 1)]

    chip = lax.ppermute(kv, "seq", chip_pairs)

    order = [(devices - 1 - devices // 2 - p) % devices for p in range(devices)]

    def exchange(value):
        return lax.all_to_all(
            value, "seq", split_axis=0, concat_axis=0, tiled=True, axis_index_groups=[order]
        )

    core = lax.ppermute(kv, "seq", core_pairs)
    me = lax.axis_index("seq")
    odd = me & 1
    where = jnp.stack([(me - 1) * (rows // ABLK), 2 * (1 - odd) * rows, 2 * odd * rows])
    video_cross = video(
        video_q, kv, core, chip, pairs, counts, where.astype(jnp.int32), scale
    )
    if bands == 1:
        head_out = attend(exchange(send), scale)
    else:
        queries = exchange(send[:, :, :PIECE].reshape(devices, band_rows, size))
        spread = jnp.broadcast_to(kv[:, None], (heads, bands, 2 * rows, size))
        recv = exchange(spread.reshape(devices, 2 * rows, size))
        head_out = attend_band(queries, recv, scale)
    returned, video_cross = lax.optimization_barrier((exchange(head_out), video_cross))
    audio_attn = collect(returned.reshape(heads, rows, size))
    return audio_attn, video_cross


def solution(mesh):
    in_specs = (
        P(("groups", "seq"), None, None, None),
        P(("groups", "seq"), None, None),
        P(("groups", "seq"), None),
        P(("groups", "seq")),
    )
    out_specs = (P(("groups", "seq"), None, None), P(("groups", "seq"), None, None))
    return jax.shard_map(local, mesh=mesh, in_specs=in_specs, out_specs=out_specs, check_vma=False)
```

```python
import functools

import jax
import jax.numpy as jnp
from jax import lax
from jax.experimental import pallas as pl
from jax.experimental.pallas import tpu as pltpu
from jax.sharding import PartitionSpec as P

ABLK = 32
VBLK = 128
LOG2E = 1.4426950408889634
LOWEST = -1e30
VMEM_LIMIT = 48 * 1024 * 1024


def params():
    return pltpu.CompilerParams(vmem_limit_bytes=VMEM_LIMIT)


PIECE = 16


def arrange_kernel(pieces, qkv_ref, send_ref, kv_ref, came, turned, in_sems, out_sems):
    rows = pieces * PIECE
    arrivals = [
        pltpu.make_async_copy(
            qkv_ref.at[pl.ds(piece * PIECE, PIECE)], came.at[piece], in_sems.at[piece]
        )
        for piece in range(pieces)
    ]
    for arrival in arrivals:
        arrival.start()
    departures = []
    for piece, arrival in enumerate(arrivals):
        arrival.wait()
        for part in range(3):
            by_head = jnp.swapaxes(came[piece, :, part], 0, 1)
            turned[piece, :, part * PIECE : (part + 1) * PIECE] = by_head
            if part:
                at = (part - 1) * rows + piece * PIECE
                kv_ref[:, at : at + PIECE] = by_head
        departure = pltpu.make_async_copy(
            turned.at[piece], send_ref.at[:, piece], out_sems.at[piece]
        )
        departure.start()
        departures.append(departure)
    for departure in departures:
        departure.wait()


def arrange(audio_qkv):
    rows, parts, heads, size = audio_qkv.shape
    dtype = audio_qkv.dtype
    pieces = rows // PIECE
    return pl.pallas_call(
        functools.partial(arrange_kernel, pieces),
        in_specs=[pl.BlockSpec(memory_space=pltpu.HBM)],
        out_specs=(
            pl.BlockSpec(memory_space=pltpu.HBM),
            pl.BlockSpec(memory_space=pltpu.VMEM),
        ),
        out_shape=(
            pltpu.HBM((heads, pieces, parts * PIECE, size), dtype),
            jax.ShapeDtypeStruct((heads, 2 * rows, size), dtype),
        ),
        scratch_shapes=[
            pltpu.VMEM((pieces, PIECE, parts, heads, size), dtype),
            pltpu.VMEM((pieces, heads, parts * PIECE, size), dtype),
            pltpu.SemaphoreType.DMA((pieces,)),
            pltpu.SemaphoreType.DMA((pieces,)),
        ],
        compiler_params=params(),
        name="arrange",
    )(pltpu.with_memory_space_constraint(audio_qkv, pltpu.HBM))


def scores_of(queries, keys):
    return lax.dot_general(
        queries, keys, (((1,), (1,)), ((), ())), preferred_element_type=jnp.float32
    )


def attend_kernel(scale, recv_ref, out_ref, held, sems):
    sources, pieces, unused, size = recv_ref.shape
    total = sources * pieces * PIECE
    chunk = total // sems.shape[0]
    group = chunk // (pieces * PIECE)
    factor = scale * LOG2E
    keys = recv_ref[:, :, PIECE : 2 * PIECE].reshape(total, size)
    values = recv_ref[:, :, 2 * PIECE :].reshape(total, size)
    chunks = total // chunk
    scores, weights, sums, departures = {}, {}, {}, []
    for step in range(chunks + 2):
        if step < chunks:
            first = step * group
            queries = recv_ref[first : first + group, :, :PIECE].reshape(chunk, size)
            scores[step] = scores_of(queries, keys)
        if 0 <= step - 1 < chunks:
            now = scores.pop(step - 1)
            top = jnp.max(now, axis=1, keepdims=True)
            exact = jnp.exp2((now - top) * factor)
            sums[step - 1] = jnp.sum(exact, axis=1, keepdims=True)
            weights[step - 1] = exact.astype(jnp.bfloat16)
        if step >= 2:
            summed = jnp.dot(
                weights.pop(step - 2), values, preferred_element_type=jnp.float32
            )
            result = (summed / sums.pop(step - 2)).astype(jnp.bfloat16)
            at = (step - 2) * group
            held[at : at + group] = result.reshape(group, pieces * PIECE, size)
            departure = pltpu.make_async_copy(
                held.at[pl.ds(at, group)], out_ref.at[pl.ds(at, group)], sems.at[step - 2]
            )
            departure.start()
            departures.append(departure)
    for departure in departures:
        departure.wait()


def attend(recv, scale):
    sources, pieces, unused, size = recv.shape
    rows = pieces * PIECE
    total = sources * rows
    return pl.pallas_call(
        functools.partial(attend_kernel, scale),
        in_specs=[pl.BlockSpec(memory_space=pltpu.VMEM)],
        out_specs=pl.BlockSpec(memory_space=pltpu.HBM),
        out_shape=pltpu.HBM((sources, rows, size), jnp.bfloat16),
        scratch_shapes=[
            pltpu.VMEM((sources, rows, size), jnp.bfloat16),
            pltpu.SemaphoreType.DMA((total // 128,)),
        ],
        compiler_params=params(),
        cost_estimate=pl.CostEstimate(
            flops=4 * total * total * size, bytes_accessed=8 * total * size,
            transcendentals=total * total,
        ),
        name="attend",
    )(recv)


def attend_band_kernel(query_rows, scale, query_ref, recv_ref, out_ref):
    sources, both, size = recv_ref.shape
    rows = both // 2
    group = 256 // query_rows
    factor = scale * LOG2E
    for first in range(0, sources, group):
        queries = query_ref[first : first + group].reshape(group * query_rows, size)

        def advance(step, state):
            top, total, summed = state
            at = pl.ds(step * PIECE, PIECE)
            keys = recv_ref[at, :rows].reshape(PIECE * rows, size)
            values = recv_ref[at, rows:].reshape(PIECE * rows, size)
            scores = scores_of(queries, keys)
            new_top = jnp.maximum(top, jnp.max(scores, axis=1, keepdims=True))
            weights = jnp.exp2((scores - new_top) * factor)
            rescale = jnp.exp2((top - new_top) * factor)
            new_total = total * rescale + jnp.sum(weights, axis=1, keepdims=True)
            new_summed = summed * rescale + jnp.dot(
                weights.astype(jnp.bfloat16), values, preferred_element_type=jnp.float32
            )
            return new_top, new_total, new_summed

        start = (
            jnp.full((group * query_rows, 1), LOWEST, jnp.float32),
            jnp.zeros((group * query_rows, 1), jnp.float32),
            jnp.zeros((group * query_rows, size), jnp.float32),
        )
        state = lax.fori_loop(0, sources // PIECE, advance, start)
        result = (state[2] / state[1]).astype(jnp.bfloat16)
        out_ref[first : first + group] = result.reshape(group, query_rows, size)


def attend_band(queries, recv, scale):
    return pl.pallas_call(
        functools.partial(attend_band_kernel, queries.shape[1], scale),
        out_shape=jax.ShapeDtypeStruct(queries.shape, jnp.bfloat16),
        compiler_params=params(),
        name="attend_band",
    )(queries, recv)


def collect_kernel(by_head_ref, out_ref, turned, sems):
    departures = []
    for piece in range(by_head_ref.shape[1] // PIECE):
        at = pl.ds(piece * PIECE, PIECE)
        turned[at] = jnp.swapaxes(by_head_ref[:, at], 0, 1)
        departure = pltpu.make_async_copy(turned.at[at], out_ref.at[at], sems.at[piece])
        departure.start()
        departures.append(departure)
    for departure in departures:
        departure.wait()


def collect(by_head):
    heads, rows, size = by_head.shape
    return pl.pallas_call(
        collect_kernel,
        in_specs=[pl.BlockSpec(memory_space=pltpu.VMEM)],
        out_specs=pl.BlockSpec(memory_space=pltpu.HBM),
        out_shape=pltpu.HBM((rows, heads, size), by_head.dtype),
        scratch_shapes=[
            pltpu.VMEM((rows, heads, size), by_head.dtype),
            pltpu.SemaphoreType.DMA((rows // PIECE,)),
        ],
        compiler_params=params(),
        name="collect",
    )(by_head)


def video_kernel(
    scale, group, pairs_ref, counts_ref, where_ref, video_ref, own_ref, core_ref, chip_ref, out_ref,
    near_keys, near_values, keys_ref, values_ref, queries_ref, result_ref, turned, sems,
):
    heads, both, size = own_ref.shape
    rows = both // 2
    blocks, slots = pairs_ref.shape
    for ref, place in ((own_ref, rows), (core_ref, where_ref[1]), (chip_ref, where_ref[2])):
        at = pl.ds(pl.multiple_of(place, rows), rows)
        near_keys[:, at] = ref[:, :rows]
        near_values[:, at] = ref[:, rows:]
    values_ref[:, :, :, size:] = jnp.ones((blocks, heads, slots * ABLK, size), jnp.bfloat16)
    column = lax.broadcasted_iota(jnp.int32, (VBLK, slots * ABLK), 1)
    factor = scale * LOG2E

    def prepare(block):
        queries_ref[block] = jnp.swapaxes(video_ref[block * VBLK : (block + 1) * VBLK], 0, 1)
        for slot in range(slots):
            start = pl.multiple_of((pairs_ref[block, slot] - where_ref[0]) * ABLK, ABLK)
            here = slice(slot * ABLK, (slot + 1) * ABLK)
            keys_ref[block, :, here] = near_keys[:, pl.ds(start, ABLK)]
            values_ref[block, :, here, :size] = near_values[:, pl.ds(start, ABLK)]

    def departure(block):
        at = pl.ds(block * VBLK, VBLK)
        return pltpu.make_async_copy(turned.at[block], out_ref.at[at], sems.at[block])

    units = [(block, first) for block in range(blocks) for first in range(0, heads, group)]
    scores, weights = {}, {}
    for step in range(len(units) + 2):
        if step < len(units):
            block, first = units[step]
            if first == 0:
                prepare(block)
            live = column < counts_ref[block] * ABLK
            scores[step] = [
                jnp.where(live, scores_of(queries_ref[block, head], keys_ref[block, head]), LOWEST)
                for head in range(first, first + group)
            ]
        if 1 <= step <= len(units):
            now = jnp.stack(scores.pop(step - 1))
            top = jnp.max(now, axis=2, keepdims=True)
            weights[step - 1] = jnp.exp2((now - top) * factor).astype(jnp.bfloat16)
        if step >= 2:
            block, first = units[step - 2]
            now = weights.pop(step - 2)
            for i in range(group):
                summed = jnp.dot(
                    now[i], values_ref[block, first + i], preferred_element_type=jnp.float32
                )
                result_ref[block, first + i] = (summed[:, :size] / summed[:, size:]).astype(
                    jnp.bfloat16
                )
            if first + group == heads:
                turned[block] = jnp.swapaxes(result_ref[block], 0, 1)
                departure(block).start()
    for block in range(blocks):
        departure(block).wait()


def video(video_q, own, core, chip, pairs, counts, where, scale):
    total, heads, size = video_q.shape
    rows = own.shape[1] // 2
    blocks, slots = pairs.shape
    work = total * heads * slots * ABLK
    in_smem = pl.BlockSpec(memory_space=pltpu.SMEM)
    in_vmem = pl.BlockSpec(memory_space=pltpu.VMEM)
    return pl.pallas_call(
        functools.partial(video_kernel, scale, 4),
        in_specs=[in_smem] * 3 + [in_vmem] * 4,
        out_specs=pl.BlockSpec(memory_space=pltpu.HBM),
        out_shape=pltpu.HBM(video_q.shape, jnp.bfloat16),
        scratch_shapes=[
            pltpu.VMEM((heads, 3 * rows, size), jnp.bfloat16),
            pltpu.VMEM((heads, 3 * rows, size), jnp.bfloat16),
            pltpu.VMEM((blocks, heads, slots * ABLK, size), jnp.bfloat16),
            pltpu.VMEM((blocks, heads, slots * ABLK, 2 * size), jnp.bfloat16),
            pltpu.VMEM((blocks, heads, VBLK, size), jnp.bfloat16),
            pltpu.VMEM((blocks, heads, VBLK, size), jnp.bfloat16),
            pltpu.VMEM((blocks, VBLK, heads, size), jnp.bfloat16),
            pltpu.SemaphoreType.DMA((blocks,)),
        ],
        compiler_params=params(),
        cost_estimate=pl.CostEstimate(
            flops=4 * work * size, bytes_accessed=32 * total * heads * size, transcendentals=work
        ),
        name="video",
    )(pairs, counts, where, video_q, own, core, chip)


def local(audio_qkv, video_q, pairs, counts):
    devices = lax.axis_size("seq")
    rows, unused, heads, size = audio_qkv.shape
    bands = devices // heads
    band_rows = rows // bands
    scale = size ** (-0.5)
    send, kv = arrange(audio_qkv)
    core_pairs = [(i, i ^ 1) for i in range(devices)]
    chip_pairs = [(i, ((i + 1) ^ 1) - 1) for i in range(1, devices - 1)]

    chip = lax.ppermute(kv, "seq", chip_pairs)

    order = [(devices // 4 + 1 - p) % devices for p in range(devices)]

    def exchange(value):
        return lax.all_to_all(
            value, "seq", split_axis=0, concat_axis=0, tiled=True, axis_index_groups=[order]
        )

    core = lax.ppermute(kv, "seq", core_pairs)
    me = lax.axis_index("seq")
    odd = me & 1
    where = jnp.stack([(me - 1) * (rows // ABLK), 2 * (1 - odd) * rows, 2 * odd * rows])
    video_cross = video(
        video_q, kv, core, chip, pairs, counts, where.astype(jnp.int32), scale
    )
    if bands == 1:
        head_out = attend(exchange(send), scale)
    else:
        queries = exchange(send[:, :, :PIECE].reshape(devices, band_rows, size))
        spread = jnp.broadcast_to(kv[:, None], (heads, bands, 2 * rows, size))
        recv = exchange(spread.reshape(devices, 2 * rows, size))
        head_out = attend_band(queries, recv, scale)
    returned, video_cross = lax.optimization_barrier((exchange(head_out), video_cross))
    audio_attn = collect(returned.reshape(heads, rows, size))
    return audio_attn, video_cross


def solution(mesh):
    in_specs = (
        P(("groups", "seq"), None, None, None),
        P(("groups", "seq"), None, None),
        P(("groups", "seq"), None),
        P(("groups", "seq")),
    )
    out_specs = (P(("groups", "seq"), None, None), P(("groups", "seq"), None, None))
    return jax.shard_map(local, mesh=mesh, in_specs=in_specs, out_specs=out_specs, check_vma=False)
```

```python
import functools

import jax
import jax.numpy as jnp
from jax import lax
from jax.experimental import pallas as pl
from jax.experimental.pallas import tpu as pltpu
from jax.sharding import PartitionSpec as P

ABLK = 32
VBLK = 128
LOG2E = 1.4426950408889634
LOWEST = -1e30
VMEM_LIMIT = 48 * 1024 * 1024


def params():
    return pltpu.CompilerParams(vmem_limit_bytes=VMEM_LIMIT)


PIECE = 16


def arrange_kernel(pieces, qkv_ref, send_ref, kv_ref, came, turned, in_sems, out_sems):
    rows = pieces * PIECE
    arrivals = [
        pltpu.make_async_copy(
            qkv_ref.at[pl.ds(piece * PIECE, PIECE)], came.at[piece], in_sems.at[piece]
        )
        for piece in range(pieces)
    ]
    for arrival in arrivals:
        arrival.start()
    departures = []
    for piece, arrival in enumerate(arrivals):
        arrival.wait()
        for part in range(3):
            by_head = jnp.swapaxes(came[piece, :, part], 0, 1)
            turned[piece, :, part * PIECE : (part + 1) * PIECE] = by_head
            if part:
                at = (part - 1) * rows + piece * PIECE
                kv_ref[:, at : at + PIECE] = by_head
        departure = pltpu.make_async_copy(
            turned.at[piece], send_ref.at[:, piece], out_sems.at[piece]
        )
        departure.start()
        departures.append(departure)
    for departure in departures:
        departure.wait()


def arrange(audio_qkv):
    rows, parts, heads, size = audio_qkv.shape
    dtype = audio_qkv.dtype
    pieces = rows // PIECE
    return pl.pallas_call(
        functools.partial(arrange_kernel, pieces),
        in_specs=[pl.BlockSpec(memory_space=pltpu.HBM)],
        out_specs=(
            pl.BlockSpec(memory_space=pltpu.HBM),
            pl.BlockSpec(memory_space=pltpu.VMEM),
        ),
        out_shape=(
            pltpu.HBM((heads, pieces, parts * PIECE, size), dtype),
            jax.ShapeDtypeStruct((heads, 2 * rows, size), dtype),
        ),
        scratch_shapes=[
            pltpu.VMEM((pieces, PIECE, parts, heads, size), dtype),
            pltpu.VMEM((pieces, heads, parts * PIECE, size), dtype),
            pltpu.SemaphoreType.DMA((pieces,)),
            pltpu.SemaphoreType.DMA((pieces,)),
        ],
        compiler_params=params(),
        name="arrange",
    )(pltpu.with_memory_space_constraint(audio_qkv, pltpu.HBM))


def scores_of(queries, keys):
    return lax.dot_general(
        queries, keys, (((1,), (1,)), ((), ())), preferred_element_type=jnp.float32
    )


def attend_kernel(scale, recv_ref, out_ref, held, sems):
    sources, pieces, unused, size = recv_ref.shape
    total = sources * pieces * PIECE
    chunk = total // sems.shape[0]
    group = chunk // (pieces * PIECE)
    factor = scale * LOG2E
    keys = recv_ref[:, :, PIECE : 2 * PIECE].reshape(total, size)
    values = recv_ref[:, :, 2 * PIECE :].reshape(total, size)
    chunks = total // chunk
    scores, weights, sums, departures = {}, {}, {}, []
    for step in range(chunks + 2):
        if step < chunks:
            first = step * group
            queries = recv_ref[first : first + group, :, :PIECE].reshape(chunk, size)
            scores[step] = scores_of(queries, keys)
        if 0 <= step - 1 < chunks:
            now = scores.pop(step - 1)
            top = jnp.max(now, axis=1, keepdims=True)
            exact = jnp.exp2((now - top) * factor)
            sums[step - 1] = jnp.sum(exact, axis=1, keepdims=True)
            weights[step - 1] = exact.astype(jnp.bfloat16)
        if step >= 2:
            summed = jnp.dot(
                weights.pop(step - 2), values, preferred_element_type=jnp.float32
            )
            result = (summed / sums.pop(step - 2)).astype(jnp.bfloat16)
            at = (step - 2) * group
            held[at : at + group] = result.reshape(group, pieces * PIECE, size)
            departure = pltpu.make_async_copy(
                held.at[pl.ds(at, group)], out_ref.at[pl.ds(at, group)], sems.at[step - 2]
            )
            departure.start()
            departures.append(departure)
    for departure in departures:
        departure.wait()


def attend(recv, scale):
    sources, pieces, unused, size = recv.shape
    rows = pieces * PIECE
    total = sources * rows
    return pl.pallas_call(
        functools.partial(attend_kernel, scale),
        in_specs=[pl.BlockSpec(memory_space=pltpu.VMEM)],
        out_specs=pl.BlockSpec(memory_space=pltpu.HBM),
        out_shape=pltpu.HBM((sources, rows, size), jnp.bfloat16),
        scratch_shapes=[
            pltpu.VMEM((sources, rows, size), jnp.bfloat16),
            pltpu.SemaphoreType.DMA((total // 128,)),
        ],
        compiler_params=params(),
        cost_estimate=pl.CostEstimate(
            flops=4 * total * total * size, bytes_accessed=8 * total * size,
            transcendentals=total * total,
        ),
        name="attend",
    )(recv)


def attend_band_kernel(query_rows, scale, query_ref, recv_ref, out_ref):
    sources, both, size = recv_ref.shape
    rows = both // 2
    group = 256 // query_rows
    factor = scale * LOG2E
    for first in range(0, sources, group):
        queries = query_ref[first : first + group].reshape(group * query_rows, size)

        def advance(step, state):
            top, total, summed = state
            at = pl.ds(step * PIECE, PIECE)
            keys = recv_ref[at, :rows].reshape(PIECE * rows, size)
            values = recv_ref[at, rows:].reshape(PIECE * rows, size)
            scores = scores_of(queries, keys)
            new_top = jnp.maximum(top, jnp.max(scores, axis=1, keepdims=True))
            weights = jnp.exp2((scores - new_top) * factor)
            rescale = jnp.exp2((top - new_top) * factor)
            new_total = total * rescale + jnp.sum(weights, axis=1, keepdims=True)
            new_summed = summed * rescale + jnp.dot(
                weights.astype(jnp.bfloat16), values, preferred_element_type=jnp.float32
            )
            return new_top, new_total, new_summed

        start = (
            jnp.full((group * query_rows, 1), LOWEST, jnp.float32),
            jnp.zeros((group * query_rows, 1), jnp.float32),
            jnp.zeros((group * query_rows, size), jnp.float32),
        )
        state = lax.fori_loop(0, sources // PIECE, advance, start)
        result = (state[2] / state[1]).astype(jnp.bfloat16)
        out_ref[first : first + group] = result.reshape(group, query_rows, size)


def attend_band(queries, recv, scale):
    return pl.pallas_call(
        functools.partial(attend_band_kernel, queries.shape[1], scale),
        out_shape=jax.ShapeDtypeStruct(queries.shape, jnp.bfloat16),
        compiler_params=params(),
        name="attend_band",
    )(queries, recv)


def collect_kernel(by_head_ref, out_ref, turned, sems):
    departures = []
    for piece in range(by_head_ref.shape[1] // PIECE):
        at = pl.ds(piece * PIECE, PIECE)
        turned[at] = jnp.swapaxes(by_head_ref[:, at], 0, 1)
        departure = pltpu.make_async_copy(turned.at[at], out_ref.at[at], sems.at[piece])
        departure.start()
        departures.append(departure)
    for departure in departures:
        departure.wait()


def collect(by_head):
    heads, rows, size = by_head.shape
    return pl.pallas_call(
        collect_kernel,
        in_specs=[pl.BlockSpec(memory_space=pltpu.VMEM)],
        out_specs=pl.BlockSpec(memory_space=pltpu.HBM),
        out_shape=pltpu.HBM((rows, heads, size), by_head.dtype),
        scratch_shapes=[
            pltpu.VMEM((rows, heads, size), by_head.dtype),
            pltpu.SemaphoreType.DMA((rows // PIECE,)),
        ],
        compiler_params=params(),
        name="collect",
    )(by_head)


def video_kernel(
    scale, group, pairs_ref, counts_ref, where_ref, video_ref, own_ref, core_ref, chip_ref, out_ref,
    near_keys, near_values, keys_ref, values_ref, queries_ref, result_ref, turned, sems,
):
    heads, both, size = own_ref.shape
    rows = both // 2
    blocks, slots = pairs_ref.shape
    for ref, place in ((own_ref, rows), (core_ref, where_ref[1]), (chip_ref, where_ref[2])):
        at = pl.ds(pl.multiple_of(place, rows), rows)
        near_keys[:, at] = ref[:, :rows]
        near_values[:, at] = ref[:, rows:]
    values_ref[:, :, :, size:] = jnp.ones((blocks, heads, slots * ABLK, size), jnp.bfloat16)
    column = lax.broadcasted_iota(jnp.int32, (VBLK, slots * ABLK), 1)
    factor = scale * LOG2E

    def prepare(block):
        queries_ref[block] = jnp.swapaxes(video_ref[block * VBLK : (block + 1) * VBLK], 0, 1)
        for slot in range(slots):
            start = pl.multiple_of((pairs_ref[block, slot] - where_ref[0]) * ABLK, ABLK)
            here = slice(slot * ABLK, (slot + 1) * ABLK)
            keys_ref[block, :, here] = near_keys[:, pl.ds(start, ABLK)]
            values_ref[block, :, here, :size] = near_values[:, pl.ds(start, ABLK)]

    def departure(block):
        at = pl.ds(block * VBLK, VBLK)
        return pltpu.make_async_copy(turned.at[block], out_ref.at[at], sems.at[block])

    units = [(block, first) for block in range(blocks) for first in range(0, heads, group)]
    scores, weights = {}, {}
    for step in range(len(units) + 2):
        if step < len(units):
            block, first = units[step]
            if first == 0:
                prepare(block)
            live = column < counts_ref[block] * ABLK
            scores[step] = [
                jnp.where(live, scores_of(queries_ref[block, head], keys_ref[block, head]), LOWEST)
                for head in range(first, first + group)
            ]
        if 1 <= step <= len(units):
            now = jnp.stack(scores.pop(step - 1))
            top = jnp.max(now, axis=2, keepdims=True)
            weights[step - 1] = jnp.exp2((now - top) * factor).astype(jnp.bfloat16)
        if step >= 2:
            block, first = units[step - 2]
            now = weights.pop(step - 2)
            for i in range(group):
                summed = jnp.dot(
                    now[i], values_ref[block, first + i], preferred_element_type=jnp.float32
                )
                result_ref[block, first + i] = (summed[:, :size] / summed[:, size:]).astype(
                    jnp.bfloat16
                )
            if first + group == heads:
                turned[block] = jnp.swapaxes(result_ref[block], 0, 1)
                departure(block).start()
    for block in range(blocks):
        departure(block).wait()


def video(video_q, own, core, chip, pairs, counts, where, scale):
    total, heads, size = video_q.shape
    rows = own.shape[1] // 2
    blocks, slots = pairs.shape
    work = total * heads * slots * ABLK
    in_smem = pl.BlockSpec(memory_space=pltpu.SMEM)
    in_vmem = pl.BlockSpec(memory_space=pltpu.VMEM)
    return pl.pallas_call(
        functools.partial(video_kernel, scale, 4),
        in_specs=[in_smem] * 3 + [in_vmem] * 4,
        out_specs=pl.BlockSpec(memory_space=pltpu.HBM),
        out_shape=pltpu.HBM(video_q.shape, jnp.bfloat16),
        scratch_shapes=[
            pltpu.VMEM((heads, 3 * rows, size), jnp.bfloat16),
            pltpu.VMEM((heads, 3 * rows, size), jnp.bfloat16),
            pltpu.VMEM((blocks, heads, slots * ABLK, size), jnp.bfloat16),
            pltpu.VMEM((blocks, heads, slots * ABLK, 2 * size), jnp.bfloat16),
            pltpu.VMEM((blocks, heads, VBLK, size), jnp.bfloat16),
            pltpu.VMEM((blocks, heads, VBLK, size), jnp.bfloat16),
            pltpu.VMEM((blocks, VBLK, heads, size), jnp.bfloat16),
            pltpu.SemaphoreType.DMA((blocks,)),
        ],
        compiler_params=params(),
        cost_estimate=pl.CostEstimate(
            flops=4 * work * size, bytes_accessed=32 * total * heads * size, transcendentals=work
        ),
        name="video",
    )(pairs, counts, where, video_q, own, core, chip)


def local(audio_qkv, video_q, pairs, counts):
    devices = lax.axis_size("seq")
    rows, unused, heads, size = audio_qkv.shape
    bands = devices // heads
    band_rows = rows // bands
    scale = size ** (-0.5)
    send, kv = arrange(audio_qkv)
    core_pairs = [(i, i ^ 1) for i in range(devices)]
    chip_pairs = [(i, ((i + 1) ^ 1) - 1) for i in range(1, devices - 1)]

    chip = lax.ppermute(kv, "seq", chip_pairs)

    order = [(devices // 2 + 1 - p) % devices for p in range(devices)]

    def exchange(value):
        return lax.all_to_all(
            value, "seq", split_axis=0, concat_axis=0, tiled=True, axis_index_groups=[order]
        )

    core = lax.ppermute(kv, "seq", core_pairs)
    me = lax.axis_index("seq")
    odd = me & 1
    where = jnp.stack([(me - 1) * (rows // ABLK), 2 * (1 - odd) * rows, 2 * odd * rows])
    video_cross = video(
        video_q, kv, core, chip, pairs, counts, where.astype(jnp.int32), scale
    )
    if bands == 1:
        head_out = attend(exchange(send), scale)
    else:
        queries = exchange(send[:, :, :PIECE].reshape(devices, band_rows, size))
        spread = jnp.broadcast_to(kv[:, None], (heads, bands, 2 * rows, size))
        recv = exchange(spread.reshape(devices, 2 * rows, size))
        head_out = attend_band(queries, recv, scale)
    returned, video_cross = lax.optimization_barrier((exchange(head_out), video_cross))
    audio_attn = collect(returned.reshape(heads, rows, size))
    return audio_attn, video_cross


def solution(mesh):
    in_specs = (
        P(("groups", "seq"), None, None, None),
        P(("groups", "seq"), None, None),
        P(("groups", "seq"), None),
        P(("groups", "seq")),
    )
    out_specs = (P(("groups", "seq"), None, None), P(("groups", "seq"), None, None))
    return jax.shard_map(local, mesh=mesh, in_specs=in_specs, out_specs=out_specs, check_vma=False)
```

```python
import functools

import jax
import jax.numpy as jnp
from jax import lax
from jax.experimental import pallas as pl
from jax.experimental.pallas import tpu as pltpu
from jax.sharding import PartitionSpec as P

ABLK = 32
VBLK = 128
LOG2E = 1.4426950408889634
LOWEST = -1e30
VMEM_LIMIT = 48 * 1024 * 1024


def params():
    return pltpu.CompilerParams(vmem_limit_bytes=VMEM_LIMIT)


PIECE = 16


def arrange_kernel(pieces, qkv_ref, send_ref, kv_ref, came, turned, in_sems, out_sems):
    rows = pieces * PIECE
    arrivals = [
        pltpu.make_async_copy(
            qkv_ref.at[pl.ds(piece * PIECE, PIECE)], came.at[piece], in_sems.at[piece]
        )
        for piece in range(pieces)
    ]
    for arrival in arrivals:
        arrival.start()
    departures = []
    for piece, arrival in enumerate(arrivals):
        arrival.wait()
        for part in range(3):
            by_head = jnp.swapaxes(came[piece, :, part], 0, 1)
            turned[piece, :, part * PIECE : (part + 1) * PIECE] = by_head
        departure = pltpu.make_async_copy(
            turned.at[piece], send_ref.at[:, piece], out_sems.at[piece]
        )
        departure.start()
        departures.append(departure)
    for piece in range(pieces):
        for half in range(2):
            at = half * rows + piece * PIECE
            part = (half + 1) * PIECE
            kv_ref[:, at : at + PIECE] = turned[piece, :, part : part + PIECE]
    for departure in departures:
        departure.wait()


def arrange(audio_qkv):
    rows, parts, heads, size = audio_qkv.shape
    dtype = audio_qkv.dtype
    pieces = rows // PIECE
    return pl.pallas_call(
        functools.partial(arrange_kernel, pieces),
        in_specs=[pl.BlockSpec(memory_space=pltpu.HBM)],
        out_specs=(
            pl.BlockSpec(memory_space=pltpu.HBM),
            pl.BlockSpec(memory_space=pltpu.VMEM),
        ),
        out_shape=(
            pltpu.HBM((heads, pieces, parts * PIECE, size), dtype),
            jax.ShapeDtypeStruct((heads, 2 * rows, size), dtype),
        ),
        scratch_shapes=[
            pltpu.VMEM((pieces, PIECE, parts, heads, size), dtype),
            pltpu.VMEM((pieces, heads, parts * PIECE, size), dtype),
            pltpu.SemaphoreType.DMA((pieces,)),
            pltpu.SemaphoreType.DMA((pieces,)),
        ],
        compiler_params=params(),
        name="arrange",
    )(pltpu.with_memory_space_constraint(audio_qkv, pltpu.HBM))


def scores_of(queries, keys):
    return lax.dot_general(
        queries, keys, (((1,), (1,)), ((), ())), preferred_element_type=jnp.float32
    )


def attend_kernel(scale, recv_ref, out_ref, held, sems):
    sources, pieces, unused, size = recv_ref.shape
    total = sources * pieces * PIECE
    chunk = total // sems.shape[0]
    group = chunk // (pieces * PIECE)
    factor = scale * LOG2E
    keys = recv_ref[:, :, PIECE : 2 * PIECE].reshape(total, size)
    values = recv_ref[:, :, 2 * PIECE :].reshape(total, size)
    chunks = total // chunk
    scores, weights, sums, departures = {}, {}, {}, []
    for step in range(chunks + 2):
        if step < chunks:
            first = step * group
            queries = recv_ref[first : first + group, :, :PIECE].reshape(chunk, size)
            scores[step] = scores_of(queries, keys)
        if 0 <= step - 1 < chunks:
            now = scores.pop(step - 1)
            top = jnp.max(now, axis=1, keepdims=True)
            exact = jnp.exp2((now - top) * factor)
            sums[step - 1] = jnp.sum(exact, axis=1, keepdims=True)
            weights[step - 1] = exact.astype(jnp.bfloat16)
        if step >= 2:
            summed = jnp.dot(
                weights.pop(step - 2), values, preferred_element_type=jnp.float32
            )
            result = (summed / sums.pop(step - 2)).astype(jnp.bfloat16)
            at = (step - 2) * group
            held[at : at + group] = result.reshape(group, pieces * PIECE, size)
            departure = pltpu.make_async_copy(
                held.at[pl.ds(at, group)], out_ref.at[pl.ds(at, group)], sems.at[step - 2]
            )
            departure.start()
            departures.append(departure)
    for departure in departures:
        departure.wait()


def attend(recv, scale):
    sources, pieces, unused, size = recv.shape
    rows = pieces * PIECE
    total = sources * rows
    return pl.pallas_call(
        functools.partial(attend_kernel, scale),
        in_specs=[pl.BlockSpec(memory_space=pltpu.VMEM)],
        out_specs=pl.BlockSpec(memory_space=pltpu.HBM),
        out_shape=pltpu.HBM((sources, rows, size), jnp.bfloat16),
        scratch_shapes=[
            pltpu.VMEM((sources, rows, size), jnp.bfloat16),
            pltpu.SemaphoreType.DMA((total // 128,)),
        ],
        compiler_params=params(),
        cost_estimate=pl.CostEstimate(
            flops=4 * total * total * size, bytes_accessed=8 * total * size,
            transcendentals=total * total,
        ),
        name="attend",
    )(recv)


def attend_band_kernel(query_rows, scale, query_ref, recv_ref, out_ref):
    sources, both, size = recv_ref.shape
    rows = both // 2
    group = 256 // query_rows
    factor = scale * LOG2E
    for first in range(0, sources, group):
        queries = query_ref[first : first + group].reshape(group * query_rows, size)

        def advance(step, state):
            top, total, summed = state
            at = pl.ds(step * PIECE, PIECE)
            keys = recv_ref[at, :rows].reshape(PIECE * rows, size)
            values = recv_ref[at, rows:].reshape(PIECE * rows, size)
            scores = scores_of(queries, keys)
            new_top = jnp.maximum(top, jnp.max(scores, axis=1, keepdims=True))
            weights = jnp.exp2((scores - new_top) * factor)
            rescale = jnp.exp2((top - new_top) * factor)
            new_total = total * rescale + jnp.sum(weights, axis=1, keepdims=True)
            new_summed = summed * rescale + jnp.dot(
                weights.astype(jnp.bfloat16), values, preferred_element_type=jnp.float32
            )
            return new_top, new_total, new_summed

        start = (
            jnp.full((group * query_rows, 1), LOWEST, jnp.float32),
            jnp.zeros((group * query_rows, 1), jnp.float32),
            jnp.zeros((group * query_rows, size), jnp.float32),
        )
        state = lax.fori_loop(0, sources // PIECE, advance, start)
        result = (state[2] / state[1]).astype(jnp.bfloat16)
        out_ref[first : first + group] = result.reshape(group, query_rows, size)


def attend_band(queries, recv, scale):
    return pl.pallas_call(
        functools.partial(attend_band_kernel, queries.shape[1], scale),
        out_shape=jax.ShapeDtypeStruct(queries.shape, jnp.bfloat16),
        compiler_params=params(),
        name="attend_band",
    )(queries, recv)


def collect_kernel(by_head_ref, out_ref, turned, sems):
    departures = []
    for piece in range(by_head_ref.shape[1] // PIECE):
        at = pl.ds(piece * PIECE, PIECE)
        turned[at] = jnp.swapaxes(by_head_ref[:, at], 0, 1)
        departure = pltpu.make_async_copy(turned.at[at], out_ref.at[at], sems.at[piece])
        departure.start()
        departures.append(departure)
    for departure in departures:
        departure.wait()


def collect(by_head):
    heads, rows, size = by_head.shape
    return pl.pallas_call(
        collect_kernel,
        in_specs=[pl.BlockSpec(memory_space=pltpu.VMEM)],
        out_specs=pl.BlockSpec(memory_space=pltpu.HBM),
        out_shape=pltpu.HBM((rows, heads, size), by_head.dtype),
        scratch_shapes=[
            pltpu.VMEM((rows, heads, size), by_head.dtype),
            pltpu.SemaphoreType.DMA((rows // PIECE,)),
        ],
        compiler_params=params(),
        name="collect",
    )(by_head)


def video_kernel(
    scale, group, pairs_ref, counts_ref, where_ref, video_ref, own_ref, core_ref, chip_ref, out_ref,
    near_keys, near_values, keys_ref, values_ref, queries_ref, result_ref, turned, sems,
):
    heads, both, size = own_ref.shape
    rows = both // 2
    blocks, slots = pairs_ref.shape
    for ref, place in ((own_ref, rows), (core_ref, where_ref[1]), (chip_ref, where_ref[2])):
        at = pl.ds(pl.multiple_of(place, rows), rows)
        near_keys[:, at] = ref[:, :rows]
        near_values[:, at] = ref[:, rows:]
    values_ref[:, :, :, size:] = jnp.ones((blocks, heads, slots * ABLK, size), jnp.bfloat16)
    column = lax.broadcasted_iota(jnp.int32, (VBLK, slots * ABLK), 1)
    factor = scale * LOG2E

    def prepare(block):
        queries_ref[block] = jnp.swapaxes(video_ref[block * VBLK : (block + 1) * VBLK], 0, 1)
        for slot in range(slots):
            start = pl.multiple_of((pairs_ref[block, slot] - where_ref[0]) * ABLK, ABLK)
            here = slice(slot * ABLK, (slot + 1) * ABLK)
            keys_ref[block, :, here] = near_keys[:, pl.ds(start, ABLK)]
            values_ref[block, :, here, :size] = near_values[:, pl.ds(start, ABLK)]

    def departure(block):
        at = pl.ds(block * VBLK, VBLK)
        return pltpu.make_async_copy(turned.at[block], out_ref.at[at], sems.at[block])

    units = [(block, first) for block in range(blocks) for first in range(0, heads, group)]
    scores, weights = {}, {}
    for step in range(len(units) + 2):
        if step < len(units):
            block, first = units[step]
            if first == 0:
                prepare(block)
            live = column < counts_ref[block] * ABLK
            scores[step] = [
                jnp.where(live, scores_of(queries_ref[block, head], keys_ref[block, head]), LOWEST)
                for head in range(first, first + group)
            ]
        if 1 <= step <= len(units):
            now = jnp.stack(scores.pop(step - 1))
            top = jnp.max(now, axis=2, keepdims=True)
            weights[step - 1] = jnp.exp2((now - top) * factor).astype(jnp.bfloat16)
        if step >= 2:
            block, first = units[step - 2]
            now = weights.pop(step - 2)
            for i in range(group):
                summed = jnp.dot(
                    now[i], values_ref[block, first + i], preferred_element_type=jnp.float32
                )
                result_ref[block, first + i] = (summed[:, :size] / summed[:, size:]).astype(
                    jnp.bfloat16
                )
            if first + group == heads:
                turned[block] = jnp.swapaxes(result_ref[block], 0, 1)
                departure(block).start()
    for block in range(blocks):
        departure(block).wait()


def video(video_q, own, core, chip, pairs, counts, where, scale):
    total, heads, size = video_q.shape
    rows = own.shape[1] // 2
    blocks, slots = pairs.shape
    work = total * heads * slots * ABLK
    in_smem = pl.BlockSpec(memory_space=pltpu.SMEM)
    in_vmem = pl.BlockSpec(memory_space=pltpu.VMEM)
    return pl.pallas_call(
        functools.partial(video_kernel, scale, 4),
        in_specs=[in_smem] * 3 + [in_vmem] * 4,
        out_specs=pl.BlockSpec(memory_space=pltpu.HBM),
        out_shape=pltpu.HBM(video_q.shape, jnp.bfloat16),
        scratch_shapes=[
            pltpu.VMEM((heads, 3 * rows, size), jnp.bfloat16),
            pltpu.VMEM((heads, 3 * rows, size), jnp.bfloat16),
            pltpu.VMEM((blocks, heads, slots * ABLK, size), jnp.bfloat16),
            pltpu.VMEM((blocks, heads, slots * ABLK, 2 * size), jnp.bfloat16),
            pltpu.VMEM((blocks, heads, VBLK, size), jnp.bfloat16),
            pltpu.VMEM((blocks, heads, VBLK, size), jnp.bfloat16),
            pltpu.VMEM((blocks, VBLK, heads, size), jnp.bfloat16),
            pltpu.SemaphoreType.DMA((blocks,)),
        ],
        compiler_params=params(),
        cost_estimate=pl.CostEstimate(
            flops=4 * work * size, bytes_accessed=32 * total * heads * size, transcendentals=work
        ),
        name="video",
    )(pairs, counts, where, video_q, own, core, chip)


def local(audio_qkv, video_q, pairs, counts):
    devices = lax.axis_size("seq")
    rows, unused, heads, size = audio_qkv.shape
    bands = devices // heads
    band_rows = rows // bands
    scale = size ** (-0.5)
    send, kv = arrange(audio_qkv)
    core_pairs = [(i, i ^ 1) for i in range(devices)]
    chip_pairs = [(i, ((i + 1) ^ 1) - 1) for i in range(1, devices - 1)]

    chip = lax.ppermute(kv, "seq", chip_pairs)

    order = [(devices - 1 - devices // 2 - p) % devices for p in range(devices)]

    def exchange(value):
        return lax.all_to_all(
            value, "seq", split_axis=0, concat_axis=0, tiled=True, axis_index_groups=[order]
        )

    core = lax.ppermute(kv, "seq", core_pairs)
    me = lax.axis_index("seq")
    odd = me & 1
    where = jnp.stack([(me - 1) * (rows // ABLK), 2 * (1 - odd) * rows, 2 * odd * rows])
    video_cross = video(
        video_q, kv, core, chip, pairs, counts, where.astype(jnp.int32), scale
    )
    if bands == 1:
        head_out = attend(exchange(send), scale)
    else:
        queries = exchange(send[:, :, :PIECE].reshape(devices, band_rows, size))
        spread = jnp.broadcast_to(kv[:, None], (heads, bands, 2 * rows, size))
        recv = exchange(spread.reshape(devices, 2 * rows, size))
        head_out = attend_band(queries, recv, scale)
    returned, video_cross = lax.optimization_barrier((exchange(head_out), video_cross))
    audio_attn = collect(returned.reshape(heads, rows, size))
    return audio_attn, video_cross


def solution(mesh):
    in_specs = (
        P(("groups", "seq"), None, None, None),
        P(("groups", "seq"), None, None),
        P(("groups", "seq"), None),
        P(("groups", "seq")),
    )
    out_specs = (P(("groups", "seq"), None, None), P(("groups", "seq"), None, None))
    return jax.shard_map(local, mesh=mesh, in_specs=in_specs, out_specs=out_specs, check_vma=False)
```

```python
import functools

import jax
import jax.numpy as jnp
from jax import lax
from jax.experimental import pallas as pl
from jax.experimental.pallas import tpu as pltpu
from jax.sharding import PartitionSpec as P

ABLK = 32
VBLK = 128
LOG2E = 1.4426950408889634
LOWEST = -1e30
VMEM_LIMIT = 48 * 1024 * 1024


def params():
    return pltpu.CompilerParams(vmem_limit_bytes=VMEM_LIMIT)


PIECE = 16


def arrange_kernel(pieces, qkv_ref, send_ref, kv_ref, came, turned, in_sems, out_sems):
    rows = pieces * PIECE
    arrivals = [
        pltpu.make_async_copy(
            qkv_ref.at[pl.ds(piece * PIECE, PIECE)], came.at[piece], in_sems.at[piece]
        )
        for piece in range(pieces)
    ]
    for arrival in arrivals:
        arrival.start()
    departures = []
    for piece, arrival in enumerate(arrivals):
        arrival.wait()
        for part in range(3):
            by_head = jnp.swapaxes(came[piece, :, part], 0, 1)
            turned[piece, :, part * PIECE : (part + 1) * PIECE] = by_head
            if part:
                at = (part - 1) * rows + piece * PIECE
                kv_ref[:, at : at + PIECE] = by_head
        departure = pltpu.make_async_copy(
            turned.at[piece], send_ref.at[:, piece], out_sems.at[piece]
        )
        departure.start()
        departures.append(departure)
    for departure in departures:
        departure.wait()


def arrange(audio_qkv):
    rows, parts, heads, size = audio_qkv.shape
    dtype = audio_qkv.dtype
    pieces = rows // PIECE
    return pl.pallas_call(
        functools.partial(arrange_kernel, pieces),
        in_specs=[pl.BlockSpec(memory_space=pltpu.HBM)],
        out_specs=(
            pl.BlockSpec(memory_space=pltpu.HBM),
            pl.BlockSpec(memory_space=pltpu.VMEM),
        ),
        out_shape=(
            pltpu.HBM((heads, pieces, parts * PIECE, size), dtype),
            jax.ShapeDtypeStruct((heads, 2 * rows, size), dtype),
        ),
        scratch_shapes=[
            pltpu.VMEM((pieces, PIECE, parts, heads, size), dtype),
            pltpu.VMEM((pieces, heads, parts * PIECE, size), dtype),
            pltpu.SemaphoreType.DMA((pieces,)),
            pltpu.SemaphoreType.DMA((pieces,)),
        ],
        compiler_params=params(),
        name="arrange",
    )(pltpu.with_memory_space_constraint(audio_qkv, pltpu.HBM))


def scores_of(queries, keys):
    return lax.dot_general(
        queries, keys, (((1,), (1,)), ((), ())), preferred_element_type=jnp.float32
    )


def attend_kernel(scale, recv_ref, out_ref, held, sems):
    sources, pieces, unused, size = recv_ref.shape
    total = sources * pieces * PIECE
    chunk = total // sems.shape[0]
    group = chunk // (pieces * PIECE)
    factor = scale * LOG2E
    keys = recv_ref[:, :, PIECE : 2 * PIECE].reshape(total, size)
    values = recv_ref[:, :, 2 * PIECE :].reshape(total, size)
    chunks = total // chunk
    scores, weights, sums, departures = {}, {}, {}, []
    for step in range(chunks + 2):
        if step < chunks:
            first = step * group
            queries = recv_ref[first : first + group, :, :PIECE].reshape(chunk, size)
            scores[step] = scores_of(queries, keys)
        if 0 <= step - 1 < chunks:
            now = scores.pop(step - 1)
            top = jnp.max(now, axis=1, keepdims=True)
            exact = jnp.exp2((now - top) * factor)
            sums[step - 1] = jnp.sum(exact, axis=1, keepdims=True)
            weights[step - 1] = exact.astype(jnp.bfloat16)
        if step >= 2:
            summed = jnp.dot(
                weights.pop(step - 2), values, preferred_element_type=jnp.float32
            )
            result = (summed / sums.pop(step - 2)).astype(jnp.bfloat16)
            at = (step - 2) * group
            held[at : at + group] = result.reshape(group, pieces * PIECE, size)
            departure = pltpu.make_async_copy(
                held.at[pl.ds(at, group)], out_ref.at[pl.ds(at, group)], sems.at[step - 2]
            )
            departure.start()
            departures.append(departure)
    for departure in departures:
        departure.wait()


def attend(recv, scale):
    sources, pieces, unused, size = recv.shape
    rows = pieces * PIECE
    total = sources * rows
    return pl.pallas_call(
        functools.partial(attend_kernel, scale),
        in_specs=[pl.BlockSpec(memory_space=pltpu.VMEM)],
        out_specs=pl.BlockSpec(memory_space=pltpu.HBM),
        out_shape=pltpu.HBM((sources, rows, size), jnp.bfloat16),
        scratch_shapes=[
            pltpu.VMEM((sources, rows, size), jnp.bfloat16),
            pltpu.SemaphoreType.DMA((total // 128,)),
        ],
        compiler_params=params(),
        cost_estimate=pl.CostEstimate(
            flops=4 * total * total * size, bytes_accessed=8 * total * size,
            transcendentals=total * total,
        ),
        name="attend",
    )(recv)


def attend_band_kernel(query_rows, scale, query_ref, recv_ref, out_ref):
    sources, both, size = recv_ref.shape
    rows = both // 2
    group = 256 // query_rows
    factor = scale * LOG2E
    for first in range(0, sources, group):
        queries = query_ref[first : first + group].reshape(group * query_rows, size)

        def advance(step, state):
            top, total, summed = state
            at = pl.ds(step * PIECE, PIECE)
            keys = recv_ref[at, :rows].reshape(PIECE * rows, size)
            values = recv_ref[at, rows:].reshape(PIECE * rows, size)
            scores = scores_of(queries, keys)
            new_top = jnp.maximum(top, jnp.max(scores, axis=1, keepdims=True))
            weights = jnp.exp2((scores - new_top) * factor)
            rescale = jnp.exp2((top - new_top) * factor)
            new_total = total * rescale + jnp.sum(weights, axis=1, keepdims=True)
            new_summed = summed * rescale + jnp.dot(
                weights.astype(jnp.bfloat16), values, preferred_element_type=jnp.float32
            )
            return new_top, new_total, new_summed

        start = (
            jnp.full((group * query_rows, 1), LOWEST, jnp.float32),
            jnp.zeros((group * query_rows, 1), jnp.float32),
            jnp.zeros((group * query_rows, size), jnp.float32),
        )
        state = lax.fori_loop(0, sources // PIECE, advance, start)
        result = (state[2] / state[1]).astype(jnp.bfloat16)
        out_ref[first : first + group] = result.reshape(group, query_rows, size)


def attend_band(queries, recv, scale):
    return pl.pallas_call(
        functools.partial(attend_band_kernel, queries.shape[1], scale),
        out_shape=jax.ShapeDtypeStruct(queries.shape, jnp.bfloat16),
        compiler_params=params(),
        name="attend_band",
    )(queries, recv)


def collect_kernel(by_head_ref, out_ref, turned, sems):
    departures = []
    for piece in range(by_head_ref.shape[1] // PIECE):
        at = pl.ds(piece * PIECE, PIECE)
        turned[at] = jnp.swapaxes(by_head_ref[:, at], 0, 1)
        departure = pltpu.make_async_copy(turned.at[at], out_ref.at[at], sems.at[piece])
        departure.start()
        departures.append(departure)
    for departure in departures:
        departure.wait()


def collect(by_head):
    heads, rows, size = by_head.shape
    return pl.pallas_call(
        collect_kernel,
        in_specs=[pl.BlockSpec(memory_space=pltpu.VMEM)],
        out_specs=pl.BlockSpec(memory_space=pltpu.HBM),
        out_shape=pltpu.HBM((rows, heads, size), by_head.dtype),
        scratch_shapes=[
            pltpu.VMEM((rows, heads, size), by_head.dtype),
            pltpu.SemaphoreType.DMA((rows // PIECE,)),
        ],
        compiler_params=params(),
        name="collect",
    )(by_head)


def video_kernel(
    scale, group, pairs_ref, counts_ref, where_ref, video_ref, own_ref, core_ref, chip_ref, out_ref,
    near_keys, near_values, keys_ref, values_ref, queries_ref, result_ref, turned, sems,
):
    heads, both, size = own_ref.shape
    rows = both // 2
    blocks, slots = pairs_ref.shape
    for ref, place in ((own_ref, rows), (core_ref, where_ref[1]), (chip_ref, where_ref[2])):
        at = pl.ds(pl.multiple_of(place, rows), rows)
        near_keys[:, at] = ref[:, :rows]
        near_values[:, at] = ref[:, rows:]
    values_ref[:, :, :, size:] = jnp.ones((blocks, heads, slots * ABLK, size), jnp.bfloat16)
    column = lax.broadcasted_iota(jnp.int32, (VBLK, slots * ABLK), 1)
    factor = scale * LOG2E

    def prepare(block):
        queries_ref[block] = jnp.swapaxes(video_ref[block * VBLK : (block + 1) * VBLK], 0, 1)
        for slot in range(slots):
            start = pl.multiple_of((pairs_ref[block, slot] - where_ref[0]) * ABLK, ABLK)
            here = slice(slot * ABLK, (slot + 1) * ABLK)
            keys_ref[block, :, here] = near_keys[:, pl.ds(start, ABLK)]
            values_ref[block, :, here, :size] = near_values[:, pl.ds(start, ABLK)]

    def departure(block):
        at = pl.ds(block * VBLK, VBLK)
        return pltpu.make_async_copy(turned.at[block], out_ref.at[at], sems.at[block])

    units = [(block, first) for block in range(blocks) for first in range(0, heads, group)]
    scores, weights = {}, {}
    for step in range(len(units) + 2):
        if step < len(units):
            block, first = units[step]
            if first == 0:
                prepare(block)
            live = column < counts_ref[block] * ABLK
            scores[step] = [
                jnp.where(live, scores_of(queries_ref[block, head], keys_ref[block, head]), LOWEST)
                for head in range(first, first + group)
            ]
        if 1 <= step <= len(units):
            now = jnp.stack(scores.pop(step - 1))
            top = jnp.max(now, axis=2, keepdims=True)
            weights[step - 1] = jnp.exp2((now - top) * factor).astype(jnp.bfloat16)
        if step >= 2:
            block, first = units[step - 2]
            now = weights.pop(step - 2)
            for i in range(group):
                summed = jnp.dot(
                    now[i], values_ref[block, first + i], preferred_element_type=jnp.float32
                )
                result_ref[block, first + i] = (summed[:, :size] / summed[:, size:]).astype(
                    jnp.bfloat16
                )
            if first + group == heads:
                turned[block] = jnp.swapaxes(result_ref[block], 0, 1)
                departure(block).start()
    for block in range(blocks):
        departure(block).wait()


def video(video_q, own, core, chip, pairs, counts, where, scale):
    total, heads, size = video_q.shape
    rows = own.shape[1] // 2
    blocks, slots = pairs.shape
    work = total * heads * slots * ABLK
    in_smem = pl.BlockSpec(memory_space=pltpu.SMEM)
    in_vmem = pl.BlockSpec(memory_space=pltpu.VMEM)
    return pl.pallas_call(
        functools.partial(video_kernel, scale, 4),
        in_specs=[in_smem] * 3 + [in_vmem] * 4,
        out_specs=pl.BlockSpec(memory_space=pltpu.HBM),
        out_shape=pltpu.HBM(video_q.shape, jnp.bfloat16),
        scratch_shapes=[
            pltpu.VMEM((heads, 3 * rows, size), jnp.bfloat16),
            pltpu.VMEM((heads, 3 * rows, size), jnp.bfloat16),
            pltpu.VMEM((blocks, heads, slots * ABLK, size), jnp.bfloat16),
            pltpu.VMEM((blocks, heads, slots * ABLK, 2 * size), jnp.bfloat16),
            pltpu.VMEM((blocks, heads, VBLK, size), jnp.bfloat16),
            pltpu.VMEM((blocks, heads, VBLK, size), jnp.bfloat16),
            pltpu.VMEM((blocks, VBLK, heads, size), jnp.bfloat16),
            pltpu.SemaphoreType.DMA((blocks,)),
        ],
        compiler_params=params(),
        cost_estimate=pl.CostEstimate(
            flops=4 * work * size, bytes_accessed=32 * total * heads * size, transcendentals=work
        ),
        name="video",
    )(pairs, counts, where, video_q, own, core, chip)


def local(audio_qkv, video_q, pairs, counts):
    devices = lax.axis_size("seq")
    rows, unused, heads, size = audio_qkv.shape
    bands = devices // heads
    band_rows = rows // bands
    scale = size ** (-0.5)
    send, kv = arrange(audio_qkv)
    core_pairs = [(i, i ^ 1) for i in range(devices)]
    chip_pairs = [(i, ((i + 1) ^ 1) - 1) for i in range(1, devices - 1)]

    chip = lax.ppermute(kv, "seq", chip_pairs)

    plane = devices // 4
    within = list(range(1, plane, 2))[::-1] + list(range(0, plane, 2))[::-1]
    order = [z * plane + r for z in (1, 0, 3, 2) for r in within]

    def exchange(value):
        return lax.all_to_all(
            value, "seq", split_axis=0, concat_axis=0, tiled=True, axis_index_groups=[order]
        )

    core = lax.ppermute(kv, "seq", core_pairs)
    me = lax.axis_index("seq")
    odd = me & 1
    where = jnp.stack([(me - 1) * (rows // ABLK), 2 * (1 - odd) * rows, 2 * odd * rows])
    video_cross = video(
        video_q, kv, core, chip, pairs, counts, where.astype(jnp.int32), scale
    )
    if bands == 1:
        head_out = attend(exchange(send), scale)
    else:
        queries = exchange(send[:, :, :PIECE].reshape(devices, band_rows, size))
        spread = jnp.broadcast_to(kv[:, None], (heads, bands, 2 * rows, size))
        recv = exchange(spread.reshape(devices, 2 * rows, size))
        head_out = attend_band(queries, recv, scale)
    returned, video_cross = lax.optimization_barrier((exchange(head_out), video_cross))
    audio_attn = collect(returned.reshape(heads, rows, size))
    return audio_attn, video_cross


def solution(mesh):
    in_specs = (
        P(("groups", "seq"), None, None, None),
        P(("groups", "seq"), None, None),
        P(("groups", "seq"), None),
        P(("groups", "seq")),
    )
    out_specs = (P(("groups", "seq"), None, None), P(("groups", "seq"), None, None))
    return jax.shard_map(local, mesh=mesh, in_specs=in_specs, out_specs=out_specs, check_vma=False)
```

```python
import functools

import jax
import jax.numpy as jnp
from jax import lax
from jax.experimental import pallas as pl
from jax.experimental.pallas import tpu as pltpu
from jax.sharding import PartitionSpec as P

ABLK = 32
VBLK = 128
LOG2E = 1.4426950408889634
LOWEST = -1e30
VMEM_LIMIT = 48 * 1024 * 1024


def params():
    return pltpu.CompilerParams(vmem_limit_bytes=VMEM_LIMIT)


PIECE = 16


def arrange_kernel(pieces, qkv_ref, send_ref, kv_ref, came, turned, in_sems, out_sems):
    rows = pieces * PIECE
    arrivals = [
        pltpu.make_async_copy(
            qkv_ref.at[pl.ds(piece * PIECE, PIECE)], came.at[piece], in_sems.at[piece]
        )
        for piece in range(pieces)
    ]
    for arrival in arrivals:
        arrival.start()
    departures = []
    for piece, arrival in enumerate(arrivals):
        arrival.wait()
        for part in range(3):
            by_head = jnp.swapaxes(came[piece, :, part], 0, 1)
            turned[piece, :, part * PIECE : (part + 1) * PIECE] = by_head
            if part:
                at = (part - 1) * rows + piece * PIECE
                kv_ref[:, at : at + PIECE] = by_head
        departure = pltpu.make_async_copy(
            turned.at[piece], send_ref.at[:, piece], out_sems.at[piece]
        )
        departure.start()
        departures.append(departure)
    for departure in departures:
        departure.wait()


def arrange(audio_qkv):
    rows, parts, heads, size = audio_qkv.shape
    dtype = audio_qkv.dtype
    pieces = rows // PIECE
    return pl.pallas_call(
        functools.partial(arrange_kernel, pieces),
        in_specs=[pl.BlockSpec(memory_space=pltpu.HBM)],
        out_specs=(
            pl.BlockSpec(memory_space=pltpu.HBM),
            pl.BlockSpec(memory_space=pltpu.VMEM),
        ),
        out_shape=(
            pltpu.HBM((heads, pieces, parts * PIECE, size), dtype),
            jax.ShapeDtypeStruct((heads, 2 * rows, size), dtype),
        ),
        scratch_shapes=[
            pltpu.VMEM((pieces, PIECE, parts, heads, size), dtype),
            pltpu.VMEM((pieces, heads, parts * PIECE, size), dtype),
            pltpu.SemaphoreType.DMA((pieces,)),
            pltpu.SemaphoreType.DMA((pieces,)),
        ],
        compiler_params=params(),
        name="arrange",
    )(pltpu.with_memory_space_constraint(audio_qkv, pltpu.HBM))


def scores_of(queries, keys):
    return lax.dot_general(
        queries, keys, (((1,), (1,)), ((), ())), preferred_element_type=jnp.float32
    )


def attend_kernel(scale, recv_ref, out_ref, held, sems):
    sources, pieces, unused, size = recv_ref.shape
    total = sources * pieces * PIECE
    chunk = total // sems.shape[0]
    group = chunk // (pieces * PIECE)
    factor = scale * LOG2E
    keys = recv_ref[:, :, PIECE : 2 * PIECE].reshape(total, size)
    values = recv_ref[:, :, 2 * PIECE :].reshape(total, size)
    chunks = total // chunk
    scores, weights, sums, departures = {}, {}, {}, []
    for step in range(chunks + 2):
        if step < chunks:
            first = step * group
            queries = recv_ref[first : first + group, :, :PIECE].reshape(chunk, size)
            scores[step] = scores_of(queries, keys)
        if 0 <= step - 1 < chunks:
            now = scores.pop(step - 1)
            top = jnp.max(now, axis=1, keepdims=True)
            exact = jnp.exp2((now - top) * factor)
            sums[step - 1] = jnp.sum(exact, axis=1, keepdims=True)
            weights[step - 1] = exact.astype(jnp.bfloat16)
        if step >= 2:
            summed = jnp.dot(
                weights.pop(step - 2), values, preferred_element_type=jnp.float32
            )
            result = (summed / sums.pop(step - 2)).astype(jnp.bfloat16)
            at = (step - 2) * group
            held[at : at + group] = result.reshape(group, pieces * PIECE, size)
            departure = pltpu.make_async_copy(
                held.at[pl.ds(at, group)], out_ref.at[pl.ds(at, group)], sems.at[step - 2]
            )
            departure.start()
            departures.append(departure)
    for departure in departures:
        departure.wait()


def attend(recv, scale):
    sources, pieces, unused, size = recv.shape
    rows = pieces * PIECE
    total = sources * rows
    return pl.pallas_call(
        functools.partial(attend_kernel, scale),
        in_specs=[pl.BlockSpec(memory_space=pltpu.VMEM)],
        out_specs=pl.BlockSpec(memory_space=pltpu.HBM),
        out_shape=pltpu.HBM((sources, rows, size), jnp.bfloat16),
        scratch_shapes=[
            pltpu.VMEM((sources, rows, size), jnp.bfloat16),
            pltpu.SemaphoreType.DMA((total // 128,)),
        ],
        compiler_params=params(),
        cost_estimate=pl.CostEstimate(
            flops=4 * total * total * size, bytes_accessed=8 * total * size,
            transcendentals=total * total,
        ),
        name="attend",
    )(recv)


def attend_band_kernel(query_rows, scale, query_ref, recv_ref, out_ref):
    sources, both, size = recv_ref.shape
    rows = both // 2
    group = 256 // query_rows
    factor = scale * LOG2E
    for first in range(0, sources, group):
        queries = query_ref[first : first + group].reshape(group * query_rows, size)

        def advance(step, state):
            top, total, summed = state
            at = pl.ds(step * PIECE, PIECE)
            keys = recv_ref[at, :rows].reshape(PIECE * rows, size)
            values = recv_ref[at, rows:].reshape(PIECE * rows, size)
            scores = scores_of(queries, keys)
            new_top = jnp.maximum(top, jnp.max(scores, axis=1, keepdims=True))
            weights = jnp.exp2((scores - new_top) * factor)
            rescale = jnp.exp2((top - new_top) * factor)
            new_total = total * rescale + jnp.sum(weights, axis=1, keepdims=True)
            new_summed = summed * rescale + jnp.dot(
                weights.astype(jnp.bfloat16), values, preferred_element_type=jnp.float32
            )
            return new_top, new_total, new_summed

        start = (
            jnp.full((group * query_rows, 1), LOWEST, jnp.float32),
            jnp.zeros((group * query_rows, 1), jnp.float32),
            jnp.zeros((group * query_rows, size), jnp.float32),
        )
        state = lax.fori_loop(0, sources // PIECE, advance, start)
        result = (state[2] / state[1]).astype(jnp.bfloat16)
        out_ref[first : first + group] = result.reshape(group, query_rows, size)


def attend_band(queries, recv, scale):
    return pl.pallas_call(
        functools.partial(attend_band_kernel, queries.shape[1], scale),
        out_shape=jax.ShapeDtypeStruct(queries.shape, jnp.bfloat16),
        compiler_params=params(),
        name="attend_band",
    )(queries, recv)


def collect_kernel(by_head_ref, out_ref, turned, sems):
    departures = []
    for piece in range(by_head_ref.shape[1] // PIECE):
        at = pl.ds(piece * PIECE, PIECE)
        turned[at] = jnp.swapaxes(by_head_ref[:, at], 0, 1)
        departure = pltpu.make_async_copy(turned.at[at], out_ref.at[at], sems.at[piece])
        departure.start()
        departures.append(departure)
    for departure in departures:
        departure.wait()


def collect(by_head):
    heads, rows, size = by_head.shape
    return pl.pallas_call(
        collect_kernel,
        in_specs=[pl.BlockSpec(memory_space=pltpu.VMEM)],
        out_specs=pl.BlockSpec(memory_space=pltpu.HBM),
        out_shape=pltpu.HBM((rows, heads, size), by_head.dtype),
        scratch_shapes=[
            pltpu.VMEM((rows, heads, size), by_head.dtype),
            pltpu.SemaphoreType.DMA((rows // PIECE,)),
        ],
        compiler_params=params(),
        name="collect",
    )(by_head)


def video_kernel(
    scale, group, pairs_ref, counts_ref, where_ref, video_ref, own_ref, core_ref, chip_ref, out_ref,
    near_keys, near_values, keys_ref, values_ref, queries_ref, result_ref, turned, sems,
):
    heads, both, size = own_ref.shape
    rows = both // 2
    blocks, slots = pairs_ref.shape
    for ref, place in ((own_ref, rows), (core_ref, where_ref[1]), (chip_ref, where_ref[2])):
        at = pl.ds(pl.multiple_of(place, rows), rows)
        near_keys[:, at] = ref[:, :rows]
        near_values[:, at] = ref[:, rows:]
    values_ref[:, :, :, size:] = jnp.ones((blocks, heads, slots * ABLK, size), jnp.bfloat16)
    column = lax.broadcasted_iota(jnp.int32, (VBLK, slots * ABLK), 1)
    factor = scale * LOG2E

    def prepare(block):
        queries_ref[block] = jnp.swapaxes(video_ref[block * VBLK : (block + 1) * VBLK], 0, 1)
        for slot in range(slots):
            start = pl.multiple_of((pairs_ref[block, slot] - where_ref[0]) * ABLK, ABLK)
            here = slice(slot * ABLK, (slot + 1) * ABLK)
            keys_ref[block, :, here] = near_keys[:, pl.ds(start, ABLK)]
            values_ref[block, :, here, :size] = near_values[:, pl.ds(start, ABLK)]

    def departure(block):
        at = pl.ds(block * VBLK, VBLK)
        return pltpu.make_async_copy(turned.at[block], out_ref.at[at], sems.at[block])

    units = [(block, first) for block in range(blocks) for first in range(0, heads, group)]
    scores, weights = {}, {}
    for step in range(len(units) + 2):
        if step < len(units):
            block, first = units[step]
            if first == 0:
                prepare(block)
            live = column < counts_ref[block] * ABLK
            scores[step] = [
                jnp.where(live, scores_of(queries_ref[block, head], keys_ref[block, head]), LOWEST)
                for head in range(first, first + group)
            ]
        if 1 <= step <= len(units):
            now = jnp.stack(scores.pop(step - 1))
            top = jnp.max(now, axis=2, keepdims=True)
            weights[step - 1] = jnp.exp2((now - top) * factor).astype(jnp.bfloat16)
        if step >= 2:
            block, first = units[step - 2]
            now = weights.pop(step - 2)
            for i in range(group):
                summed = jnp.dot(
                    now[i], values_ref[block, first + i], preferred_element_type=jnp.float32
                )
                result_ref[block, first + i] = (summed[:, :size] / summed[:, size:]).astype(
                    jnp.bfloat16
                )
            if first + group == heads:
                turned[block] = jnp.swapaxes(result_ref[block], 0, 1)
                departure(block).start()
    for block in range(blocks):
        departure(block).wait()


def video(video_q, own, core, chip, pairs, counts, where, scale):
    total, heads, size = video_q.shape
    rows = own.shape[1] // 2
    blocks, slots = pairs.shape
    work = total * heads * slots * ABLK
    in_smem = pl.BlockSpec(memory_space=pltpu.SMEM)
    in_vmem = pl.BlockSpec(memory_space=pltpu.VMEM)
    return pl.pallas_call(
        functools.partial(video_kernel, scale, 4),
        in_specs=[in_smem] * 3 + [in_vmem] * 4,
        out_specs=pl.BlockSpec(memory_space=pltpu.HBM),
        out_shape=pltpu.HBM(video_q.shape, jnp.bfloat16),
        scratch_shapes=[
            pltpu.VMEM((heads, 3 * rows, size), jnp.bfloat16),
            pltpu.VMEM((heads, 3 * rows, size), jnp.bfloat16),
            pltpu.VMEM((blocks, heads, slots * ABLK, size), jnp.bfloat16),
            pltpu.VMEM((blocks, heads, slots * ABLK, 2 * size), jnp.bfloat16),
            pltpu.VMEM((blocks, heads, VBLK, size), jnp.bfloat16),
            pltpu.VMEM((blocks, heads, VBLK, size), jnp.bfloat16),
            pltpu.VMEM((blocks, VBLK, heads, size), jnp.bfloat16),
            pltpu.SemaphoreType.DMA((blocks,)),
        ],
        compiler_params=params(),
        cost_estimate=pl.CostEstimate(
            flops=4 * work * size, bytes_accessed=32 * total * heads * size, transcendentals=work
        ),
        name="video",
    )(pairs, counts, where, video_q, own, core, chip)


def local(audio_qkv, video_q, pairs, counts):
    devices = lax.axis_size("seq")
    rows, unused, heads, size = audio_qkv.shape
    bands = devices // heads
    band_rows = rows // bands
    scale = size ** (-0.5)
    send, kv = arrange(audio_qkv)
    core_pairs = [(i, i ^ 1) for i in range(devices)]
    chip_pairs = [(i, ((i + 1) ^ 1) - 1) for i in range(1, devices - 1)]

    chip = lax.ppermute(kv, "seq", chip_pairs)

    order = [(devices // 4 - 1 - p) % devices for p in range(devices)]

    def exchange(value):
        return lax.all_to_all(
            value, "seq", split_axis=0, concat_axis=0, tiled=True, axis_index_groups=[order]
        )

    core = lax.ppermute(kv, "seq", core_pairs)
    me = lax.axis_index("seq")
    odd = me & 1
    where = jnp.stack([(me - 1) * (rows // ABLK), 2 * (1 - odd) * rows, 2 * odd * rows])
    video_cross = video(
        video_q, kv, core, chip, pairs, counts, where.astype(jnp.int32), scale
    )
    if bands == 1:
        head_out = attend(exchange(send), scale)
    else:
        queries = exchange(send[:, :, :PIECE].reshape(devices, band_rows, size))
        spread = jnp.broadcast_to(kv[:, None], (heads, bands, 2 * rows, size))
        recv = exchange(spread.reshape(devices, 2 * rows, size))
        head_out = attend_band(queries, recv, scale)
    returned, video_cross = lax.optimization_barrier((exchange(head_out), video_cross))
    audio_attn = collect(returned.reshape(heads, rows, size))
    return audio_attn, video_cross


def solution(mesh):
    in_specs = (
        P(("groups", "seq"), None, None, None),
        P(("groups", "seq"), None, None),
        P(("groups", "seq"), None),
        P(("groups", "seq")),
    )
    out_specs = (P(("groups", "seq"), None, None), P(("groups", "seq"), None, None))
    return jax.shard_map(local, mesh=mesh, in_specs=in_specs, out_specs=out_specs, check_vma=False)
```
